1024 devices in a mesh: lon: 32 (over z_lo, core), lat: 32 (over y, z_hi, x).
Axes of the slice: x: 4, y: 4, z: 32 (z_hi: 2, z_lo: 16; z = z_hi * 16 + z_lo), core: 2. Of those that a mesh axis runs over, the one named last changes fastest.
Arguments:
- tracer: float32 [8, 768, 7200], P(None, 'lat', 'lon'), may hold values from -6 to 6
- zonal_wind: float32 [8, 768, 7200], P(None, 'lat', 'lon'), may hold values from -6 to 6
- meridional_wind: float32 [8, 768, 7200], P(None, 'lat', 'lon'), may hold values from -6 to 6
- polar_target: int32 [256], replicated, may hold values from 0 to 255, as said below
- cutoff_wave: int32 [256], replicated, may hold values from 1 to 3599
Outputs:
- tracer_next: float32 [8, 768, 7200], P(None, 'lat', 'lon')
- polar_slots: float32 [256, 8, 7200], P('lat', None, 'lon')
The draws below stay inside these ranges and needn't reach their ends.
Inputs may be any that keep to these rules, and one draw needn't show every extreme that they name: `polar_target`: each of the 256 slots is named by exactly one polar row, so each lat index owns 8 slots (slot s belongs to lat index s // 8); the polar rows held by one lat index name slots of any one lat index at most 1 times, and that many somewhere.
All inputs are finite; a program needn't handle non-finite values.
Results may differ from the reference program's by a relative error of at most 0.00008.
Values sent between devices are 32-bit elements; how exact they have to be, the bound alone decides.
A program may use at most 32 MiB of HBM per device.

```python
import math
import jax
import jax.numpy as jnp

LEV = 8
NLON = 7200
NLAT = 768
NH = 128
NPOLAR = 256
SLOTS = 8
N_LAT = 32


def draw_polar_target(key, part):
    key = jax.random.fold_in(key, 11)
    first_key, second_key = jax.random.split(key)
    device_order = jax.random.permutation(first_key, N_LAT)
    slot_order = jax.random.permutation(second_key, SLOTS)
    polar_index = jnp.arange(NPOLAR, dtype=jnp.int32)
    return (device_order[polar_index % N_LAT] * SLOTS + slot_order[polar_index // N_LAT]).astype(jnp.int32)


def touch_ends(result, stream_key, smallest, high):
    shape = result.shape
    index_at = [jax.random.randint(jax.random.fold_in(stream_key, axis), (), 0, shape[axis]) for axis in range(len(shape))]
    result = result.at[tuple(index_at)].set(smallest)
    longest = shape.index(max(shape))
    index_at[longest] = (index_at[longest] + 1) % shape[longest]
    return result.at[tuple(index_at)].set(high)


def levels(own_key, dims, cuts, smallest, high):
    loudness = 1.0
    for position, blocks in cuts:
        draws = jax.random.uniform(jax.random.fold_in(jax.random.fold_in(own_key, 6), position), (blocks,), jnp.float32, smallest / len(cuts), high / len(cuts))
        loudness = loudness * jnp.repeat(jnp.exp(draws), dims[position] // blocks).reshape((-1,) + (1,) * (len(dims) - 1 - position))
    return loudness


def bell_draw(rng, extent, deviation, reach, pieces=(), kind=jnp.bfloat16):
    array = deviation * jax.random.normal(rng, extent, jnp.float32)
    if pieces:
        array = array * levels(rng, extent, pieces, -0.22, 0.18)
    return jnp.clip(array, -reach, reach).astype(kind)


def setup_inputs(seed: int = 0) -> dict:
    keys = jax.random.split(jax.random.key(seed), 6)
    return {
        "tracer": bell_draw(keys[0], (LEV, NLAT, NLON), 1.0, 6.0, ((1, 32), (2, 32)), jnp.float32),
        "zonal_wind": bell_draw(keys[1], (LEV, NLAT, NLON), 1.0, 6.0, ((1, 32), (2, 32)), jnp.float32),
        "meridional_wind": bell_draw(keys[2], (LEV, NLAT, NLON), 1.0, 6.0, ((1, 32), (2, 32)), jnp.float32),
        "polar_target": draw_polar_target(jax.random.fold_in(keys[5], 71), 0),
        "cutoff_wave": touch_ends(jax.random.randint(keys[4], (NPOLAR,), 1, NLON // 2), jax.random.fold_in(keys[4], 1), 1, (NLON // 2) - 1).astype(jnp.int32),
    }


courant_number = 0.4


def polar_latitudes():
    polar_index = jnp.arange(NPOLAR, dtype=jnp.int32)
    return jnp.where(polar_index < NH, polar_index, polar_index + NLAT - 2 * NH).astype(jnp.int32)


def tracer_increment(tracer, zonal_wind, meridional_wind):
    east_flux = zonal_wind * (tracer + jnp.roll(tracer, -1, axis=2)) * 0.5
    zonal_div = east_flux - jnp.roll(east_flux, 1, axis=2)
    row_index = jnp.arange(NLAT, dtype=jnp.int32)
    row_float = row_index.astype(jnp.float32)
    face_cos = jnp.where(row_index < NLAT - 1, jnp.sin((row_float + 1.0) * (math.pi / NLAT)), 0.0)
    centre_cos = jnp.sin((row_float + 0.5) * (math.pi / NLAT))
    above_row = jnp.concatenate([tracer[:, 1:], jnp.zeros_like(tracer[:, :1])], axis=1)
    north_flux = meridional_wind * face_cos[None, :, None] * (tracer + above_row) * 0.5
    south_flux = jnp.concatenate([jnp.zeros_like(north_flux[:, :1]), north_flux[:, :-1]], axis=1)
    merid_div = (north_flux - south_flux) / centre_cos[None, :, None]
    return -courant_number * (zonal_div + merid_div)


def band_filter(values, cutoff):
    spectrum = jnp.fft.rfft(values, axis=-1)
    kept_mask = jnp.arange(NLON // 2 + 1, dtype=jnp.int32)[None, None, :] <= cutoff[None, :, None]
    return jnp.fft.irfft(jnp.where(kept_mask, spectrum, 0.0), n=NLON, axis=-1).astype(jnp.float32)


def reference(tracer, zonal_wind, meridional_wind, polar_target, cutoff_wave):
    increment = tracer_increment(tracer, zonal_wind, meridional_wind)
    latitudes = polar_latitudes()
    filtered = band_filter(increment[:, latitudes, :], cutoff_wave)
    combined = increment.at[:, latitudes, :].set(filtered)
    tracer_next = tracer + combined
    polar_slots = jnp.zeros((NPOLAR, LEV, NLON), jnp.float32).at[polar_target].set(jnp.transpose(filtered, (1, 0, 2)))
    return tracer_next, polar_slots
```

```python
import math

import jax
import jax.numpy as jnp
import numpy as np
from jax import lax
from jax.experimental import pallas as pl
from jax.experimental.pallas import tpu as pltpu
from jax.sharding import PartitionSpec as P

courant_number = 0.4


def extended(array, sides, width, wrap):
    for axis, dim in sides:
        devices, length = (lax.axis_size(axis), array.shape[dim])
        up = [(i, (i + 1) % devices) for i in range(devices if wrap else devices - 1)]
        down = [(j, i) for i, j in up]
        last = lax.slice_in_dim(array, length - width, length, axis=dim)
        initial = lax.slice_in_dim(array, 0, width, axis=dim)
        before = lax.ppermute(last, axis, up)
        after = lax.ppermute(initial, axis, down)
        array = jnp.concatenate([before, array, after], axis=dim)
    return array


def exact_dot(left_side, right_side):
    return jnp.dot(
        left_side, right_side, precision=lax.Precision.HIGHEST, preferred_element_type=jnp.float32
    )


def dot_rows(left_side, right_side):
    return lax.dot_general(
        left_side,
        right_side,
        (((1,), (1,)), ((), ())),
        precision=lax.Precision.HIGHEST,
        preferred_element_type=jnp.float32,
    )


def split_table(table):
    high = table.astype(jnp.bfloat16)
    low = (table - high.astype(np.float64)).astype(jnp.bfloat16)
    return high, low


def filter_tables(blocks, width):
    total = blocks * width
    lanes = -(-width // 128) * 128
    outer = np.arange(blocks)[:, None] * np.arange(blocks)[None, :] % blocks * (2 * np.pi / blocks)
    forward = np.block([[np.cos(outer), np.sin(outer)], [-np.sin(outer), np.cos(outer)]])
    middle = np.arange(blocks)[:, None] * np.arange(width)[None, :] * (2 * np.pi / total)
    twiddle = np.zeros((2, blocks, lanes), np.float32)
    twiddle[0, :, :width] = np.cos(middle)
    twiddle[1, :, :width] = np.sin(middle)
    inner = np.arange(width)[:, None] * np.arange(width)[None, :] % width * (2 * np.pi / width)
    within = np.zeros((lanes, 2 * lanes))
    within[:width, :width] = np.cos(inner)
    within[:width, lanes : lanes + width] = np.sin(inner)
    return (*split_table(forward), *split_table(forward.T), twiddle, *split_table(within))


def split_value(value):
    high = value.astype(jnp.bfloat16)
    low = (value - high.astype(jnp.float32)).astype(jnp.bfloat16)
    return high, low


def mxu(left_side, right_side):
    return jnp.dot(left_side, right_side, preferred_element_type=jnp.float32)


def dot_left(table_high, table_low, value):
    high, low = split_value(value)
    return mxu(table_high, high) + (mxu(table_high, low) + mxu(table_low, high))


def dot_right(value, table_high, table_low):
    high, low = split_value(value)
    return mxu(high, table_high) + (mxu(low, table_high) + mxu(high, table_low))


def band_filter(values, cut, tables, blocks, width):
    fwd_high, fwd_low, inv_high, inv_low, cos_mid, sin_mid, in_high, in_low = tables
    lanes = values.shape[-1]
    total = blocks * width
    spread = dot_left(fwd_high, fwd_low, values)
    real, imag = spread[:blocks], spread[blocks:]
    turned = jnp.concatenate(
        [real * cos_mid + imag * sin_mid, imag * cos_mid - real * sin_mid], axis=0
    )
    parts = dot_right(turned, in_high, in_low)
    real = parts[:blocks, :lanes] + parts[blocks:, lanes:]
    imag = parts[blocks:, :lanes] - parts[:blocks, lanes:]
    wave = lax.broadcasted_iota(jnp.int32, (blocks, lanes), 0) + blocks * lax.broadcasted_iota(
        jnp.int32, (blocks, lanes), 1
    )
    kept = jnp.minimum(wave, total - wave) <= cut
    scale = jnp.where(kept, 1.0 / total, 0.0)
    parts = dot_right(jnp.concatenate([real * scale, imag * scale], axis=0), in_high, in_low)
    real = parts[:blocks, :lanes] - parts[blocks:, lanes:]
    imag = parts[blocks:, :lanes] + parts[:blocks, lanes:]
    turned = jnp.concatenate(
        [real * cos_mid - imag * sin_mid, imag * cos_mid + real * sin_mid], axis=0
    )
    return dot_left(inv_high, inv_low, turned)


def filter_kernel(cut_ref, values_ref, fh, fl, ih, il, tw, wh, wl, out_ref):
    blocks = values_ref.shape[1]
    lanes = tw.shape[2]
    width = values_ref.shape[2]
    pad = jnp.zeros((blocks, lanes - width), jnp.float32)
    values = jnp.concatenate(
        [
            jnp.concatenate([values_ref[0], pad], axis=1),
            jnp.concatenate([values_ref[1], pad], axis=1),
        ],
        axis=0,
    )
    tables = (fh[...], fl[...], ih[...], il[...], tw[0], tw[1], wh[...], wl[...])
    out = band_filter(values, cut_ref[0], tables, blocks, width)
    out_ref[0] = out[:blocks, :width]
    out_ref[1] = out[blocks:, :width]


def shards(tracer, zonal_wind, meridional_wind, polar_target, cutoff_wave):
    levels, lat_dev, lon_dev = tracer.shape
    lat_count = lax.axis_size("lat")
    lon_count = lax.axis_size("lon")
    own_lat = lax.axis_index("lat")
    own_lon = lax.axis_index("lon")
    total_lat = lat_dev * lat_count
    total_lon = lon_dev * lon_count
    half_rows = total_lat // 6
    polar_count = 2 * half_rows
    slots_dev = polar_count // lat_count
    capacity = (min(lat_dev, half_rows) + lat_count - 1) // lat_count
    positions_all = lat_count * capacity
    zonal_pad = extended(jnp.stack([tracer, zonal_wind]), (("lon", 3),), 1, True)
    tracer_zonal = zonal_pad[0]
    wind_zonal = zonal_pad[1]
    east_flux = (
        wind_zonal[:, :, : lon_dev + 1]
        * (tracer_zonal[:, :, : lon_dev + 1] + tracer_zonal[:, :, 1:])
        * 0.5
    )
    zonal_div = east_flux[:, :, 1:] - east_flux[:, :, :-1]
    merid_pad = extended(jnp.stack([tracer, meridional_wind]), (("lat", 2),), 1, False)
    tracer_merid = merid_pad[0]
    wind_merid = merid_pad[1]
    face_rows = own_lat * lat_dev - 1 + jnp.arange(lat_dev + 1, dtype=jnp.int32)
    inside_mask = (face_rows >= 0) & (face_rows < total_lat - 1)
    face_cos = jnp.where(
        inside_mask, jnp.sin((face_rows.astype(jnp.float32) + 1.0) * (math.pi / total_lat)), 0.0
    )
    centre_rows = own_lat * lat_dev + jnp.arange(lat_dev, dtype=jnp.int32)
    centre_cos = jnp.sin((centre_rows.astype(jnp.float32) + 0.5) * (math.pi / total_lat))
    north_flux = (
        wind_merid[:, : lat_dev + 1]
        * face_cos[None, :, None]
        * (tracer_merid[:, : lat_dev + 1] + tracer_merid[:, 1:])
        * 0.5
    )
    merid_div = (north_flux[:, 1:] - north_flux[:, :-1]) / centre_cos[None, :, None]
    increment = -courant_number * (zonal_div + merid_div)
    polar_index = jnp.arange(polar_count, dtype=jnp.int32)
    global_rows = jnp.where(
        polar_index < half_rows, polar_index, polar_index + total_lat - 2 * half_rows
    )
    home_device = global_rows // lat_dev
    dest_device = polar_target // slots_dev
    dest_slot = polar_target % slots_dev
    same_route = (
        (home_device[:, None] == home_device[None, :])
        & (dest_device[:, None] == dest_device[None, :])
        & (polar_index[None, :] < polar_index[:, None])
    )
    arrival_rank = jnp.sum(same_route.astype(jnp.int32), axis=1)
    send_position = dest_device * capacity + arrival_rank
    receive_position = home_device * capacity + arrival_rank
    position_index = jnp.arange(positions_all, dtype=jnp.int32)
    out_pick = (position_index[:, None] == send_position[None, :]) & (home_device == own_lat)[
        None, :
    ]
    local_of = (
        global_rows[:, None] == (own_lat * lat_dev + jnp.arange(lat_dev, dtype=jnp.int32))[None, :]
    )
    send_select = exact_dot(out_pick.astype(jnp.float32), local_of.astype(jnp.float32))
    in_pick = (dest_slot[None, :] == jnp.arange(slots_dev, dtype=jnp.int32)[:, None]) & (
        dest_device == own_lat
    )[None, :]
    receive_onehot = (receive_position[:, None] == position_index[None, :]).astype(jnp.float32)
    receive_select = exact_dot(in_pick.astype(jnp.float32), receive_onehot)
    slot_cut = jnp.sum(jnp.where(in_pick, cutoff_wave[None, :], 0), axis=1)
    outgoing = jnp.einsum("pj,ljx->plx", send_select, increment, precision=lax.Precision.HIGHEST)
    arrived = lax.all_to_all(
        outgoing.reshape(lat_count, capacity, levels, lon_dev),
        "lat",
        split_axis=0,
        concat_axis=0,
        tiled=True,
    )
    slot_rows = jnp.einsum(
        "sp,plx->slx",
        receive_select,
        arrived.reshape(positions_all, levels, lon_dev),
        precision=lax.Precision.HIGHEST,
    )
    flat_count = slots_dev * levels
    flat_rows = slot_rows.reshape(flat_count, lon_dev)
    cut_rows = jnp.repeat(slot_cut, levels)
    share = flat_count // lon_count
    gathered = lax.all_to_all(
        flat_rows.reshape(lon_count, share, lon_dev), "lon", split_axis=0, concat_axis=0, tiled=True
    )
    own_cut = lax.dynamic_slice_in_dim(cut_rows, own_lon * share, 1, 0)
    tables = filter_tables(lon_count, lon_dev)
    in_vmem = pl.BlockSpec(memory_space=pltpu.VMEM)
    smoothed = pl.pallas_call(
        filter_kernel,
        out_shape=jax.ShapeDtypeStruct((share, lon_count, lon_dev), jnp.float32),
        in_specs=[pl.BlockSpec(memory_space=pltpu.SMEM)] + [in_vmem] * 8,
        out_specs=in_vmem,
        name="band_filter",
    )(own_cut, gathered.transpose(1, 0, 2), *[jnp.asarray(t) for t in tables])
    filtered_flat = lax.all_to_all(
        smoothed.transpose(1, 0, 2), "lon", split_axis=0, concat_axis=0, tiled=True
    )
    filtered = filtered_flat.reshape(slots_dev, levels, lon_dev)
    back_send = jnp.einsum("sp,slx->plx", receive_select, filtered, precision=lax.Precision.HIGHEST)
    returned = lax.all_to_all(
        back_send.reshape(lat_count, capacity, levels, lon_dev),
        "lat",
        split_axis=0,
        concat_axis=0,
        tiled=True,
    )
    polar_increment = jnp.einsum(
        "pj,plx->ljx",
        send_select,
        returned.reshape(positions_all, levels, lon_dev),
        precision=lax.Precision.HIGHEST,
    )
    polar_local = jnp.sum(local_of.astype(jnp.int32), axis=0) > 0
    tracer_next = tracer + jnp.where(polar_local[None, :, None], polar_increment, increment)
    return (tracer_next, filtered)


def solution(mesh):
    placed = (P(None, "lat", "lon"), P(None, "lat", "lon"), P(None, "lat", "lon"), P(), P())
    return jax.shard_map(
        shards,
        mesh=mesh,
        in_specs=placed,
        out_specs=(P(None, "lat", "lon"), P("lat", None, "lon")),
        check_vma=False,
    )
```

```python
import math

import jax
import jax.numpy as jnp
import numpy as np
from jax import lax
from jax.experimental import pallas as pl
from jax.experimental.pallas import tpu as pltpu
from jax.sharding import PartitionSpec as P

courant_number = 0.4
LEV, NLAT, NLON = 8, 768, 7200
NH, NPOLAR, SLOTS = 128, 256, 8
N_LAT, N_LON = 32, 32
ROWS, COLS, LANES = NLAT // N_LAT, NLON // N_LON, 256
FLAT = LEV * ROWS
SOURCES, PLACES = 6, 16
MESH = pl.DeviceIdType.MESH


def half_of(lat):
    return lax.rem(lax.div(lat, 4), 2)


def place_of(lat):
    return lax.div(lat, 8) * 4 + lax.rem(lat, 4)


def lat_of(place, half):
    return lax.div(place, 4) * 8 + half * 4 + lax.rem(place, 4)


def source_place(source, half):
    return jnp.where(source < 4 - 2 * half, source, source + 10)


def worker_lon(worker):
    return lax.div(8 * worker + 4, 3)


def worker_at(lon):
    worker = lax.div(3 * lon + 3, 8)
    return worker, 8 * worker + 4 <= 3 * lon + 2


def filter_tables():
    angle = np.arange(N_LON)[:, None] * np.arange(N_LON)[None, :] % N_LON * (2 * np.pi / N_LON)
    across = np.zeros((2, LEV // 2, N_LON, N_LON, LEV))
    for pair in range(LEV // 2):
        across[0, pair, :, :, 2 * pair] = np.cos(angle)
        across[0, pair, :, :, 2 * pair + 1] = np.sin(angle)
        across[1, pair, :, :, 2 * pair] = -np.sin(angle)
        across[1, pair, :, :, 2 * pair + 1] = np.cos(angle)
    across = across.reshape(LEV * N_LON, LEV * N_LON)
    middle = np.arange(N_LON)[:, None] * np.arange(COLS)[None, :] * (2 * np.pi / NLON)
    twiddle = np.zeros((2, N_LON, LANES), np.float32)
    twiddle[0, :, :COLS] = np.cos(middle)
    twiddle[1, :, :COLS] = np.sin(middle)
    inner = np.arange(COLS)[:, None] * np.arange(COLS)[None, :] % COLS * (2 * np.pi / COLS)
    within = np.zeros((LANES, 2 * LANES))
    within[:COLS, :COLS] = np.cos(inner)
    within[:COLS, LANES : LANES + COLS] = np.sin(inner)
    return [a.astype(np.float32) for a in (across, across.T, within, twiddle)]


def row_factors():
    row = np.arange(NLAT, dtype=np.float32)
    step = np.float32(math.pi / NLAT)
    face = np.sin(((row + np.float32(1.0)) * step).astype(np.float64)).astype(np.float32)
    face[-1] = 0.0
    centre = np.sin(((row + np.float32(0.5)) * step).astype(np.float64)).astype(np.float32)
    below = np.concatenate([np.zeros(1, np.float32), face[:-1]])
    table = np.stack([face, below, centre]).reshape(3, N_LAT, ROWS).transpose(1, 0, 2)
    return np.ascontiguousarray(np.broadcast_to(table[..., None], (N_LAT, 3, ROWS, 128)))


def routing_plan(polar_target, cutoff_wave):
    lat, lon = lax.axis_index("lat"), lax.axis_index("lon")
    half, place = half_of(lat), place_of(lat)
    index = np.arange(NPOLAR)
    glob = np.where(index < NH, index, index + NLAT - NPOLAR)
    home, own_row = glob // ROWS, glob % ROWS
    home_half, home_place = (home // 4) % 2, home // 8 * 4 + home % 4
    home_source = home_half * SOURCES + np.where(
        home_place < 4 - 2 * home_half, home_place, home_place - 10
    )
    home, own_row, home_source = (
        jnp.asarray(a, jnp.int32)[None, :] for a in (home, own_row, home_source)
    )
    target = polar_target[None, :]
    target_lat = target // SLOTS
    target_code = place_of(target_lat) * 2 + half_of(target_lat)
    worker, _ = worker_at(lon)
    worker_home = lat_of(source_place(lax.div(worker, 2), half), half)
    worker_target = place * 2 + lax.rem(worker, 2)
    entry = lax.broadcasted_iota(jnp.int32, (65, 1), 0)
    mine = home == lat
    value = jnp.where(
        entry < 32,
        jnp.where(mine & (target_code == entry), own_row, 0),
        jnp.where(
            entry < 56,
            jnp.where(mine & (own_row == entry - 32), target_code, 0),
            jnp.where(
                entry < 64,
                jnp.where(target == lat * SLOTS + entry - 56, home_source, 0),
                jnp.where(
                    (home == worker_home) & (target_code == worker_target), cutoff_wave[None, :], 0
                ),
            ),
        ),
    )
    return jnp.sum(value, axis=1)


def split_value(value):
    high = value.astype(jnp.bfloat16)
    low = (value - high.astype(jnp.float32)).astype(jnp.bfloat16)
    return high, low


def mxu(left_side, right_side):
    return jnp.dot(left_side, right_side, preferred_element_type=jnp.float32)


def dot_left(table_high, table_low, value):
    high, low = split_value(value)
    return mxu(table_high, high) + (mxu(table_high, low) + mxu(table_low, high))


def dot_right(value, table_high, table_low):
    high, low = split_value(value)
    return mxu(high, table_high) + (mxu(low, table_high) + mxu(high, table_low))


def band_filter(values, cut, tables):
    fwd_high, fwd_low, inv_high, inv_low, in_high, in_low, cos_mid, sin_mid = tables
    part = N_LON * LEV // 2
    spread = dot_left(fwd_high, fwd_low, values)
    real, imag = spread[:part], spread[part:]
    turned = jnp.concatenate(
        [real * cos_mid + imag * sin_mid, imag * cos_mid - real * sin_mid], axis=0
    )
    parts = dot_right(turned, in_high, in_low)
    real = parts[:part, :LANES] + parts[part:, LANES:]
    imag = parts[part:, :LANES] - parts[:part, LANES:]
    shape = (N_LON, LANES)
    wave = lax.broadcasted_iota(jnp.int32, shape, 0) + N_LON * lax.broadcasted_iota(
        jnp.int32, shape, 1
    )
    scale = jnp.where(jnp.minimum(wave, NLON - wave) <= cut, 1.0 / NLON, 0.0)
    scale = jnp.concatenate([scale] * (LEV // 2), axis=0)
    parts = dot_right(jnp.concatenate([real * scale, imag * scale], axis=0), in_high, in_low)
    real = parts[:part, :LANES] - parts[part:, LANES:]
    imag = parts[part:, :LANES] + parts[:part, LANES:]
    turned = jnp.concatenate(
        [real * cos_mid - imag * sin_mid, imag * cos_mid + real * sin_mid], axis=0
    )
    return dot_left(inv_high, inv_low, turned)


def each(count, step):
    lax.fori_loop(0, count, lambda k, carry: (step(k), carry)[1], 0)


def widened(block):
    pad = jnp.zeros((LEV, ROWS, LANES - COLS), jnp.float32)
    return jnp.concatenate([block, pad], axis=2).reshape(FLAT, LANES)


def spread_rows(edge):
    return jnp.broadcast_to(edge[:, None, :], (LEV, ROWS, LANES)).reshape(FLAT, LANES)


def substep_kernel(
    plan,
    tracer_hbm,
    zonal_hbm,
    merid_hbm,
    factor_hbm,
    forward_hbm,
    inverse_hbm,
    within_hbm,
    tw_hbm,
    next_out,
    slots_out,
    tracer,
    zonal,
    merid,
    factor,
    forward,
    inverse,
    within,
    fh,
    fl,
    ih,
    il,
    wh,
    wl,
    tw,
    lon_edge,
    east_in,
    west_in,
    south_edge,
    north_edge,
    south_in,
    north_in,
    increment,
    by_row,
    outbound,
    column,
    gathered,
    smoothed,
    returned,
    slot_in,
    homeward,
    load_sem,
    edge_send,
    edge_recv,
    out_send,
    out_recv,
    gather_send,
    gather_recv,
    back_send,
    back_recv,
    cross_send,
    cross_recv,
    home_send,
    home_recv,
):
    lon, lat = lax.axis_index("lon"), lax.axis_index("lat")
    half, place = half_of(lat), place_of(lat)
    first_places = 4 - 2 * half
    is_source = jnp.logical_or(place < first_places, place >= first_places + 10)
    source = jnp.where(place < first_places, place, place - 10)
    worker, is_worker = worker_at(lon)
    work_source, work_half = lax.div(worker, 2), lax.rem(worker, 2)
    across = jnp.logical_and(is_worker, work_half != half)
    east, west = lax.rem(lon + 1, N_LON), lax.rem(lon + N_LON - 1, N_LON)
    has_north, has_south = lat < N_LAT - 1, lat > 0

    loads = [
        pltpu.make_async_copy(a, b, load_sem.at[i])
        for i, (a, b) in enumerate(
            [
                (tracer_hbm, tracer),
                (zonal_hbm, zonal),
                (merid_hbm, merid),
                (factor_hbm.at[lat], factor),
                (forward_hbm, forward),
                (inverse_hbm, inverse),
                (within_hbm, within),
                (tw_hbm, tw),
            ]
        )
    ]
    for load in loads:
        load.start()

    barrier = pltpu.get_barrier_semaphore()

    def greet(to_lon, to_lat):
        pl.semaphore_signal(
            barrier, inc=1, device_id={"lon": to_lon, "lat": to_lat}, device_id_type=MESH
        )

    @pl.when(has_north)
    def _():
        greet(lon, lat + 1)

    @pl.when(has_south)
    def _():
        greet(lon, lat - 1)

    each(N_LON, lambda k: greet(k, lat_of(place, 1 - half)))
    each(N_LON - 1, lambda k: greet(lax.rem(lon + 1 + k, N_LON), lat))

    @pl.when(is_source)
    def _():
        each(PLACES - 1, lambda k: greet(lon, lat_of(lax.rem(place + 1 + k, PLACES), half)))

    @pl.when(jnp.logical_not(is_source))
    def _():
        each(SOURCES, lambda k: greet(lon, lat_of(source_place(k, half), half)))

    def send(what, where, send_sem, recv_sem, to_lon, to_lat):
        return pltpu.make_async_remote_copy(
            src_ref=what,
            dst_ref=where,
            send_sem=send_sem,
            recv_sem=recv_sem,
            device_id={"lon": to_lon, "lat": to_lat},
            device_id_type=MESH,
        )

    def take(where, recv_sem):
        send(where, where, recv_sem, recv_sem, lon, lat).wait_recv()

    def sent(what, send_sem):
        send(what, what, send_sem, send_sem, lon, lat).wait_send()

    for load in loads[:4]:
        load.wait()
    t = widened(tracer[...])
    u = widened(zonal[...])
    v = widened(merid[...])
    lane = lax.broadcasted_iota(jnp.int32, (FLAT, LANES), 1)
    row = lax.rem(lax.broadcasted_iota(jnp.int32, (FLAT, LANES), 0), ROWS)
    narrow = lane[:, :128]
    last = COLS - 1 - 128
    edge = jnp.where(
        narrow == 0,
        t[:, :128],
        jnp.where(
            narrow == 1,
            pltpu.roll(t[:, 128:], 128 + 1 - last, 1),
            pltpu.roll(u[:, 128:], 128 + 2 - last, 1),
        ),
    )
    edge = jnp.concatenate([edge, jnp.zeros((LANES - FLAT, 128), jnp.float32)], axis=0)
    lon_edge[...] = edge.T[:8]
    for level in range(LEV):
        top, bottom = level * ROWS + ROWS - 1, level * ROWS
        south_edge[0, level : level + 1, :] = t[top : top + 1]
        south_edge[1, level : level + 1, :] = v[top : top + 1]
        north_edge[level : level + 1, :] = t[bottom : bottom + 1]

    for load in loads[4:]:
        load.wait()

    @pl.when(is_worker)
    def _():
        fh[...], fl[...] = split_value(forward[...])
        ih[...], il[...] = split_value(inverse[...])
        wh[...], wl[...] = split_value(within[...])

    pl.semaphore_wait(
        barrier,
        2 * N_LON
        - 1
        + jnp.where(is_source, PLACES - 1, SOURCES)
        + jnp.where(has_north, 1, 0)
        + jnp.where(has_south, 1, 0),
    )

    @pl.when(has_north)
    def _():
        send(south_edge, south_in, edge_send.at[0], edge_recv.at[0], lon, lat + 1).start()

    @pl.when(has_south)
    def _():
        send(north_edge, north_in, edge_send.at[1], edge_recv.at[1], lon, lat - 1).start()

    send(lon_edge, west_in, edge_send.at[2], edge_recv.at[2], east, lat).start()
    send(lon_edge, east_in, edge_send.at[3], edge_recv.at[3], west, lat).start()

    @pl.when(jnp.logical_not(has_south))
    def _():
        south_in[...] = jnp.zeros(south_in.shape, jnp.float32)

    @pl.when(jnp.logical_not(has_north))
    def _():
        north_in[...] = jnp.zeros(north_in.shape, jnp.float32)

    take(west_in, edge_recv.at[2])
    take(east_in, edge_recv.at[3])
    columns = jnp.concatenate(
        [east_in[...], west_in[...], jnp.zeros((112, LANES), jnp.float32)], axis=0
    ).T[:FLAT]
    tracer_east, tracer_west, wind_west = columns[:, 0:1], columns[:, 9:10], columns[:, 10:11]
    shifted = jnp.where(lane == COLS - 1, tracer_east, pltpu.roll(t, LANES - 1, 1))
    east_flux = u * (t + shifted) * 0.5
    west_flux = jnp.where(lane == 0, wind_west * (tracer_west + t) * 0.5, pltpu.roll(east_flux, 1, 1))
    zonal_div = east_flux - west_flux

    @pl.when(has_south)
    def _():
        take(south_in, edge_recv.at[0])

    @pl.when(has_north)
    def _():
        take(north_in, edge_recv.at[1])

    def by_lane(i):
        rows = jnp.concatenate([factor[i], factor[i]], axis=1)
        return jnp.broadcast_to(rows[None], (LEV, ROWS, LANES)).reshape(FLAT, LANES)

    above = jnp.where(row == ROWS - 1, spread_rows(north_in[...]), pltpu.roll(t, FLAT - 1, 0))
    north_flux = v * by_lane(0) * (t + above) * 0.5
    below_flux = spread_rows(south_in[1]) * by_lane(1) * (spread_rows(south_in[0]) + t) * 0.5
    south_flux = jnp.where(row == 0, below_flux, pltpu.roll(north_flux, 1, 0))
    change = -courant_number * (zonal_div + (north_flux - south_flux) / by_lane(2))
    change = jnp.where(lane < COLS, change, 0.0)
    increment[...] = change

    @pl.when(is_source)
    def _():
        for level in range(LEV):
            by_row[:, level, :] = increment[level * ROWS : (level + 1) * ROWS, :]

        def leave(k):
            to = lax.rem(place + 1 + k, PLACES)
            outbound[2 * to] = by_row[plan[2 * to]]
            outbound[2 * to + 1] = by_row[plan[2 * to + 1]]
            send(
                outbound.at[pl.ds(2 * to, 2)],
                column.at[source],
                out_send,
                out_recv.at[source],
                lon,
                lat_of(to, half),
            ).start()

        each(PLACES - 1, leave)
        column[source, 0] = by_row[plan[2 * place]]
        column[source, 1] = by_row[plan[2 * place + 1]]

    def pass_on(s):
        @pl.when(jnp.logical_not(jnp.logical_and(is_source, source == s)))
        def _():
            take(column.at[s], out_recv.at[s])

        for t_half in range(2):
            to = worker_lon(2 * s + t_half)

            @pl.when(to != lon)
            def _():
                send(
                    column.at[s, t_half], gathered.at[lon], gather_send, gather_recv, to, lat
                ).start()

            @pl.when(to == lon)
            def _():
                gathered[lon] = column[s, t_half]

    each(SOURCES, pass_on)

    next_out[...] = tracer[...] + increment[...].reshape(LEV, ROWS, LANES)[:, :, :COLS]
    @pl.when(is_worker)
    def _():
        take(gathered.at[pl.ds(0, N_LON - 1)], gather_recv)
        cos_mid = jnp.concatenate([tw[0]] * (LEV // 2), axis=0)
        sin_mid = jnp.concatenate([tw[1]] * (LEV // 2), axis=0)
        tables = (fh[...], fl[...], ih[...], il[...], wh[...], wl[...], cos_mid, sin_mid)
        result = band_filter(gathered[...].reshape(N_LON * LEV, LANES), plan[64], tables)
        smoothed[...] = result.reshape(N_LON, LEV, LANES)

        @pl.when(across)
        def _():
            each(
                N_LON,
                lambda k: send(
                    smoothed.at[lax.rem(lon + k, N_LON)],
                    slot_in.at[half * SOURCES + work_source],
                    cross_send,
                    cross_recv,
                    lax.rem(lon + k, N_LON),
                    lat_of(place, 1 - half),
                ).start(),
            )

        each(
            N_LON - 1,
            lambda k: send(
                smoothed.at[lax.rem(lon + 1 + k, N_LON)],
                returned.at[work_source, work_half],
                back_send,
                back_recv.at[work_source],
                lax.rem(lon + 1 + k, N_LON),
                lat,
            ).start(),
        )
        returned[work_source, work_half] = smoothed[lon]

    def go_home(s):
        own = jnp.logical_and(is_worker, work_source == s)

        @pl.when(own)
        def _():
            take(returned.at[s, 0], back_recv.at[s])

        @pl.when(jnp.logical_not(own))
        def _():
            take(returned.at[s], back_recv.at[s])

        stays = jnp.logical_and(is_source, source == s)

        @pl.when(stays)
        def _():
            homeward[2 * place] = returned[s, 0]
            homeward[2 * place + 1] = returned[s, 1]

        @pl.when(jnp.logical_not(stays))
        def _():
            send(
                returned.at[s],
                homeward.at[pl.ds(2 * place, 2)],
                home_send,
                home_recv,
                lon,
                lat_of(source_place(s, half), half),
            ).start()

        slot_in[half * SOURCES + s] = returned[s, half]

    each(SOURCES, go_home)
    take(slot_in.at[pl.ds(0, SOURCES)], cross_recv)
    for slot in range(SLOTS):
        slots_out[slot] = slot_in[plan[56 + slot]][:, :COLS]

    @pl.when(is_source)
    def _():
        take(homeward.at[pl.ds(0, 2 * PLACES - 2)], home_recv)
        for j in range(ROWS):
            lat_row = lat * ROWS + j
            polar = jnp.logical_or(lat_row < NH, lat_row >= NLAT - NH)
            filtered = homeward[plan[32 + j]][:, :COLS]
            next_out[:, j, :] = jnp.where(polar, tracer[:, j, :] + filtered, next_out[:, j, :])

    @pl.when(has_north)
    def _():
        sent(south_edge, edge_send.at[0])

    @pl.when(has_south)
    def _():
        sent(north_edge, edge_send.at[1])

    sent(lon_edge, edge_send.at[2])
    sent(lon_edge, edge_send.at[3])

    @pl.when(is_source)
    def _():
        sent(outbound.at[pl.ds(0, 2 * PLACES - 2)], out_send)
        sent(homeward.at[pl.ds(0, 2 * SOURCES - 2)], home_send)

    @pl.when(jnp.logical_not(is_source))
    def _():
        sent(homeward.at[pl.ds(0, 2 * SOURCES)], home_send)

    @pl.when(is_worker)
    def _():
        sent(smoothed.at[pl.ds(0, 2 * SOURCES - 1)], gather_send)
        sent(smoothed.at[pl.ds(0, N_LON - 1)], back_send)

    @pl.when(jnp.logical_not(is_worker))
    def _():
        sent(smoothed.at[pl.ds(0, 2 * SOURCES)], gather_send)

    @pl.when(across)
    def _():
        sent(smoothed, cross_send)


def shards(tracer, zonal_wind, meridional_wind, polar_target, cutoff_wave):
    plan = routing_plan(polar_target, cutoff_wave)
    tables = [jnp.asarray(table) for table in filter_tables()]
    factors = jnp.asarray(row_factors())
    f32, bf16 = jnp.float32, jnp.bfloat16
    block = (LEV, ROWS, COLS)
    anywhere, in_vmem = pl.BlockSpec(memory_space=pltpu.HBM), pl.BlockSpec(memory_space=pltpu.VMEM)
    dma = pltpu.SemaphoreType.DMA
    square, wide = (LEV * N_LON, LEV * N_LON), (LANES, 2 * LANES)
    message = (LEV, LANES)
    return pl.pallas_call(
        substep_kernel,
        out_shape=(
            jax.ShapeDtypeStruct(block, f32),
            jax.ShapeDtypeStruct((SLOTS, LEV, COLS), f32),
        ),
        in_specs=[pl.BlockSpec(memory_space=pltpu.SMEM)] + [anywhere] * 8,
        out_specs=(in_vmem, in_vmem),
        scratch_shapes=[
            pltpu.VMEM(block, f32),
            pltpu.VMEM(block, f32),
            pltpu.VMEM(block, f32),
            pltpu.VMEM((3, ROWS, 128), f32),
            pltpu.VMEM(square, f32),
            pltpu.VMEM(square, f32),
            pltpu.VMEM(wide, f32),
            pltpu.VMEM(square, bf16),
            pltpu.VMEM(square, bf16),
            pltpu.VMEM(square, bf16),
            pltpu.VMEM(square, bf16),
            pltpu.VMEM(wide, bf16),
            pltpu.VMEM(wide, bf16),
            pltpu.VMEM((2, N_LON, LANES), f32),
            pltpu.VMEM(message, f32),
            pltpu.VMEM(message, f32),
            pltpu.VMEM(message, f32),
            pltpu.VMEM((2, *message), f32),
            pltpu.VMEM(message, f32),
            pltpu.VMEM((2, *message), f32),
            pltpu.VMEM(message, f32),
            pltpu.VMEM((FLAT, LANES), f32),
            pltpu.VMEM((ROWS, *message), f32),
            pltpu.VMEM((2 * PLACES, *message), f32),
            pltpu.VMEM((SOURCES, 2, *message), f32),
            pltpu.VMEM((N_LON, *message), f32),
            pltpu.VMEM((N_LON, *message), f32),
            pltpu.VMEM((SOURCES, 2, *message), f32),
            pltpu.VMEM((2 * SOURCES, *message), f32),
            pltpu.VMEM((2 * PLACES, *message), f32),
            dma((8,)),
            dma((4,)),
            dma((4,)),
            dma,
            dma((SOURCES,)),
            dma,
            dma,
            dma,
            dma((SOURCES,)),
            dma,
            dma,
            dma,
            dma,
        ],
        compiler_params=pltpu.CompilerParams(
            collective_id=0, has_side_effects=True, vmem_limit_bytes=60 * 2**20
        ),
        name="substep",
    )(plan, tracer, zonal_wind, meridional_wind, factors, *tables)


def solution(mesh):
    placed = (P(None, "lat", "lon"), P(None, "lat", "lon"), P(None, "lat", "lon"), P(), P())
    return jax.shard_map(
        shards,
        mesh=mesh,
        in_specs=placed,
        out_specs=(P(None, "lat", "lon"), P("lat", None, "lon")),
        check_vma=False,
    )
```

```python
import math

import jax
import jax.numpy as jnp
import numpy as np
from jax import lax
from jax.experimental import pallas as pl
from jax.experimental.pallas import tpu as pltpu
from jax.sharding import PartitionSpec as P

courant_number = 0.4
LEV, NLAT, NLON = 8, 768, 7200
NH, NPOLAR, SLOTS = 128, 256, 8
N_LAT, N_LON = 32, 32
ROWS, COLS, LANES = NLAT // N_LAT, NLON // N_LON, 256
FLAT = LEV * ROWS
SOURCES, PLACES = 6, 16
SEAM_LOW = (3, 27)
SEAM_LON = 15
MESH = pl.DeviceIdType.MESH


def half_of(lat):
    return lax.rem(lax.div(lat, 4), 2)


def place_of(lat):
    return lax.div(lat, 8) * 4 + lax.rem(lat, 4)


def lat_of(place, half):
    return lax.div(place, 4) * 8 + half * 4 + lax.rem(place, 4)


def source_place(source, half):
    return jnp.where(source < 4 - 2 * half, source, source + 10)


def worker_lon(worker):
    return lax.div(8 * worker + 4, 3)


def worker_at(lon):
    worker = lax.div(3 * lon + 3, 8)
    return worker, 8 * worker + 4 <= 3 * lon + 2


def filter_tables():
    angle = np.arange(N_LON)[:, None] * np.arange(N_LON)[None, :] % N_LON * (2 * np.pi / N_LON)
    across = np.zeros((2, LEV // 2, N_LON, N_LON, LEV))
    for pair in range(LEV // 2):
        across[0, pair, :, :, 2 * pair] = np.cos(angle)
        across[0, pair, :, :, 2 * pair + 1] = np.sin(angle)
        across[1, pair, :, :, 2 * pair] = -np.sin(angle)
        across[1, pair, :, :, 2 * pair + 1] = np.cos(angle)
    across = across.reshape(LEV * N_LON, LEV * N_LON)
    middle = np.arange(N_LON)[:, None] * np.arange(COLS)[None, :] * (2 * np.pi / NLON)
    twiddle = np.zeros((2, N_LON, LANES), np.float32)
    twiddle[0, :, :COLS] = np.cos(middle)
    twiddle[1, :, :COLS] = np.sin(middle)
    inner = np.arange(COLS)[:, None] * np.arange(COLS)[None, :] % COLS * (2 * np.pi / COLS)
    within = np.zeros((LANES, 2 * LANES))
    within[:COLS, :COLS] = np.cos(inner)
    within[:COLS, LANES : LANES + COLS] = np.sin(inner)
    return [a.astype(np.float32) for a in (across, across.T, within, twiddle)]


def row_factors():
    row = np.arange(NLAT, dtype=np.float32)
    step = np.float32(math.pi / NLAT)
    face = np.sin(((row + np.float32(1.0)) * step).astype(np.float64)).astype(np.float32)
    face[-1] = 0.0
    centre = np.sin(((row + np.float32(0.5)) * step).astype(np.float64)).astype(np.float32)
    below = np.concatenate([np.zeros(1, np.float32), face[:-1]])
    table = np.stack([face, below, centre]).reshape(3, N_LAT, ROWS).transpose(1, 0, 2)
    return np.ascontiguousarray(np.broadcast_to(table[..., None], (N_LAT, 3, ROWS, 128)))


def routing_plan(polar_target, cutoff_wave):
    lat, lon = lax.axis_index("lat"), lax.axis_index("lon")
    half, place = half_of(lat), place_of(lat)
    index = np.arange(NPOLAR)
    glob = np.where(index < NH, index, index + NLAT - NPOLAR)
    home, own_row = glob // ROWS, glob % ROWS
    home_half, home_place = (home // 4) % 2, home // 8 * 4 + home % 4
    home_source = home_half * SOURCES + np.where(
        home_place < 4 - 2 * home_half, home_place, home_place - 10
    )
    seam = np.zeros(NPOLAR, np.int32)
    for pair, low in enumerate(SEAM_LOW):
        for side in range(2):
            row = (home == low + side) & (own_row == (0 if side else ROWS - 1))
            home_source = np.where(row, 2 * SOURCES + 2 * pair + side, home_source)
            seam[row] = 1
    home, own_row, home_source, seam = (
        jnp.asarray(a, jnp.int32)[None, :] for a in (home, own_row, home_source, seam)
    )
    target = polar_target[None, :]
    target_lat = target // SLOTS
    target_code = place_of(target_lat) * 2 + half_of(target_lat)
    worker, is_worker = worker_at(lon)
    worker_home = lat_of(source_place(lax.div(worker, 2), half), half)
    worker_target = place * 2 + lax.rem(worker, 2)
    entry = lax.broadcasted_iota(jnp.int32, (65, 1), 0)
    mine = home == lat
    value = jnp.where(
        entry < 32,
        jnp.where(mine & (target_code == entry), own_row, 0),
        jnp.where(
            entry < 56,
            jnp.where(mine & (own_row == entry - 32), jnp.where(seam == 1, 2 * PLACES, target_code), 0),
            jnp.where(
                entry < 64,
                jnp.where(target == lat * SLOTS + entry - 56, home_source, 0),
                jnp.where(
                    jnp.where(
                        is_worker,
                        (home == worker_home) & (target_code == worker_target),
                        mine & (seam == 1),
                    ),
                    cutoff_wave[None, :],
                    0,
                ),
            ),
        ),
    )
    return jnp.sum(value, axis=1)


def is_any(value, choices):
    found = value == choices[0]
    for choice in choices[1:]:
        found = jnp.logical_or(found, value == choice)
    return found


def split_value(value):
    high = value.astype(jnp.bfloat16)
    low = (value - high.astype(jnp.float32)).astype(jnp.bfloat16)
    return high, low


def mxu(left_side, right_side):
    return jnp.dot(left_side, right_side, preferred_element_type=jnp.float32)


def dot_left(table_high, table_low, value):
    high, low = split_value(value)
    return mxu(table_high, high) + (mxu(table_high, low) + mxu(table_low, high))


def dot_right(value, table_high, table_low):
    high, low = split_value(value)
    return mxu(high, table_high) + (mxu(low, table_high) + mxu(high, table_low))


def band_filter(values, cut, tables):
    fwd_high, fwd_low, inv_high, inv_low, in_high, in_low, cos_mid, sin_mid = tables
    part = N_LON * LEV // 2
    spread = dot_left(fwd_high, fwd_low, values)
    real, imag = spread[:part], spread[part:]
    turned = jnp.concatenate(
        [real * cos_mid + imag * sin_mid, imag * cos_mid - real * sin_mid], axis=0
    )
    parts = dot_right(turned, in_high, in_low)
    real = parts[:part, :LANES] + parts[part:, LANES:]
    imag = parts[part:, :LANES] - parts[:part, LANES:]
    shape = (N_LON, LANES)
    wave = lax.broadcasted_iota(jnp.int32, shape, 0) + N_LON * lax.broadcasted_iota(
        jnp.int32, shape, 1
    )
    scale = jnp.where(jnp.minimum(wave, NLON - wave) <= cut, 1.0 / NLON, 0.0)
    scale = jnp.concatenate([scale] * (LEV // 2), axis=0)
    parts = dot_right(jnp.concatenate([real * scale, imag * scale], axis=0), in_high, in_low)
    real = parts[:part, :LANES] - parts[part:, LANES:]
    imag = parts[part:, :LANES] + parts[:part, LANES:]
    turned = jnp.concatenate(
        [real * cos_mid - imag * sin_mid, imag * cos_mid + real * sin_mid], axis=0
    )
    return dot_left(inv_high, inv_low, turned)


def with_edge_terms(values):
    low, high = values[:, :128], values[:, 128:]
    lane = lax.broadcasted_iota(jnp.int32, low.shape, 1)
    last = COLS - 1 - 128
    count = values.shape[0]
    next_first = pltpu.roll(pltpu.roll(high, 1, 1), count - LEV, 0)
    product = high * next_first
    flux = pltpu.roll(pltpu.roll(high, 127, 1) + product, 128 - (last + 2), 1)
    low = jnp.where(lane == 0, low + pltpu.roll(flux, LEV, 0), low)
    high = jnp.where(lane == last, high - pltpu.roll(product, 126, 1), high)
    return jnp.concatenate([low, jnp.where(lane <= last, high, 0.0)], axis=1)


def each(count, step):
    lax.fori_loop(0, count, lambda k, carry: (step(k), carry)[1], 0)


def widened(block):
    pad = jnp.zeros((LEV, ROWS, LANES - COLS), jnp.float32)
    return jnp.concatenate([block, pad], axis=2).reshape(FLAT, LANES)


def spread_rows(edge):
    return jnp.broadcast_to(edge[:, None, :], (LEV, ROWS, LANES)).reshape(FLAT, LANES)


def substep_kernel(
    plan,
    tracer_hbm,
    zonal_hbm,
    merid_hbm,
    factor_hbm,
    forward_hbm,
    inverse_hbm,
    within_hbm,
    tw_hbm,
    next_out,
    slots_out,
    tracer,
    zonal,
    merid,
    factor,
    forward,
    inverse,
    within,
    fh,
    fl,
    ih,
    il,
    wh,
    wl,
    tw,
    lon_edge,
    east_in,
    west_in,
    south_edge,
    north_edge,
    south_in,
    north_in,
    increment,
    by_row,
    outbound,
    column,
    gathered,
    smoothed,
    returned,
    slot_in,
    homeward,
    seam_own,
    seam_other,
    seam_result,
    load_sem,
    edge_send,
    edge_recv,
    out_send,
    out_recv,
    gather_send,
    gather_recv,
    back_send,
    back_recv,
    cross_send,
    cross_recv,
    home_send,
    home_recv,
    seam_send,
    seam_recv,
    seam_back_send,
    seam_back_recv,
    seam_out_send,
    seam_out_recv,
):
    lon, lat = lax.axis_index("lon"), lax.axis_index("lat")
    half, place = half_of(lat), place_of(lat)
    first_places = 4 - 2 * half
    is_source = jnp.logical_or(place < first_places, place >= first_places + 10)
    source = jnp.where(place < first_places, place, place - 10)
    worker, is_worker = worker_at(lon)
    work_source, work_half = lax.div(worker, 2), lax.rem(worker, 2)
    across = jnp.logical_and(is_worker, work_half != half)
    east, west = lax.rem(lon + 1, N_LON), lax.rem(lon + N_LON - 1, N_LON)
    low_seam = is_any(lat, SEAM_LOW)
    high_seam = is_any(lat, [low + 1 for low in SEAM_LOW])
    at_seam = jnp.logical_or(low_seam, high_seam)
    seam_side = jnp.where(high_seam, 1, 0)
    other_lat = jnp.where(high_seam, lat - 1, lat + 1)
    seam_worker = jnp.logical_and(at_seam, lon == SEAM_LON)
    has_north = jnp.logical_and(lat < N_LAT - 1, jnp.logical_not(low_seam))
    has_south = jnp.logical_and(lat > 0, jnp.logical_not(high_seam))
    all_polar = jnp.logical_or(lat * ROWS + ROWS <= NH, lat * ROWS >= NLAT - NH)

    loads = [
        pltpu.make_async_copy(a, b, load_sem.at[i])
        for i, (a, b) in enumerate(
            [
                (tracer_hbm, tracer),
                (zonal_hbm, zonal),
                (merid_hbm, merid),
                (factor_hbm.at[lat], factor),
                (forward_hbm, forward),
                (inverse_hbm, inverse),
                (within_hbm, within),
                (tw_hbm, tw),
            ]
        )
    ]
    for load in loads:
        load.start()

    barrier = pltpu.get_barrier_semaphore()

    def greet(to_lon, to_lat):
        pl.semaphore_signal(
            barrier, inc=1, device_id={"lon": to_lon, "lat": to_lat}, device_id_type=MESH
        )

    @pl.when(has_north)
    def _():
        greet(lon, lat + 1)

    @pl.when(has_south)
    def _():
        greet(lon, lat - 1)

    each(N_LON, lambda k: greet(k, lat_of(place, 1 - half)))
    each(N_LON - 1, lambda k: greet(lax.rem(lon + 1 + k, N_LON), lat))

    @pl.when(is_source)
    def _():
        each(PLACES - 1, lambda k: greet(lon, lat_of(lax.rem(place + 1 + k, PLACES), half)))

    @pl.when(jnp.logical_not(is_source))
    def _():
        each(SOURCES, lambda k: greet(lon, lat_of(source_place(k, half), half)))

    @pl.when(at_seam)
    def _():
        greet(SEAM_LON, other_lat)

        @pl.when(seam_worker)
        def _():
            each(N_LON, lambda k: greet(lax.rem(lon + k, N_LON), other_lat))

    def send(what, where, send_sem, recv_sem, to_lon, to_lat):
        return pltpu.make_async_remote_copy(
            src_ref=what,
            dst_ref=where,
            send_sem=send_sem,
            recv_sem=recv_sem,
            device_id={"lon": to_lon, "lat": to_lat},
            device_id_type=MESH,
        )

    def take(where, recv_sem):
        send(where, where, recv_sem, recv_sem, lon, lat).wait_recv()

    def sent(what, send_sem):
        send(what, what, send_sem, send_sem, lon, lat).wait_send()

    for load in loads[:4]:
        load.wait()
    t = widened(tracer[...])
    u = widened(zonal[...])
    v = widened(merid[...])
    lane = lax.broadcasted_iota(jnp.int32, (FLAT, LANES), 1)
    narrow = lane[:, :128]
    last = COLS - 1 - 128
    edge = jnp.where(
        narrow == 0,
        t[:, :128],
        jnp.where(
            narrow == 1,
            pltpu.roll(t[:, 128:], 128 + 1 - last, 1),
            pltpu.roll(u[:, 128:], 128 + 2 - last, 1),
        ),
    )
    edge = jnp.concatenate([edge, jnp.zeros((LANES - FLAT, 128), jnp.float32)], axis=0)
    lon_edge[...] = edge.T[:8]
    for level in range(LEV):
        top, bottom = level * ROWS + ROWS - 1, level * ROWS
        south_edge[0, level : level + 1, :] = t[top : top + 1]
        south_edge[1, level : level + 1, :] = v[top : top + 1]
        north_edge[level : level + 1, :] = t[bottom : bottom + 1]

    for load in loads[4:]:
        load.wait()

    @pl.when(jnp.logical_or(is_worker, seam_worker))
    def _():
        fh[...], fl[...] = split_value(forward[...])
        ih[...], il[...] = split_value(inverse[...])
        wh[...], wl[...] = split_value(within[...])

    pl.semaphore_wait(
        barrier,
        2 * N_LON
        - 1
        + jnp.where(is_source, PLACES - 1, SOURCES)
        + jnp.where(has_north, 1, 0)
        + jnp.where(has_south, 1, 0)
        + jnp.where(at_seam, 1, 0)
        + jnp.where(seam_worker, N_LON, 0),
    )

    @pl.when(has_north)
    def _():
        send(south_edge, south_in, edge_send.at[0], edge_recv.at[0], lon, lat + 1).start()

    @pl.when(has_south)
    def _():
        send(north_edge, north_in, edge_send.at[1], edge_recv.at[1], lon, lat - 1).start()

    @pl.when(jnp.logical_not(all_polar))
    def _():
        send(lon_edge, west_in, edge_send.at[2], edge_recv.at[2], east, lat).start()
        send(lon_edge, east_in, edge_send.at[3], edge_recv.at[3], west, lat).start()

    @pl.when(low_seam)
    def _():
        send(
            south_edge, seam_other.at[lon], seam_send.at[0], seam_recv.at[0], SEAM_LON, other_lat
        ).start()

    @pl.when(high_seam)
    def _():
        send(
            north_edge, seam_other.at[lon, 0], seam_send.at[0], seam_recv.at[0], SEAM_LON, other_lat
        ).start()

    @pl.when(jnp.logical_not(has_south))
    def _():
        south_in[...] = jnp.zeros(south_in.shape, jnp.float32)

    @pl.when(jnp.logical_not(has_north))
    def _():
        north_in[...] = jnp.zeros(north_in.shape, jnp.float32)

    def by_lane(i):
        rows = jnp.concatenate([factor[i], factor[i]], axis=1)
        return jnp.broadcast_to(rows[None], (LEV, ROWS, LANES)).reshape(FLAT, LANES)

    def change_within():
        @pl.when(has_south)
        def _():
            take(south_in, edge_recv.at[0])

        @pl.when(has_north)
        def _():
            take(north_in, edge_recv.at[1])

        t, u, v = widened(tracer[...]), widened(zonal[...]), widened(merid[...])
        row = lax.rem(lax.broadcasted_iota(jnp.int32, (FLAT, LANES), 0), ROWS)
        lane = lax.broadcasted_iota(jnp.int32, (FLAT, LANES), 1)
        east_flux = u * (t + pltpu.roll(t, LANES - 1, 1)) * 0.5
        zonal_div = east_flux - pltpu.roll(east_flux, 1, 1)
        above = jnp.where(row == ROWS - 1, spread_rows(north_in[...]), pltpu.roll(t, FLAT - 1, 0))
        north_flux = v * by_lane(0) * (t + above) * 0.5
        below_flux = spread_rows(south_in[1]) * by_lane(1) * (spread_rows(south_in[0]) + t) * 0.5
        south_flux = jnp.where(row == 0, below_flux, pltpu.roll(north_flux, 1, 0))
        change = -courant_number * (zonal_div + (north_flux - south_flux) / by_lane(2))
        return t, u, jnp.where(lane < COLS, change, 0.0), lane

    @pl.when(is_source)
    def _():
        t, u, change, lane = change_within()
        increment[...] = change
        last_wind = 0.5 * courant_number * u[:, COLS - 1 : COLS]
        marked = jnp.where(lane == COLS, t[:, 0:1], change)
        marked = jnp.where(lane == COLS + 1, last_wind, marked)
        marked = jnp.where(lane == COLS + 2, last_wind * t[:, COLS - 1 : COLS], marked)
        for level in range(LEV):
            by_row[:, level, :] = marked[level * ROWS : (level + 1) * ROWS, :]

        @pl.when(low_seam)
        def _():
            seam_own[lon, 0] = by_row[ROWS - 1]
            seam_own[lon, 1] = south_edge[1]

        @pl.when(high_seam)
        def _():
            seam_own[lon, 0] = by_row[0]
            seam_own[lon, 1] = north_edge[...]

        @pl.when(jnp.logical_and(at_seam, lon != SEAM_LON))
        def _():
            send(
                seam_own.at[lon],
                seam_own.at[lon],
                seam_send.at[1],
                seam_recv.at[1],
                SEAM_LON,
                lat,
            ).start()

        def leave(k):
            to = lax.rem(place + 1 + k, PLACES)
            outbound[2 * to] = by_row[plan[2 * to]]
            outbound[2 * to + 1] = by_row[plan[2 * to + 1]]
            send(
                outbound.at[pl.ds(2 * to, 2)],
                column.at[source],
                out_send,
                out_recv.at[source],
                lon,
                lat_of(to, half),
            ).start()

        each(PLACES - 1, leave)
        column[source, 0] = by_row[plan[2 * place]]
        column[source, 1] = by_row[plan[2 * place + 1]]

    def pass_on(s):
        @pl.when(jnp.logical_not(jnp.logical_and(is_source, source == s)))
        def _():
            take(column.at[s], out_recv.at[s])

        for t_half in range(2):
            to = worker_lon(2 * s + t_half)

            @pl.when(to != lon)
            def _():
                send(
                    column.at[s, t_half], gathered.at[lon], gather_send, gather_recv, to, lat
                ).start()

            @pl.when(to == lon)
            def _():
                gathered[lon] = column[s, t_half]

    each(SOURCES, pass_on)

    @pl.when(jnp.logical_not(is_source))
    def _():
        increment[...] = change_within()[2]

    @pl.when(jnp.logical_not(all_polar))
    def _():
        take(west_in, edge_recv.at[2])
        take(east_in, edge_recv.at[3])
        columns = jnp.concatenate(
            [east_in[...], west_in[...], jnp.zeros((112, LANES), jnp.float32)], axis=0
        ).T[:FLAT]
        tracer_east, tracer_west, wind_west = columns[:, 0:1], columns[:, 9:10], columns[:, 10:11]
        t, u = widened(tracer[...]), widened(zonal[...])
        lane = lax.broadcasted_iota(jnp.int32, (FLAT, LANES), 1)
        half_courant = 0.5 * courant_number
        change = increment[...]
        change = jnp.where(lane == COLS - 1, change - half_courant * (u * tracer_east), change)
        change = jnp.where(lane == 0, change + half_courant * (wind_west * (tracer_west + t)), change)
        next_out[...] = (t + change).reshape(LEV, ROWS, LANES)[:, :, :COLS]

    @pl.when(seam_worker)
    def _():
        take(seam_own.at[pl.ds(0, N_LON - 1)], seam_recv.at[1])

        @pl.when(low_seam)
        def _():
            take(seam_other.at[pl.ds(0, N_LON // 2)], seam_recv.at[0])
            scale = -0.5 * courant_number * factor[0, ROWS - 1 :, :] / factor[2, ROWS - 1 :, :]
            scale = jnp.concatenate([scale, scale], axis=1)[None]
            gathered[...] = seam_own[:, 0] + scale * seam_own[:, 1] * seam_other[:, 0]

        @pl.when(high_seam)
        def _():
            take(seam_other, seam_recv.at[0])
            scale = 0.5 * courant_number * factor[1, :1, :] / factor[2, :1, :]
            scale = jnp.concatenate([scale, scale], axis=1)[None]
            gathered[...] = seam_own[:, 0] + scale * seam_other[:, 1] * (
                seam_other[:, 0] + seam_own[:, 1]
            )

    @pl.when(is_worker)
    def _():
        take(gathered.at[pl.ds(0, N_LON - 1)], gather_recv)

    @pl.when(jnp.logical_or(is_worker, seam_worker))
    def _():
        cos_mid = jnp.concatenate([tw[0]] * (LEV // 2), axis=0)
        sin_mid = jnp.concatenate([tw[1]] * (LEV // 2), axis=0)
        tables = (fh[...], fl[...], ih[...], il[...], wh[...], wl[...], cos_mid, sin_mid)
        values = with_edge_terms(gathered[...].reshape(N_LON * LEV, LANES))
        smoothed[...] = band_filter(values, plan[64], tables).reshape(N_LON, LEV, LANES)

    @pl.when(is_worker)
    def _():
        @pl.when(across)
        def _():
            each(
                N_LON,
                lambda k: send(
                    smoothed.at[lax.rem(lon + k, N_LON)],
                    slot_in.at[half * SOURCES + work_source],
                    cross_send,
                    cross_recv,
                    lax.rem(lon + k, N_LON),
                    lat_of(place, 1 - half),
                ).start(),
            )

        each(
            N_LON - 1,
            lambda k: send(
                smoothed.at[lax.rem(lon + 1 + k, N_LON)],
                returned.at[work_source, work_half],
                back_send,
                back_recv.at[work_source],
                lax.rem(lon + 1 + k, N_LON),
                lat,
            ).start(),
        )
        returned[work_source, work_half] = smoothed[lon]

    @pl.when(seam_worker)
    def _():
        each(
            N_LON,
            lambda k: send(
                smoothed.at[lax.rem(lon + k, N_LON)],
                seam_result.at[seam_side],
                seam_back_send.at[0],
                seam_back_recv,
                lax.rem(lon + k, N_LON),
                other_lat,
            ).start(),
        )
        each(
            N_LON - 1,
            lambda k: send(
                smoothed.at[lax.rem(lon + 1 + k, N_LON)],
                seam_result.at[seam_side],
                seam_back_send.at[1],
                seam_back_recv,
                lax.rem(lon + 1 + k, N_LON),
                lat,
            ).start(),
        )
        seam_result[seam_side] = smoothed[lon]

    seam_pair = jnp.where(lat < NLAT // ROWS // 2, 0, 1)
    seam_slots = [slot_in.at[pl.ds(2 * SOURCES + 2 * pair, 2)] for pair in range(2)]

    @pl.when(at_seam)
    def _():
        @pl.when(seam_worker)
        def _():
            take(seam_result.at[0], seam_back_recv)

        @pl.when(jnp.logical_not(seam_worker))
        def _():
            take(seam_result, seam_back_recv)

        own_slots = slot_in.at[pl.ds(2 * SOURCES + 2 * seam_pair, 2)]

        def spread(k):
            to = lat_of(lax.rem(place + 1 + k, PLACES), half)
            send(seam_result, own_slots, seam_out_send, seam_out_recv.at[seam_pair], lon, to).start()

        each(PLACES - 1, spread)
        slot_in[2 * SOURCES + 2 * seam_pair] = seam_result[0]
        slot_in[2 * SOURCES + 2 * seam_pair + 1] = seam_result[1]
        homeward[2 * PLACES] = seam_result[seam_side]

    def go_home(s):
        own = jnp.logical_and(is_worker, work_source == s)

        @pl.when(own)
        def _():
            take(returned.at[s, 0], back_recv.at[s])

        @pl.when(jnp.logical_not(own))
        def _():
            take(returned.at[s], back_recv.at[s])

        stays = jnp.logical_and(is_source, source == s)

        @pl.when(stays)
        def _():
            homeward[2 * place] = returned[s, 0]
            homeward[2 * place + 1] = returned[s, 1]

        @pl.when(jnp.logical_not(stays))
        def _():
            send(
                returned.at[s],
                homeward.at[pl.ds(2 * place, 2)],
                home_send,
                home_recv,
                lon,
                lat_of(source_place(s, half), half),
            ).start()

        slot_in[half * SOURCES + s] = returned[s, half]

    each(SOURCES, go_home)
    take(slot_in.at[pl.ds(0, SOURCES)], cross_recv)
    for pair in range(2):

        @pl.when(jnp.logical_not(jnp.logical_and(at_seam, seam_pair == pair)))
        def _(pair=pair):
            take(seam_slots[pair], seam_out_recv.at[pair])

    for slot in range(SLOTS):
        slots_out[slot] = slot_in[plan[56 + slot]][:, :COLS]

    @pl.when(is_source)
    def _():
        take(homeward.at[pl.ds(0, 2 * PLACES - 2)], home_recv)
        for j in range(ROWS):
            lat_row = lat * ROWS + j
            polar = jnp.logical_or(lat_row < NH, lat_row >= NLAT - NH)
            filtered = homeward[plan[32 + j]][:, :COLS]
            next_out[:, j, :] = jnp.where(polar, tracer[:, j, :] + filtered, next_out[:, j, :])

    @pl.when(has_north)
    def _():
        sent(south_edge, edge_send.at[0])

    @pl.when(has_south)
    def _():
        sent(north_edge, edge_send.at[1])

    @pl.when(jnp.logical_not(all_polar))
    def _():
        sent(lon_edge, edge_send.at[2])
        sent(lon_edge, edge_send.at[3])

    @pl.when(low_seam)
    def _():
        sent(south_edge, seam_send.at[0])

    @pl.when(high_seam)
    def _():
        sent(north_edge, seam_send.at[0])

    @pl.when(at_seam)
    def _():
        sent(homeward.at[pl.ds(0, 2 * PLACES - 2)], seam_out_send)

        @pl.when(jnp.logical_not(seam_worker))
        def _():
            sent(seam_own.at[lon], seam_send.at[1])

        @pl.when(seam_worker)
        def _():
            sent(smoothed, seam_back_send.at[0])
            sent(smoothed.at[pl.ds(0, N_LON - 1)], seam_back_send.at[1])

    @pl.when(is_source)
    def _():
        sent(outbound.at[pl.ds(0, 2 * PLACES - 2)], out_send)
        sent(homeward.at[pl.ds(0, 2 * SOURCES - 2)], home_send)

    @pl.when(jnp.logical_not(is_source))
    def _():
        sent(homeward.at[pl.ds(0, 2 * SOURCES)], home_send)

    @pl.when(is_worker)
    def _():
        sent(smoothed.at[pl.ds(0, 2 * SOURCES - 1)], gather_send)
        sent(smoothed.at[pl.ds(0, N_LON - 1)], back_send)

    @pl.when(jnp.logical_not(is_worker))
    def _():
        sent(smoothed.at[pl.ds(0, 2 * SOURCES)], gather_send)

    @pl.when(across)
    def _():
        sent(smoothed, cross_send)


def shards(tracer, zonal_wind, meridional_wind, polar_target, cutoff_wave):
    plan = routing_plan(polar_target, cutoff_wave)
    tables = [jnp.asarray(table) for table in filter_tables()]
    factors = jnp.asarray(row_factors())
    f32, bf16 = jnp.float32, jnp.bfloat16
    block = (LEV, ROWS, COLS)
    anywhere, in_vmem = pl.BlockSpec(memory_space=pltpu.HBM), pl.BlockSpec(memory_space=pltpu.VMEM)
    dma = pltpu.SemaphoreType.DMA
    square, wide = (LEV * N_LON, LEV * N_LON), (LANES, 2 * LANES)
    message = (LEV, LANES)
    return pl.pallas_call(
        substep_kernel,
        out_shape=(
            jax.ShapeDtypeStruct(block, f32),
            jax.ShapeDtypeStruct((SLOTS, LEV, COLS), f32),
        ),
        in_specs=[pl.BlockSpec(memory_space=pltpu.SMEM)] + [anywhere] * 8,
        out_specs=(in_vmem, in_vmem),
        scratch_shapes=[
            pltpu.VMEM(block, f32),
            pltpu.VMEM(block, f32),
            pltpu.VMEM(block, f32),
            pltpu.VMEM((3, ROWS, 128), f32),
            pltpu.VMEM(square, f32),
            pltpu.VMEM(square, f32),
            pltpu.VMEM(wide, f32),
            pltpu.VMEM(square, bf16),
            pltpu.VMEM(square, bf16),
            pltpu.VMEM(square, bf16),
            pltpu.VMEM(square, bf16),
            pltpu.VMEM(wide, bf16),
            pltpu.VMEM(wide, bf16),
            pltpu.VMEM((2, N_LON, LANES), f32),
            pltpu.VMEM(message, f32),
            pltpu.VMEM(message, f32),
            pltpu.VMEM(message, f32),
            pltpu.VMEM((2, *message), f32),
            pltpu.VMEM(message, f32),
            pltpu.VMEM((2, *message), f32),
            pltpu.VMEM(message, f32),
            pltpu.VMEM((FLAT, LANES), f32),
            pltpu.VMEM((ROWS, *message), f32),
            pltpu.VMEM((2 * PLACES, *message), f32),
            pltpu.VMEM((SOURCES, 2, *message), f32),
            pltpu.VMEM((N_LON, *message), f32),
            pltpu.VMEM((N_LON, *message), f32),
            pltpu.VMEM((SOURCES, 2, *message), f32),
            pltpu.VMEM((2 * SOURCES + 4, *message), f32),
            pltpu.VMEM((2 * PLACES + 1, *message), f32),
            pltpu.VMEM((N_LON, 2, *message), f32),
            pltpu.VMEM((N_LON, 2, *message), f32),
            pltpu.VMEM((2, *message), f32),
            dma((8,)),
            dma((4,)),
            dma((4,)),
            dma,
            dma((SOURCES,)),
            dma,
            dma,
            dma,
            dma((SOURCES,)),
            dma,
            dma,
            dma,
            dma,
            dma((2,)),
            dma((2,)),
            dma((2,)),
            dma,
            dma,
            dma((2,)),
        ],
        compiler_params=pltpu.CompilerParams(
            collective_id=0, has_side_effects=True, vmem_limit_bytes=60 * 2**20
        ),
        name="substep",
    )(plan, tracer, zonal_wind, meridional_wind, factors, *tables)


def solution(mesh):
    placed = (P(None, "lat", "lon"), P(None, "lat", "lon"), P(None, "lat", "lon"), P(), P())
    return jax.shard_map(
        shards,
        mesh=mesh,
        in_specs=placed,
        out_specs=(P(None, "lat", "lon"), P("lat", None, "lon")),
        check_vma=False,
    )
```

```python
import math

import jax
import jax.numpy as jnp
import numpy as np
from jax import lax
from jax.experimental import pallas as pl
from jax.experimental.pallas import tpu as pltpu
from jax.sharding import PartitionSpec as P

courant_number = 0.4
LEV, NLAT, NLON = 8, 768, 7200
NH, NPOLAR, SLOTS = 128, 256, 8
N_LAT, N_LON = 32, 32
ROWS, COLS, LANES = NLAT // N_LAT, NLON // N_LON, 256
FLAT = LEV * ROWS
SOURCES, PLACES = 6, 16
SEAM_LOW = (3, 27)
SEAM_LON = 15
WORKERS_FROM = 4
ENTRIES = 72
MESH = pl.DeviceIdType.MESH


def half_of(lat):
    return lax.rem(lax.div(lat, 4), 2)


def place_of(lat):
    return lax.div(lat, 8) * 4 + lax.rem(lat, 4)


def lat_of(place, half):
    return lax.div(place, 4) * 8 + half * 4 + lax.rem(place, 4)


def source_place(source, half):
    return jnp.where(source < 4 - 2 * half, source, source + 10)


def worker_lon(worker):
    return 2 * worker + WORKERS_FROM


def worker_at(lon):
    worker = lax.div(lon + 32 - WORKERS_FROM, 2) - 16
    found = jnp.logical_and(lon >= WORKERS_FROM, lon < WORKERS_FROM + 4 * SOURCES)
    return worker, jnp.logical_and(found, lax.rem(lon - WORKERS_FROM + 32, 2) == 0)


def alternate(lon, k):
    step = lax.div(k + 1, 2)
    return lax.rem(lon + N_LON + jnp.where(lax.rem(k, 2) == 1, step, -step), N_LON)


def inward(k):
    step = lax.div(k, 2)
    return jnp.where(lax.rem(k, 2) == 1, N_LON - 1 - step, step)


def filter_tables():
    angle = np.arange(N_LON)[:, None] * np.arange(N_LON)[None, :] % N_LON * (2 * np.pi / N_LON)
    across = np.zeros((2, LEV // 2, N_LON, N_LON, LEV))
    for pair in range(LEV // 2):
        across[0, pair, :, :, 2 * pair] = np.cos(angle)
        across[0, pair, :, :, 2 * pair + 1] = np.sin(angle)
        across[1, pair, :, :, 2 * pair] = -np.sin(angle)
        across[1, pair, :, :, 2 * pair + 1] = np.cos(angle)
    across = across.reshape(LEV * N_LON, LEV * N_LON)
    middle = np.arange(N_LON)[:, None] * np.arange(COLS)[None, :] * (2 * np.pi / NLON)
    twiddle = np.zeros((2, N_LON, LANES), np.float32)
    twiddle[0, :, :COLS] = np.cos(middle)
    twiddle[1, :, :COLS] = np.sin(middle)
    inner = np.arange(COLS)[:, None] * np.arange(COLS)[None, :] % COLS * (2 * np.pi / COLS)
    within = np.zeros((LANES, 2 * LANES))
    within[:COLS, :COLS] = np.cos(inner)
    within[:COLS, LANES : LANES + COLS] = np.sin(inner)
    return [a.astype(np.float32) for a in (across, across.T, within, twiddle)]


def row_factors():
    row = np.arange(NLAT, dtype=np.float32)
    step = np.float32(math.pi / NLAT)
    face = np.sin(((row + np.float32(1.0)) * step).astype(np.float64)).astype(np.float32)
    face[-1] = 0.0
    centre = np.sin(((row + np.float32(0.5)) * step).astype(np.float64)).astype(np.float32)
    below = np.concatenate([np.zeros(1, np.float32), face[:-1]])
    table = np.stack([face, below, centre]).reshape(3, N_LAT, ROWS).transpose(1, 0, 2)
    return np.ascontiguousarray(np.broadcast_to(table[..., None], (N_LAT, 3, ROWS, 128)))


def polar_row_table():
    index = np.arange(NPOLAR)
    glob = np.where(index < NH, index, index + NLAT - NPOLAR)
    home, own_row = glob // ROWS, glob % ROWS
    home_half, home_place = (home // 4) % 2, home // 8 * 4 + home % 4
    home_source = home_half * SOURCES + np.where(
        home_place < 4 - 2 * home_half, home_place, home_place - 10
    )
    seam = np.zeros(NPOLAR, np.int32)
    for pair, low in enumerate(SEAM_LOW):
        for side in range(2):
            row = (home == low + side) & (own_row == (0 if side else ROWS - 1))
            home_source = np.where(row, 2 * SOURCES + 2 * pair + side, home_source)
            seam[row] = 1
    return np.stack([home, own_row, home_source, seam] * 2).astype(np.int32)


def routing_plan(target, cutoff, rows, lon, lat):
    half, place = half_of(lat), place_of(lat)
    home, own_row, home_source, seam = (rows[i : i + 1] for i in range(4))
    target = jnp.concatenate([target[0:1], target[1:2]], axis=1)
    cutoff = jnp.concatenate([cutoff[0:1], cutoff[1:2]], axis=1)
    target_lat = target >> 3
    target_code = ((target_lat >> 3) * 4 + (target_lat & 3)) * 2 + ((target_lat >> 2) & 1)
    worker, is_worker = worker_at(lon)
    worker_home = jnp.where(is_worker, lat_of(source_place(lax.div(worker, 2), half), half), lat)
    worker_target = jnp.where(is_worker, place * 2 + lax.rem(worker, 2), -1)
    entry = lax.broadcasted_iota(jnp.int32, (ENTRIES, NPOLAR), 0)
    none = jnp.zeros((ENTRIES, NPOLAR), jnp.int32)
    row_target = jnp.where(seam == 1, 2 * PLACES, target_code)
    filtered_code = jnp.where(is_worker, target_code, jnp.where(seam == 1, -1, 0))
    mine = home == lat
    filtered_here = jnp.where((home == worker_home) & (filtered_code == worker_target), cutoff, 0)
    leaving = jnp.where(mine & (target_code == entry), own_row, none)
    landing = jnp.where(mine & (own_row == entry - 32), row_target, none)
    slot = jnp.where(target == lat * SLOTS + entry - 56, home_source, none)
    value = jnp.where(entry < 32, leaving, jnp.where(entry < 56, landing, slot))
    value = jnp.where(entry < 64, value, jnp.where(entry == 64, filtered_here, none))
    return jnp.sum(value, axis=1, keepdims=True)


def is_any(value, choices):
    found = value == choices[0]
    for choice in choices[1:]:
        found = jnp.logical_or(found, value == choice)
    return found


def split_value(value):
    high = value.astype(jnp.bfloat16)
    low = (value - high.astype(jnp.float32)).astype(jnp.bfloat16)
    return high, low


def mxu(left_side, right_side):
    return jnp.dot(left_side, right_side, preferred_element_type=jnp.float32)


def dot_left(table_high, table_low, value):
    high, low = split_value(value)
    return mxu(table_high, high) + (mxu(table_high, low) + mxu(table_low, high))


def dot_right(value, table_high, table_low):
    high, low = split_value(value)
    return mxu(high, table_high) + (mxu(low, table_high) + mxu(high, table_low))


def band_filter(values, cut, tables):
    fwd_high, fwd_low, inv_high, inv_low, in_high, in_low, cos_mid, sin_mid = tables
    part = N_LON * LEV // 2
    spread = dot_left(fwd_high, fwd_low, values)
    real, imag = spread[:part], spread[part:]
    turned = jnp.concatenate(
        [real * cos_mid + imag * sin_mid, imag * cos_mid - real * sin_mid], axis=0
    )
    parts = dot_right(turned, in_high, in_low)
    real = parts[:part, :LANES] + parts[part:, LANES:]
    imag = parts[part:, :LANES] - parts[:part, LANES:]
    shape = (N_LON, LANES)
    wave = lax.broadcasted_iota(jnp.int32, shape, 0) + N_LON * lax.broadcasted_iota(
        jnp.int32, shape, 1
    )
    scale = jnp.where(jnp.minimum(wave, NLON - wave) <= cut, 1.0 / NLON, 0.0)
    scale = jnp.concatenate([scale] * (LEV // 2), axis=0)
    parts = dot_right(jnp.concatenate([real * scale, imag * scale], axis=0), in_high, in_low)
    real = parts[:part, :LANES] - parts[part:, LANES:]
    imag = parts[part:, :LANES] + parts[:part, LANES:]
    turned = jnp.concatenate(
        [real * cos_mid - imag * sin_mid, imag * cos_mid + real * sin_mid], axis=0
    )
    return dot_left(inv_high, inv_low, turned)


def with_edge_terms(values):
    low, high = values[:, :128], values[:, 128:]
    lane = lax.broadcasted_iota(jnp.int32, low.shape, 1)
    last = COLS - 1 - 128
    count = values.shape[0]
    next_first = pltpu.roll(pltpu.roll(high, 1, 1), count - LEV, 0)
    product = high * next_first
    flux = pltpu.roll(pltpu.roll(high, 127, 1) + product, 128 - (last + 2), 1)
    low = jnp.where(lane == 0, low + pltpu.roll(flux, LEV, 0), low)
    high = jnp.where(lane == last, high - pltpu.roll(product, 126, 1), high)
    return jnp.concatenate([low, jnp.where(lane <= last, high, 0.0)], axis=1)


def each(count, step):
    lax.fori_loop(0, count, lambda k, carry: (step(k), carry)[1], 0)


def widened(block):
    pad = jnp.zeros((LEV, ROWS, LANES - COLS), jnp.float32)
    return jnp.concatenate([block, pad], axis=2).reshape(FLAT, LANES)


def spread_rows(edge):
    return jnp.broadcast_to(edge[:, None, :], (LEV, ROWS, LANES)).reshape(FLAT, LANES)


def substep_kernel(
    target_hbm,
    cutoff_hbm,
    polar_hbm,
    tracer_hbm,
    zonal_hbm,
    merid_hbm,
    factor_hbm,
    forward_hbm,
    inverse_hbm,
    within_hbm,
    tw_hbm,
    next_out,
    slots_out,
    target,
    cutoff,
    polar_rows,
    plan_made,
    plan,
    tracer,
    zonal,
    merid,
    factor,
    forward,
    inverse,
    within,
    fh,
    fl,
    ih,
    il,
    wh,
    wl,
    tw,
    lon_edge,
    east_in,
    west_in,
    south_edge,
    north_edge,
    south_in,
    north_in,
    increment,
    by_row,
    outbound,
    column,
    gathered,
    smoothed,
    returned,
    slot_in,
    homeward,
    seam_own,
    seam_other,
    seam_result,
    load_sem,
    edge_send,
    edge_recv,
    out_send,
    out_recv,
    gather_send,
    gather_recv,
    back_send,
    back_recv,
    cross_send,
    cross_recv,
    home_send,
    home_recv,
    seam_send,
    seam_recv,
    seam_back_send,
    seam_back_recv,
    seam_out_send,
    seam_out_recv,
):
    lon, lat = lax.axis_index("lon"), lax.axis_index("lat")
    half, place = half_of(lat), place_of(lat)
    first_places = 4 - 2 * half
    is_source = jnp.logical_or(place < first_places, place >= first_places + 10)
    source = jnp.where(place < first_places, place, place - 10)
    worker, is_worker = worker_at(lon)
    work_source, work_half = lax.div(worker, 2), lax.rem(worker, 2)
    across = jnp.logical_and(is_worker, work_half != half)
    east, west = lax.rem(lon + 1, N_LON), lax.rem(lon + N_LON - 1, N_LON)
    low_seam = is_any(lat, SEAM_LOW)
    high_seam = is_any(lat, [low + 1 for low in SEAM_LOW])
    at_seam = jnp.logical_or(low_seam, high_seam)
    seam_side = jnp.where(high_seam, 1, 0)
    other_lat = jnp.where(high_seam, lat - 1, lat + 1)
    seam_worker = jnp.logical_and(at_seam, lon == SEAM_LON)
    has_north = jnp.logical_and(lat < N_LAT - 1, jnp.logical_not(low_seam))
    has_south = jnp.logical_and(lat > 0, jnp.logical_not(high_seam))
    all_polar = jnp.logical_or(lat * ROWS + ROWS <= NH, lat * ROWS >= NLAT - NH)

    loads = [
        pltpu.make_async_copy(a, b, load_sem.at[i])
        for i, (a, b) in enumerate(
            [
                (tracer_hbm, tracer),
                (zonal_hbm, zonal),
                (merid_hbm, merid),
                (factor_hbm.at[lat], factor),
                (forward_hbm, forward),
                (inverse_hbm, inverse),
                (within_hbm, within),
                (tw_hbm, tw),
                (target_hbm, target),
                (cutoff_hbm, cutoff),
                (polar_hbm, polar_rows),
            ]
        )
    ]
    for load in loads:
        load.start()

    barrier = pltpu.get_barrier_semaphore()

    def greet(to_lon, to_lat):
        pl.semaphore_signal(
            barrier, inc=1, device_id={"lon": to_lon, "lat": to_lat}, device_id_type=MESH
        )

    @pl.when(has_north)
    def _():
        greet(lon, lat + 1)

    @pl.when(has_south)
    def _():
        greet(lon, lat - 1)

    each(N_LON, lambda k: greet(k, lat_of(place, 1 - half)))
    each(N_LON - 1, lambda k: greet(lax.rem(lon + 1 + k, N_LON), lat))

    @pl.when(is_source)
    def _():
        each(PLACES - 1, lambda k: greet(lon, lat_of(lax.rem(place + 1 + k, PLACES), half)))

    @pl.when(jnp.logical_not(is_source))
    def _():
        each(SOURCES, lambda k: greet(lon, lat_of(source_place(k, half), half)))

    @pl.when(at_seam)
    def _():
        greet(SEAM_LON, other_lat)

        @pl.when(seam_worker)
        def _():
            each(N_LON, lambda k: greet(lax.rem(lon + k, N_LON), other_lat))

    def send(what, where, send_sem, recv_sem, to_lon, to_lat):
        return pltpu.make_async_remote_copy(
            src_ref=what,
            dst_ref=where,
            send_sem=send_sem,
            recv_sem=recv_sem,
            device_id={"lon": to_lon, "lat": to_lat},
            device_id_type=MESH,
        )

    def take(where, recv_sem):
        send(where, where, recv_sem, recv_sem, lon, lat).wait_recv()

    def sent(what, send_sem):
        send(what, what, send_sem, send_sem, lon, lat).wait_send()

    for load in loads[:4]:
        load.wait()
    t = widened(tracer[...])
    u = widened(zonal[...])
    v = widened(merid[...])
    lane = lax.broadcasted_iota(jnp.int32, (FLAT, LANES), 1)
    narrow = lane[:, :128]
    last = COLS - 1 - 128
    edge = jnp.where(
        narrow == 0,
        t[:, :128],
        jnp.where(
            narrow == 1,
            pltpu.roll(t[:, 128:], 128 + 1 - last, 1),
            pltpu.roll(u[:, 128:], 128 + 2 - last, 1),
        ),
    )
    edge = jnp.concatenate([edge, jnp.zeros((LANES - FLAT, 128), jnp.float32)], axis=0)
    lon_edge[...] = edge.T[:8]
    for level in range(LEV):
        top, bottom = level * ROWS + ROWS - 1, level * ROWS
        south_edge[0, level : level + 1, :] = t[top : top + 1]
        south_edge[1, level : level + 1, :] = v[top : top + 1]
        north_edge[level : level + 1, :] = t[bottom : bottom + 1]

    for load in loads[4:]:
        load.wait()
    lookup = routing_plan(target[...], cutoff[...], polar_rows[...], lon, lat)
    plan_made[...] = jnp.broadcast_to(lookup, plan_made.shape)
    plan_load = pltpu.make_async_copy(plan_made, plan, load_sem.at[11])
    plan_load.start()
    plan_load.wait()

    @pl.when(jnp.logical_or(is_worker, seam_worker))
    def _():
        fh[...], fl[...] = split_value(forward[...])
        ih[...], il[...] = split_value(inverse[...])
        wh[...], wl[...] = split_value(within[...])

    pl.semaphore_wait(
        barrier,
        2 * N_LON
        - 1
        + jnp.where(is_source, PLACES - 1, SOURCES)
        + jnp.where(has_north, 1, 0)
        + jnp.where(has_south, 1, 0)
        + jnp.where(at_seam, 1, 0)
        + jnp.where(seam_worker, N_LON, 0),
    )

    @pl.when(has_north)
    def _():
        send(south_edge, south_in, edge_send.at[0], edge_recv.at[0], lon, lat + 1).start()

    @pl.when(has_south)
    def _():
        send(north_edge, north_in, edge_send.at[1], edge_recv.at[1], lon, lat - 1).start()

    @pl.when(jnp.logical_not(all_polar))
    def _():
        send(lon_edge, west_in, edge_send.at[2], edge_recv.at[2], east, lat).start()
        send(lon_edge, east_in, edge_send.at[3], edge_recv.at[3], west, lat).start()

    @pl.when(low_seam)
    def _():
        send(
            south_edge, seam_other.at[lon], seam_send.at[0], seam_recv.at[0], SEAM_LON, other_lat
        ).start()

    @pl.when(high_seam)
    def _():
        send(
            north_edge, seam_other.at[lon, 0], seam_send.at[0], seam_recv.at[0], SEAM_LON, other_lat
        ).start()

    @pl.when(jnp.logical_not(has_south))
    def _():
        south_in[...] = jnp.zeros(south_in.shape, jnp.float32)

    @pl.when(jnp.logical_not(has_north))
    def _():
        north_in[...] = jnp.zeros(north_in.shape, jnp.float32)

    def by_lane(i):
        rows = jnp.concatenate([factor[i], factor[i]], axis=1)
        return jnp.broadcast_to(rows[None], (LEV, ROWS, LANES)).reshape(FLAT, LANES)

    def change_within():
        @pl.when(has_south)
        def _():
            take(south_in, edge_recv.at[0])

        @pl.when(has_north)
        def _():
            take(north_in, edge_recv.at[1])

        t, u, v = widened(tracer[...]), widened(zonal[...]), widened(merid[...])
        row = lax.rem(lax.broadcasted_iota(jnp.int32, (FLAT, LANES), 0), ROWS)
        lane = lax.broadcasted_iota(jnp.int32, (FLAT, LANES), 1)
        east_flux = u * (t + pltpu.roll(t, LANES - 1, 1)) * 0.5
        zonal_div = east_flux - pltpu.roll(east_flux, 1, 1)
        above = jnp.where(row == ROWS - 1, spread_rows(north_in[...]), pltpu.roll(t, FLAT - 1, 0))
        north_flux = v * by_lane(0) * (t + above) * 0.5
        below_flux = spread_rows(south_in[1]) * by_lane(1) * (spread_rows(south_in[0]) + t) * 0.5
        south_flux = jnp.where(row == 0, below_flux, pltpu.roll(north_flux, 1, 0))
        change = -courant_number * (zonal_div + (north_flux - south_flux) / by_lane(2))
        return t, u, jnp.where(lane < COLS, change, 0.0), lane

    @pl.when(is_source)
    def _():
        t, u, change, lane = change_within()
        increment[...] = change
        last_wind = 0.5 * courant_number * u[:, COLS - 1 : COLS]
        marked = jnp.where(lane == COLS, t[:, 0:1], change)
        marked = jnp.where(lane == COLS + 1, last_wind, marked)
        marked = jnp.where(lane == COLS + 2, last_wind * t[:, COLS - 1 : COLS], marked)
        for level in range(LEV):
            by_row[:, level, :] = marked[level * ROWS : (level + 1) * ROWS, :]

        @pl.when(low_seam)
        def _():
            seam_own[lon, 0] = by_row[ROWS - 1]
            seam_own[lon, 1] = south_edge[1]

        @pl.when(high_seam)
        def _():
            seam_own[lon, 0] = by_row[0]
            seam_own[lon, 1] = north_edge[...]

        @pl.when(jnp.logical_and(at_seam, lon != SEAM_LON))
        def _():
            send(
                seam_own.at[lon],
                seam_own.at[lon],
                seam_send.at[1],
                seam_recv.at[1],
                SEAM_LON,
                lat,
            ).start()

        def leave(k):
            to = lax.rem(place + 1 + k, PLACES)
            outbound[2 * to] = by_row[plan[2 * to, 0]]
            outbound[2 * to + 1] = by_row[plan[2 * to + 1, 0]]
            send(
                outbound.at[pl.ds(2 * to, 2)],
                column.at[source],
                out_send,
                out_recv.at[source],
                lon,
                lat_of(to, half),
            ).start()

        each(PLACES - 1, leave)
        column[source, 0] = by_row[plan[2 * place, 0]]
        column[source, 1] = by_row[plan[2 * place + 1, 0]]

    def pass_on(s):
        @pl.when(jnp.logical_not(jnp.logical_and(is_source, source == s)))
        def _():
            take(column.at[s], out_recv.at[s])

        for t_half in range(2):
            to = worker_lon(2 * s + t_half)

            @pl.when(to != lon)
            def _():
                send(
                    column.at[s, t_half], gathered.at[lon], gather_send, gather_recv, to, lat
                ).start()

            @pl.when(to == lon)
            def _():
                gathered[lon] = column[s, t_half]

    each(SOURCES, pass_on)

    @pl.when(jnp.logical_not(is_source))
    def _():
        increment[...] = change_within()[2]

    @pl.when(jnp.logical_not(all_polar))
    def _():
        take(west_in, edge_recv.at[2])
        take(east_in, edge_recv.at[3])
        columns = jnp.concatenate(
            [east_in[...], west_in[...], jnp.zeros((112, LANES), jnp.float32)], axis=0
        ).T[:FLAT]
        tracer_east, tracer_west, wind_west = columns[:, 0:1], columns[:, 9:10], columns[:, 10:11]
        t, u = widened(tracer[...]), widened(zonal[...])
        lane = lax.broadcasted_iota(jnp.int32, (FLAT, LANES), 1)
        half_courant = 0.5 * courant_number
        change = increment[...]
        change = jnp.where(lane == COLS - 1, change - half_courant * (u * tracer_east), change)
        change = jnp.where(lane == 0, change + half_courant * (wind_west * (tracer_west + t)), change)
        next_out[...] = (t + change).reshape(LEV, ROWS, LANES)[:, :, :COLS]

    @pl.when(seam_worker)
    def _():
        take(seam_own.at[pl.ds(0, N_LON - 1)], seam_recv.at[1])

        @pl.when(low_seam)
        def _():
            take(seam_other.at[pl.ds(0, N_LON // 2)], seam_recv.at[0])
            scale = -0.5 * courant_number * factor[0, ROWS - 1 :, :] / factor[2, ROWS - 1 :, :]
            scale = jnp.concatenate([scale, scale], axis=1)[None]
            gathered[...] = seam_own[:, 0] + scale * seam_own[:, 1] * seam_other[:, 0]

        @pl.when(high_seam)
        def _():
            take(seam_other, seam_recv.at[0])
            scale = 0.5 * courant_number * factor[1, :1, :] / factor[2, :1, :]
            scale = jnp.concatenate([scale, scale], axis=1)[None]
            gathered[...] = seam_own[:, 0] + scale * seam_other[:, 1] * (
                seam_other[:, 0] + seam_own[:, 1]
            )

    @pl.when(is_worker)
    def _():
        take(gathered.at[pl.ds(0, N_LON - 1)], gather_recv)

    @pl.when(jnp.logical_or(is_worker, seam_worker))
    def _():
        cos_mid = jnp.concatenate([tw[0]] * (LEV // 2), axis=0)
        sin_mid = jnp.concatenate([tw[1]] * (LEV // 2), axis=0)
        tables = (fh[...], fl[...], ih[...], il[...], wh[...], wl[...], cos_mid, sin_mid)
        values = with_edge_terms(gathered[...].reshape(N_LON * LEV, LANES))
        smoothed[...] = band_filter(values, plan[64, 0], tables).reshape(N_LON, LEV, LANES)

    @pl.when(is_worker)
    def _():
        @pl.when(across)
        def _():
            def far(k):
                to = alternate(lon, k)
                send(
                    smoothed.at[to],
                    slot_in.at[half * SOURCES + work_source],
                    cross_send,
                    cross_recv,
                    to,
                    lat_of(place, 1 - half),
                ).start()

            each(N_LON, far)

        def near(k):
            to = inward(k)

            @pl.when(to != lon)
            def _():
                send(
                    smoothed.at[to],
                    returned.at[work_source, work_half],
                    back_send,
                    back_recv.at[work_source],
                    to,
                    lat,
                ).start()

        each(N_LON, near)
        returned[work_source, work_half] = smoothed[lon]

    @pl.when(seam_worker)
    def _():
        each(
            N_LON,
            lambda k: send(
                smoothed.at[lax.rem(lon + k, N_LON)],
                seam_result.at[seam_side],
                seam_back_send.at[0],
                seam_back_recv,
                lax.rem(lon + k, N_LON),
                other_lat,
            ).start(),
        )
        each(
            N_LON - 1,
            lambda k: send(
                smoothed.at[lax.rem(lon + 1 + k, N_LON)],
                seam_result.at[seam_side],
                seam_back_send.at[1],
                seam_back_recv,
                lax.rem(lon + 1 + k, N_LON),
                lat,
            ).start(),
        )
        seam_result[seam_side] = smoothed[lon]

    seam_pair = jnp.where(lat < NLAT // ROWS // 2, 0, 1)
    seam_slots = [slot_in.at[pl.ds(2 * SOURCES + 2 * pair, 2)] for pair in range(2)]

    @pl.when(at_seam)
    def _():
        @pl.when(seam_worker)
        def _():
            take(seam_result.at[0], seam_back_recv)

        @pl.when(jnp.logical_not(seam_worker))
        def _():
            take(seam_result, seam_back_recv)

        own_slots = slot_in.at[pl.ds(2 * SOURCES + 2 * seam_pair, 2)]

        def spread(k):
            to = lat_of(lax.rem(place + 1 + k, PLACES), half)
            send(seam_result, own_slots, seam_out_send, seam_out_recv.at[seam_pair], lon, to).start()

        each(PLACES - 1, spread)
        slot_in[2 * SOURCES + 2 * seam_pair] = seam_result[0]
        slot_in[2 * SOURCES + 2 * seam_pair + 1] = seam_result[1]
        homeward[2 * PLACES] = seam_result[seam_side]

    def go_home(s):
        own = jnp.logical_and(is_worker, work_source == s)

        @pl.when(own)
        def _():
            take(returned.at[s, 0], back_recv.at[s])

        @pl.when(jnp.logical_not(own))
        def _():
            take(returned.at[s], back_recv.at[s])

        stays = jnp.logical_and(is_source, source == s)

        @pl.when(stays)
        def _():
            homeward[2 * place] = returned[s, 0]
            homeward[2 * place + 1] = returned[s, 1]

        @pl.when(jnp.logical_not(stays))
        def _():
            send(
                returned.at[s],
                homeward.at[pl.ds(2 * place, 2)],
                home_send,
                home_recv,
                lon,
                lat_of(source_place(s, half), half),
            ).start()

        slot_in[half * SOURCES + s] = returned[s, half]

    each(SOURCES, go_home)
    take(slot_in.at[pl.ds(0, SOURCES)], cross_recv)
    for pair in range(2):

        @pl.when(jnp.logical_not(jnp.logical_and(at_seam, seam_pair == pair)))
        def _(pair=pair):
            take(seam_slots[pair], seam_out_recv.at[pair])

    for slot in range(SLOTS):
        slots_out[slot] = slot_in[plan[56 + slot, 0]][:, :COLS]

    @pl.when(is_source)
    def _():
        take(homeward.at[pl.ds(0, 2 * PLACES - 2)], home_recv)
        for j in range(ROWS):
            lat_row = lat * ROWS + j
            polar = jnp.logical_or(lat_row < NH, lat_row >= NLAT - NH)
            filtered = homeward[plan[32 + j, 0]][:, :COLS]
            next_out[:, j, :] = jnp.where(polar, tracer[:, j, :] + filtered, next_out[:, j, :])

    @pl.when(has_north)
    def _():
        sent(south_edge, edge_send.at[0])

    @pl.when(has_south)
    def _():
        sent(north_edge, edge_send.at[1])

    @pl.when(jnp.logical_not(all_polar))
    def _():
        sent(lon_edge, edge_send.at[2])
        sent(lon_edge, edge_send.at[3])

    @pl.when(low_seam)
    def _():
        sent(south_edge, seam_send.at[0])

    @pl.when(high_seam)
    def _():
        sent(north_edge, seam_send.at[0])

    @pl.when(at_seam)
    def _():
        sent(homeward.at[pl.ds(0, 2 * PLACES - 2)], seam_out_send)

        @pl.when(jnp.logical_not(seam_worker))
        def _():
            sent(seam_own.at[lon], seam_send.at[1])

        @pl.when(seam_worker)
        def _():
            sent(smoothed, seam_back_send.at[0])
            sent(smoothed.at[pl.ds(0, N_LON - 1)], seam_back_send.at[1])

    @pl.when(is_source)
    def _():
        sent(outbound.at[pl.ds(0, 2 * PLACES - 2)], out_send)
        sent(homeward.at[pl.ds(0, 2 * SOURCES - 2)], home_send)

    @pl.when(jnp.logical_not(is_source))
    def _():
        sent(homeward.at[pl.ds(0, 2 * SOURCES)], home_send)

    @pl.when(is_worker)
    def _():
        sent(smoothed.at[pl.ds(0, 2 * SOURCES - 1)], gather_send)
        sent(smoothed.at[pl.ds(0, N_LON - 1)], back_send)

    @pl.when(jnp.logical_not(is_worker))
    def _():
        sent(smoothed.at[pl.ds(0, 2 * SOURCES)], gather_send)

    @pl.when(across)
    def _():
        sent(smoothed, cross_send)


def shards(tracer, zonal_wind, meridional_wind, polar_target, cutoff_wave):
    tables = [jnp.asarray(table) for table in filter_tables()]
    factors = jnp.asarray(row_factors())
    f32, bf16 = jnp.float32, jnp.bfloat16
    block = (LEV, ROWS, COLS)
    anywhere, in_vmem = pl.BlockSpec(memory_space=pltpu.HBM), pl.BlockSpec(memory_space=pltpu.VMEM)
    dma = pltpu.SemaphoreType.DMA
    square, wide = (LEV * N_LON, LEV * N_LON), (LANES, 2 * LANES)
    message = (LEV, LANES)
    in_hbm = [
        pltpu.with_memory_space_constraint(a, pltpu.HBM)
        for a in (
            polar_target.reshape(2, NPOLAR // 2),
            cutoff_wave.reshape(2, NPOLAR // 2),
            jnp.asarray(polar_row_table()),
            tracer,
            zonal_wind,
            meridional_wind,
            factors,
            *tables,
        )
    ]
    return pl.pallas_call(
        substep_kernel,
        out_shape=(
            jax.ShapeDtypeStruct(block, f32),
            jax.ShapeDtypeStruct((SLOTS, LEV, COLS), f32),
        ),
        in_specs=[anywhere] * 11,
        out_specs=(in_vmem, in_vmem),
        scratch_shapes=[
            pltpu.VMEM((2, NPOLAR // 2), jnp.int32),
            pltpu.VMEM((2, NPOLAR // 2), jnp.int32),
            pltpu.VMEM((8, NPOLAR), jnp.int32),
            pltpu.VMEM((ENTRIES, 128), jnp.int32),
            pltpu.SMEM((ENTRIES, 128), jnp.int32),
            pltpu.VMEM(block, f32),
            pltpu.VMEM(block, f32),
            pltpu.VMEM(block, f32),
            pltpu.VMEM((3, ROWS, 128), f32),
            pltpu.VMEM(square, f32),
            pltpu.VMEM(square, f32),
            pltpu.VMEM(wide, f32),
            pltpu.VMEM(square, bf16),
            pltpu.VMEM(square, bf16),
            pltpu.VMEM(square, bf16),
            pltpu.VMEM(square, bf16),
            pltpu.VMEM(wide, bf16),
            pltpu.VMEM(wide, bf16),
            pltpu.VMEM((2, N_LON, LANES), f32),
            pltpu.VMEM(message, f32),
            pltpu.VMEM(message, f32),
            pltpu.VMEM(message, f32),
            pltpu.VMEM((2, *message), f32),
            pltpu.VMEM(message, f32),
            pltpu.VMEM((2, *message), f32),
            pltpu.VMEM(message, f32),
            pltpu.VMEM((FLAT, LANES), f32),
            pltpu.VMEM((ROWS, *message), f32),
            pltpu.VMEM((2 * PLACES, *message), f32),
            pltpu.VMEM((SOURCES, 2, *message), f32),
            pltpu.VMEM((N_LON, *message), f32),
            pltpu.VMEM((N_LON, *message), f32),
            pltpu.VMEM((SOURCES, 2, *message), f32),
            pltpu.VMEM((2 * SOURCES + 4, *message), f32),
            pltpu.VMEM((2 * PLACES + 1, *message), f32),
            pltpu.VMEM((N_LON, 2, *message), f32),
            pltpu.VMEM((N_LON, 2, *message), f32),
            pltpu.VMEM((2, *message), f32),
            dma((12,)),
            dma((4,)),
            dma((4,)),
            dma,
            dma((SOURCES,)),
            dma,
            dma,
            dma,
            dma((SOURCES,)),
            dma,
            dma,
            dma,
            dma,
            dma((2,)),
            dma((2,)),
            dma((2,)),
            dma,
            dma,
            dma((2,)),
        ],
        compiler_params=pltpu.CompilerParams(
            collective_id=0, has_side_effects=True, vmem_limit_bytes=32 * 2**20
        ),
        name="substep",
    )(*in_hbm)


def solution(mesh):
    placed = (P(None, "lat", "lon"), P(None, "lat", "lon"), P(None, "lat", "lon"), P(), P())
    return jax.shard_map(
        shards,
        mesh=mesh,
        in_specs=placed,
        out_specs=(P(None, "lat", "lon"), P("lat", None, "lon")),
        check_vma=False,
    )
```

```python
import math

import jax
import jax.numpy as jnp
import numpy as np
from jax import lax
from jax.experimental import pallas as pl
from jax.experimental.pallas import tpu as pltpu
from jax.sharding import PartitionSpec as P

courant_number = 0.4
LEV, NLAT, NLON = 8, 768, 7200
NH, NPOLAR, SLOTS = 128, 256, 8
N_LAT, N_LON = 32, 32
ROWS, COLS, LANES = NLAT // N_LAT, NLON // N_LON, 256
FLAT = LEV * ROWS
SOURCES, PLACES = 6, 16
SEAM_LOW = (3, 27)
SEAM_LON = 15
SEAM_LINES = (3, 4, 27, 28)
RELAYS = (10, 7, 24, 21)
ENTRIES = 72
NEAR = 4
MESH = pl.DeviceIdType.MESH


def half_of(lat):
    return lax.rem(lax.div(lat, 4), 2)


def place_of(lat):
    return lax.div(lat, 8) * 4 + lax.rem(lat, 4)


def lat_of(place, half):
    return lax.div(place, 4) * 8 + half * 4 + lax.rem(place, 4)


def source_place(source, half):
    return jnp.where(source < 4 - 2 * half, source, source + 10)


def worker_lon(worker):
    return 2 * worker + jnp.where(worker < SOURCES, 2, 4)


def worker_at(lon):
    chip = lax.div(lon, 2)
    worker = jnp.where(chip < SEAM_LON // 2, chip - 1, chip - 2)
    found = jnp.logical_and(worker >= 0, worker < 2 * SOURCES)
    found = jnp.logical_and(found, chip != SEAM_LON // 2)
    return worker, jnp.logical_and(found, lax.rem(lon, 2) == 0)


def alternate(lon, k):
    step = lax.div(k + 1, 2)
    return lax.rem(lon + N_LON + jnp.where(lax.rem(k, 2) == 1, step, -step), N_LON)


def inward(k):
    step = lax.div(k, 2)
    return jnp.where(lax.rem(k, 2) == 1, N_LON - 1 - step, step)


def filter_tables():
    angle = np.arange(N_LON)[:, None] * np.arange(N_LON)[None, :] % N_LON * (2 * np.pi / N_LON)
    across = np.zeros((2, LEV // 2, N_LON, N_LON, LEV))
    for pair in range(LEV // 2):
        across[0, pair, :, :, 2 * pair] = np.cos(angle)
        across[0, pair, :, :, 2 * pair + 1] = np.sin(angle)
        across[1, pair, :, :, 2 * pair] = -np.sin(angle)
        across[1, pair, :, :, 2 * pair + 1] = np.cos(angle)
    across = across.reshape(LEV * N_LON, LEV * N_LON)
    middle = np.arange(N_LON)[:, None] * np.arange(COLS)[None, :] * (2 * np.pi / NLON)
    twiddle = np.zeros((2, N_LON, LANES), np.float32)
    twiddle[0, :, :COLS] = np.cos(middle)
    twiddle[1, :, :COLS] = np.sin(middle)
    inner = np.arange(COLS)[:, None] * np.arange(COLS)[None, :] % COLS * (2 * np.pi / COLS)
    within = np.zeros((LANES, 2 * LANES))
    within[:COLS, :COLS] = np.cos(inner)
    within[:COLS, LANES : LANES + COLS] = np.sin(inner)
    return [a.astype(np.float32) for a in (across, across.T, within, twiddle)]


def row_factors():
    row = np.arange(NLAT, dtype=np.float32)
    step = np.float32(math.pi / NLAT)
    face = np.sin(((row + np.float32(1.0)) * step).astype(np.float64)).astype(np.float32)
    face[-1] = 0.0
    centre = np.sin(((row + np.float32(0.5)) * step).astype(np.float64)).astype(np.float32)
    below = np.concatenate([np.zeros(1, np.float32), face[:-1]])
    table = np.stack([face, below, centre]).reshape(3, N_LAT, ROWS).transpose(1, 0, 2)
    return np.ascontiguousarray(np.broadcast_to(table[..., None], (N_LAT, 3, ROWS, 128)))


def polar_row_table():
    index = np.arange(NPOLAR)
    glob = np.where(index < NH, index, index + NLAT - NPOLAR)
    home, own_row = glob // ROWS, glob % ROWS
    home_half, home_place = (home // 4) % 2, home // 8 * 4 + home % 4
    home_source = home_half * SOURCES + np.where(
        home_place < 4 - 2 * home_half, home_place, home_place - 10
    )
    seam = np.zeros(NPOLAR, np.int32)
    for pair, low in enumerate(SEAM_LOW):
        for side in range(2):
            row = (home == low + side) & (own_row == (0 if side else ROWS - 1))
            home_source = np.where(row, 2 * SOURCES + 2 * pair + side, home_source)
            seam[row] = 1
    return np.stack([home, own_row, home_source, seam] * 2).astype(np.int32)


def routing_plan(target, cutoff, rows, lon, lat):
    half, place = half_of(lat), place_of(lat)
    home, own_row, home_source, seam = (rows[i : i + 1] for i in range(4))
    target = jnp.concatenate([target[0:1], target[1:2]], axis=1)
    cutoff = jnp.concatenate([cutoff[0:1], cutoff[1:2]], axis=1)
    target_lat = target >> 3
    target_code = ((target_lat >> 3) * 4 + (target_lat & 3)) * 2 + ((target_lat >> 2) & 1)
    worker, is_worker = worker_at(lon)
    worker_home = jnp.where(is_worker, lat_of(source_place(lax.div(worker, 2), half), half), lat)
    worker_target = jnp.where(is_worker, place * 2 + lax.rem(worker, 2), -1)
    entry = lax.broadcasted_iota(jnp.int32, (ENTRIES, NPOLAR), 0)
    none = jnp.zeros((ENTRIES, NPOLAR), jnp.int32)
    row_target = jnp.where(seam == 1, 2 * PLACES, target_code)
    filtered_code = jnp.where(is_worker, target_code, jnp.where(seam == 1, -1, 0))
    mine = home == lat
    filtered_here = jnp.where((home == worker_home) & (filtered_code == worker_target), cutoff, 0)
    leaving = jnp.where(mine & (target_code == entry), own_row, none)
    landing = jnp.where(mine & (own_row == entry - 32), row_target, none)
    slot = jnp.where(target == lat * SLOTS + entry - 56, home_source, none)
    value = jnp.where(entry < 32, leaving, jnp.where(entry < 56, landing, slot))
    value = jnp.where(entry < 64, value, jnp.where(entry == 64, filtered_here, none))
    return jnp.sum(value, axis=1, keepdims=True)


def is_any(value, choices):
    found = value == choices[0]
    for choice in choices[1:]:
        found = jnp.logical_or(found, value == choice)
    return found


def chosen(value, choices, results):
    found = results[-1]
    for choice, result in zip(choices[:-1], results[:-1]):
        found = jnp.where(value == choice, result, found)
    return found


def split_value(value):
    high = value.astype(jnp.bfloat16)
    low = (value - high.astype(jnp.float32)).astype(jnp.bfloat16)
    return high, low


def mxu(left_side, right_side):
    return jnp.dot(left_side, right_side, preferred_element_type=jnp.float32)


def dot_left(table_high, table_low, value):
    high, low = split_value(value)
    return mxu(table_high, high) + (mxu(table_high, low) + mxu(table_low, high))


def dot_right(value, table_high, table_low):
    high, low = split_value(value)
    return mxu(high, table_high) + (mxu(low, table_high) + mxu(high, table_low))


def band_filter(values, cut, tables):
    fwd_high, fwd_low, inv_high, inv_low, in_high, in_low, cos_mid, sin_mid = tables
    part = N_LON * LEV // 2
    spread = dot_left(fwd_high, fwd_low, values)
    real, imag = spread[:part], spread[part:]
    turned = jnp.concatenate(
        [real * cos_mid + imag * sin_mid, imag * cos_mid - real * sin_mid], axis=0
    )
    parts = dot_right(turned, in_high, in_low)
    real = parts[:part, :LANES] + parts[part:, LANES:]
    imag = parts[part:, :LANES] - parts[:part, LANES:]
    shape = (N_LON, LANES)
    wave = lax.broadcasted_iota(jnp.int32, shape, 0) + N_LON * lax.broadcasted_iota(
        jnp.int32, shape, 1
    )
    scale = jnp.where(jnp.minimum(wave, NLON - wave) <= cut, 1.0 / NLON, 0.0)
    scale = jnp.concatenate([scale] * (LEV // 2), axis=0)
    parts = dot_right(jnp.concatenate([real * scale, imag * scale], axis=0), in_high, in_low)
    real = parts[:part, :LANES] - parts[part:, LANES:]
    imag = parts[part:, :LANES] + parts[:part, LANES:]
    turned = jnp.concatenate(
        [real * cos_mid - imag * sin_mid, imag * cos_mid + real * sin_mid], axis=0
    )
    return dot_left(inv_high, inv_low, turned)


def with_edge_terms(values):
    low, high = values[:, :128], values[:, 128:]
    lane = lax.broadcasted_iota(jnp.int32, low.shape, 1)
    last = COLS - 1 - 128
    count = values.shape[0]
    next_first = pltpu.roll(pltpu.roll(high, 1, 1), count - LEV, 0)
    product = high * next_first
    flux = pltpu.roll(pltpu.roll(high, 127, 1) + product, 128 - (last + 2), 1)
    low = jnp.where(lane == 0, low + pltpu.roll(flux, LEV, 0), low)
    high = jnp.where(lane == last, high - pltpu.roll(product, 126, 1), high)
    return jnp.concatenate([low, jnp.where(lane <= last, high, 0.0)], axis=1)


def each(count, step):
    lax.fori_loop(0, count, lambda k, carry: (step(k), carry)[1], 0)


def widened(block):
    pad = jnp.zeros((LEV, ROWS, LANES - COLS), jnp.float32)
    return jnp.concatenate([block, pad], axis=2).reshape(FLAT, LANES)


def spread_rows(edge):
    return jnp.broadcast_to(edge[:, None, :], (LEV, ROWS, LANES)).reshape(FLAT, LANES)


def substep_kernel(
    target_hbm,
    cutoff_hbm,
    polar_hbm,
    tracer_hbm,
    zonal_hbm,
    merid_hbm,
    factor_hbm,
    forward_hbm,
    inverse_hbm,
    within_hbm,
    tw_hbm,
    next_out,
    slots_out,
    target,
    cutoff,
    polar_rows,
    plan_made,
    plan,
    tracer,
    zonal,
    merid,
    factor,
    forward,
    inverse,
    within,
    fh,
    fl,
    ih,
    il,
    wh,
    wl,
    tw,
    lon_edge,
    east_in,
    west_in,
    south_edge,
    north_edge,
    south_in,
    north_in,
    increment,
    by_row,
    outbound,
    column,
    gathered,
    smoothed,
    returned,
    slot_in,
    homeward,
    seam_own,
    seam_other,
    seam_result,
    far_in,
    load_sem,
    edge_send,
    edge_recv,
    out_send,
    out_recv,
    gather_send,
    gather_recv,
    back_send,
    back_recv,
    cross_send,
    cross_recv,
    home_send,
    home_recv,
    seam_send,
    seam_recv,
    seam_back_send,
    seam_back_recv,
    seam_out_send,
    seam_out_recv,
    line_sem,
    bridge_sem,
    both_sem,
    seam_ready,
    far_send,
    far_recv,
):
    lon, lat = lax.axis_index("lon"), lax.axis_index("lat")
    half, place = half_of(lat), place_of(lat)
    first_places = 4 - 2 * half
    is_source = jnp.logical_or(place < first_places, place >= first_places + 10)
    source = jnp.where(place < first_places, place, place - 10)
    worker, is_worker = worker_at(lon)
    work_source, work_half = lax.div(worker, 2), lax.rem(worker, 2)
    across = jnp.logical_and(is_worker, work_half != half)
    east, west = lax.rem(lon + 1, N_LON), lax.rem(lon + N_LON - 1, N_LON)
    low_seam = is_any(lat, SEAM_LOW)
    high_seam = is_any(lat, [low + 1 for low in SEAM_LOW])
    at_seam = jnp.logical_or(low_seam, high_seam)
    seam_side = jnp.where(high_seam, 1, 0)
    other_lat = jnp.where(high_seam, lat - 1, lat + 1)
    seam_worker = jnp.logical_and(at_seam, lon == SEAM_LON)
    has_north, has_south = lax.rem(lat, 4) != 3, lax.rem(lat, 4) != 0
    far_north = jnp.logical_not(jnp.logical_or(has_north, jnp.logical_or(low_seam, lat == N_LAT - 1)))
    far_south = jnp.logical_not(jnp.logical_or(has_south, jnp.logical_or(high_seam, lat == 0)))
    any_north, any_south = jnp.logical_or(has_north, far_north), jnp.logical_or(has_south, far_south)
    is_relay = is_any(lat, RELAYS)
    served = chosen(lat, RELAYS, SEAM_LINES)
    far_relay = chosen(other_lat, SEAM_LINES, RELAYS)
    z = lax.div(lon, 2)
    opposite = lat_of(place, 1 - half)
    hands_north = jnp.logical_and(
        lax.rem(lat, 4) == 3, jnp.logical_not(is_any(opposite, (*SEAM_LOW, N_LAT - 1)))
    )
    hands_south = jnp.logical_and(
        lax.rem(lat, 4) == 0, jnp.logical_not(is_any(opposite, (0, *[low + 1 for low in SEAM_LOW])))
    )
    z_below, z_above = lax.max(z - NEAR, 0), lax.min(z + NEAR, N_LON // 2 - 1)
    bridge = lon == jnp.where(half == 0, N_LON - 2, 0)
    bridge_to = jnp.where(half == 0, 0, N_LON - 2)
    all_polar = jnp.logical_or(lat * ROWS + ROWS <= NH, lat * ROWS >= NLAT - NH)

    loads = [
        pltpu.make_async_copy(a, b, load_sem.at[i])
        for i, (a, b) in enumerate(
            [
                (tracer_hbm, tracer),
                (zonal_hbm, zonal),
                (merid_hbm, merid),
                (factor_hbm.at[lat], factor),
                (forward_hbm, forward),
                (inverse_hbm, inverse),
                (within_hbm, within),
                (tw_hbm, tw),
                (target_hbm, target),
                (cutoff_hbm, cutoff),
                (polar_hbm, polar_rows),
            ]
        )
    ]
    for load in loads:
        load.start()

    barrier = pltpu.get_barrier_semaphore()

    def greet(to_lon, to_lat):
        pl.semaphore_signal(
            barrier, inc=1, device_id={"lon": to_lon, "lat": to_lat}, device_id_type=MESH
        )

    each(PLACES - 1, lambda k: greet(lon, lat_of(lax.rem(place + 1 + k, PLACES), half)))

    @pl.when(is_relay)
    def _():
        each(N_LON - 1, lambda k: greet(lax.rem(lon + 1 + k, N_LON), lat))

    @pl.when(jnp.logical_not(is_relay))
    def _():
        def greet_near(k):
            @pl.when(z_below * 2 + k != lon)
            def _():
                greet(z_below * 2 + k, lat)

        each(2 * (z_above - z_below + 1), greet_near)

    @pl.when(bridge)
    def _():
        greet(bridge_to, lat_of(place, 1 - half))

    @pl.when(at_seam)
    def _():
        greet(SEAM_LON, far_relay)

        @pl.when(seam_worker)
        def _():
            each(N_LON, lambda k: greet(lax.rem(lon + k, N_LON), far_relay))

    def send(what, where, send_sem, recv_sem, to_lon, to_lat):
        return pltpu.make_async_remote_copy(
            src_ref=what,
            dst_ref=where,
            send_sem=send_sem,
            recv_sem=recv_sem,
            device_id={"lon": to_lon, "lat": to_lat},
            device_id_type=MESH,
        )

    def take(where, recv_sem):
        send(where, where, recv_sem, recv_sem, lon, lat).wait_recv()

    def sent(what, send_sem):
        send(what, what, send_sem, send_sem, lon, lat).wait_send()

    for load in loads[:4]:
        load.wait()
    t = widened(tracer[...])
    u = widened(zonal[...])
    v = widened(merid[...])
    lane = lax.broadcasted_iota(jnp.int32, (FLAT, LANES), 1)
    narrow = lane[:, :128]
    last = COLS - 1 - 128
    edge = jnp.where(
        narrow == 0,
        t[:, :128],
        jnp.where(
            narrow == 1,
            pltpu.roll(t[:, 128:], 128 + 1 - last, 1),
            pltpu.roll(u[:, 128:], 128 + 2 - last, 1),
        ),
    )
    edge = jnp.concatenate([edge, jnp.zeros((LANES - FLAT, 128), jnp.float32)], axis=0)
    lon_edge[...] = edge.T[:8]
    for level in range(LEV):
        top, bottom = level * ROWS + ROWS - 1, level * ROWS
        south_edge[0, level : level + 1, :] = t[top : top + 1]
        south_edge[1, level : level + 1, :] = v[top : top + 1]
        north_edge[level : level + 1, :] = t[bottom : bottom + 1]

    for load in loads[4:]:
        load.wait()
    lookup = routing_plan(target[...], cutoff[...], polar_rows[...], lon, lat)
    plan_made[...] = jnp.broadcast_to(lookup, plan_made.shape)
    plan_load = pltpu.make_async_copy(plan_made, plan, load_sem.at[11])
    plan_load.start()
    plan_load.wait()

    @pl.when(jnp.logical_or(is_worker, seam_worker))
    def _():
        fh[...], fl[...] = split_value(forward[...])
        ih[...], il[...] = split_value(inverse[...])
        wh[...], wl[...] = split_value(within[...])

    pl.semaphore_wait(
        barrier,
        PLACES
        - 1
        + jnp.where(is_relay, N_LON - 1, 2 * (z_above - z_below) + 1)

        + jnp.where(bridge, 1, 0)
        + jnp.where(is_relay, 1, 0)
        + jnp.where(jnp.logical_and(is_relay, lon == SEAM_LON), N_LON, 0),
    )

    @pl.when(has_north)
    def _():
        send(south_edge, south_in, edge_send.at[0], edge_recv.at[0], lon, lat + 1).start()

    @pl.when(has_south)
    def _():
        send(north_edge, north_in, edge_send.at[1], edge_recv.at[1], lon, lat - 1).start()

    def tell(to_lon, to_lat, sem):
        pl.semaphore_signal(
            sem, inc=1, device_id={"lon": to_lon, "lat": to_lat}, device_id_type=MESH
        )

    def tell_along(distance, sem):
        @pl.when(z >= distance)
        def _():
            tell(lon - 2 * distance, lat, sem)

        @pl.when(z + distance < N_LON // 2)
        def _():
            tell(lon + 2 * distance, lat, sem)

    def heard_along(distance, sem):
        pl.semaphore_wait(
            sem,
            jnp.where(z >= distance, 1, 0) + jnp.where(z + distance < N_LON // 2, 1, 0),
        )

    @pl.when(is_relay)
    def _():
        tell(lon, served, seam_ready)

    @pl.when(jnp.logical_not(is_relay))
    def _():
        tell_along(NEAR, line_sem.at[0])

    @pl.when(jnp.logical_not(any_south))
    def _():
        south_in[...] = jnp.zeros(south_in.shape, jnp.float32)

    @pl.when(jnp.logical_not(any_north))
    def _():
        north_in[...] = jnp.zeros(north_in.shape, jnp.float32)

    def by_lane(i):
        rows = jnp.concatenate([factor[i], factor[i]], axis=1)
        return jnp.broadcast_to(rows[None], (LEV, ROWS, LANES)).reshape(FLAT, LANES)

    def change_within():
        @pl.when(any_south)
        def _():
            take(south_in, edge_recv.at[0])

        @pl.when(any_north)
        def _():
            take(north_in, edge_recv.at[1])

        t, u, v = widened(tracer[...]), widened(zonal[...]), widened(merid[...])
        row = lax.rem(lax.broadcasted_iota(jnp.int32, (FLAT, LANES), 0), ROWS)
        lane = lax.broadcasted_iota(jnp.int32, (FLAT, LANES), 1)
        east_flux = u * (t + pltpu.roll(t, LANES - 1, 1)) * 0.5
        zonal_div = east_flux - pltpu.roll(east_flux, 1, 1)
        above = jnp.where(row == ROWS - 1, spread_rows(north_in[...]), pltpu.roll(t, FLAT - 1, 0))
        north_flux = v * by_lane(0) * (t + above) * 0.5
        below_flux = spread_rows(south_in[1]) * by_lane(1) * (spread_rows(south_in[0]) + t) * 0.5
        south_flux = jnp.where(row == 0, below_flux, pltpu.roll(north_flux, 1, 0))
        change = -courant_number * (zonal_div + (north_flux - south_flux) / by_lane(2))
        return t, u, jnp.where(lane < COLS, change, 0.0), lane

    @pl.when(is_source)
    def _():
        t, u, change, lane = change_within()
        increment[...] = change
        last_wind = 0.5 * courant_number * u[:, COLS - 1 : COLS]
        marked = jnp.where(lane == COLS, t[:, 0:1], change)
        marked = jnp.where(lane == COLS + 1, last_wind, marked)
        marked = jnp.where(lane == COLS + 2, last_wind * t[:, COLS - 1 : COLS], marked)
        for level in range(LEV):
            by_row[:, level, :] = marked[level * ROWS : (level + 1) * ROWS, :]

        @pl.when(low_seam)
        def _():
            seam_own[lon, 0] = by_row[ROWS - 1]
            seam_own[lon, 1] = south_edge[1]

        @pl.when(high_seam)
        def _():
            seam_own[lon, 0] = by_row[0]
            seam_own[lon, 1] = north_edge[...]

        def leave(k):
            to = lax.rem(place + 1 + k, PLACES)
            outbound[2 * to] = by_row[plan[2 * to, 0]]
            outbound[2 * to + 1] = by_row[plan[2 * to + 1, 0]]
            send(
                outbound.at[pl.ds(2 * to, 2)],
                column.at[source],
                out_send,
                out_recv.at[source],
                lon,
                lat_of(to, half),
            ).start()

        each(PLACES - 1, leave)
        column[source, 0] = by_row[plan[2 * place, 0]]
        column[source, 1] = by_row[plan[2 * place + 1, 0]]

    @pl.when(jnp.logical_not(is_relay))
    def _():
        heard_along(NEAR, line_sem.at[0])
        tell_along(2 * NEAR, line_sem.at[1])

    @pl.when(at_seam)
    def _():
        pl.semaphore_wait(seam_ready, 1)

    @pl.when(low_seam)
    def _():
        send(
            south_edge, seam_other.at[lon], seam_send.at[0], seam_recv.at[0], SEAM_LON, other_lat
        ).start()

    @pl.when(high_seam)
    def _():
        send(
            north_edge, seam_other.at[lon, 0], seam_send.at[0], seam_recv.at[0], SEAM_LON, other_lat
        ).start()

    @pl.when(jnp.logical_not(is_relay))
    def _():
        heard_along(2 * NEAR, line_sem.at[1])

    @pl.when(jnp.logical_and(at_seam, lon != SEAM_LON))
    def _():
        send(
            seam_own.at[lon],
            seam_own.at[lon],
            seam_send.at[1],
            seam_recv.at[1],
            SEAM_LON,
            lat,
        ).start()

    @pl.when(bridge)
    def _():
        tell(bridge_to, lat_of(place, 1 - half), bridge_sem)
        pl.semaphore_wait(bridge_sem, 1)
        each(N_LON - 1, lambda k: tell(lax.rem(lon + 1 + k, N_LON), lat, both_sem))

    @pl.when(jnp.logical_not(all_polar))
    def _():
        send(lon_edge, west_in, edge_send.at[2], edge_recv.at[2], east, lat).start()
        send(lon_edge, east_in, edge_send.at[3], edge_recv.at[3], west, lat).start()

    def pass_on(s):
        @pl.when(jnp.logical_not(jnp.logical_and(is_source, source == s)))
        def _():
            take(column.at[s], out_recv.at[s])

        for t_half in range(2):
            to = worker_lon(2 * s + t_half)

            @pl.when(to != lon)
            def _():
                send(
                    column.at[s, t_half], gathered.at[lon], gather_send, gather_recv, to, lat
                ).start()

            @pl.when(to == lon)
            def _():
                gathered[lon] = column[s, t_half]

    each(SOURCES, pass_on)

    @pl.when(seam_worker)
    def _():
        take(seam_own.at[pl.ds(0, N_LON - 1)], seam_recv.at[1])

        @pl.when(low_seam)
        def _():
            take(seam_other.at[pl.ds(0, N_LON // 2)], seam_recv.at[0])
            scale = -0.5 * courant_number * factor[0, ROWS - 1 :, :] / factor[2, ROWS - 1 :, :]
            scale = jnp.concatenate([scale, scale], axis=1)[None]
            gathered[...] = seam_own[:, 0] + scale * seam_own[:, 1] * seam_other[:, 0]

        @pl.when(high_seam)
        def _():
            take(seam_other, seam_recv.at[0])
            scale = 0.5 * courant_number * factor[1, :1, :] / factor[2, :1, :]
            scale = jnp.concatenate([scale, scale], axis=1)[None]
            gathered[...] = seam_own[:, 0] + scale * seam_other[:, 1] * (
                seam_other[:, 0] + seam_own[:, 1]
            )

    @pl.when(is_worker)
    def _():
        take(gathered.at[pl.ds(0, N_LON - 1)], gather_recv)

    @pl.when(jnp.logical_or(is_worker, seam_worker))
    def _():
        cos_mid = jnp.concatenate([tw[0]] * (LEV // 2), axis=0)
        sin_mid = jnp.concatenate([tw[1]] * (LEV // 2), axis=0)
        tables = (fh[...], fl[...], ih[...], il[...], wh[...], wl[...], cos_mid, sin_mid)
        values = with_edge_terms(gathered[...].reshape(N_LON * LEV, LANES))
        smoothed[...] = band_filter(values, plan[64, 0], tables).reshape(N_LON, LEV, LANES)

    @pl.when(jnp.logical_not(bridge))
    def _():
        pl.semaphore_wait(both_sem, 1)

    @pl.when(far_north)
    def _():
        send(south_edge, far_in, edge_send.at[0], far_recv, lon, opposite).start()

    @pl.when(far_south)
    def _():
        send(north_edge, far_in.at[0], edge_send.at[1], far_recv, lon, opposite).start()

    @pl.when(is_worker)
    def _():
        @pl.when(across)
        def _():
            def far(k):
                to = alternate(lon, k)
                send(
                    smoothed.at[to],
                    slot_in.at[half * SOURCES + work_source],
                    cross_send,
                    cross_recv,
                    to,
                    lat_of(place, 1 - half),
                ).start()

            each(N_LON, far)

        def near(k):
            to = inward(k)

            @pl.when(to != lon)
            def _():
                send(
                    smoothed.at[to],
                    returned.at[work_source, work_half],
                    back_send,
                    back_recv.at[work_source],
                    to,
                    lat,
                ).start()

        each(N_LON, near)
        returned[work_source, work_half] = smoothed[lon]

    @pl.when(seam_worker)
    def _():
        def to_seam(to, to_lat, sem):
            send(
                smoothed.at[to], seam_result.at[seam_side], sem, seam_back_recv, to, to_lat
            ).start()

        each(N_LON, lambda k: to_seam(alternate(lon, k), other_lat, seam_back_send.at[0]))
        each(N_LON - 1, lambda k: to_seam(alternate(lon, k + 1), lat, seam_back_send.at[1]))
        seam_result[seam_side] = smoothed[lon]

    @pl.when(hands_north)
    def _():
        take(far_in, far_recv)
        send(far_in, south_in, far_send, edge_recv.at[0], lon, opposite + 1).start()

    @pl.when(hands_south)
    def _():
        take(far_in.at[0], far_recv)
        send(far_in.at[0], north_in, far_send, edge_recv.at[1], lon, opposite - 1).start()

    @pl.when(jnp.logical_not(is_source))
    def _():
        increment[...] = change_within()[2]

    @pl.when(jnp.logical_not(all_polar))
    def _():
        take(west_in, edge_recv.at[2])
        take(east_in, edge_recv.at[3])
        columns = jnp.concatenate(
            [east_in[...], west_in[...], jnp.zeros((112, LANES), jnp.float32)], axis=0
        ).T[:FLAT]
        tracer_east, tracer_west, wind_west = columns[:, 0:1], columns[:, 9:10], columns[:, 10:11]
        t, u = widened(tracer[...]), widened(zonal[...])
        lane = lax.broadcasted_iota(jnp.int32, (FLAT, LANES), 1)
        half_courant = 0.5 * courant_number
        change = increment[...]
        change = jnp.where(lane == COLS - 1, change - half_courant * (u * tracer_east), change)
        change = jnp.where(lane == 0, change + half_courant * (wind_west * (tracer_west + t)), change)
        next_out[...] = (t + change).reshape(LEV, ROWS, LANES)[:, :, :COLS]

    seam_pair = jnp.where(lat < NLAT // ROWS // 2, 0, 1)
    seam_slots = [slot_in.at[pl.ds(2 * SOURCES + 2 * pair, 2)] for pair in range(2)]

    @pl.when(at_seam)
    def _():
        @pl.when(seam_worker)
        def _():
            take(seam_result.at[0], seam_back_recv)

        @pl.when(jnp.logical_not(seam_worker))
        def _():
            take(seam_result, seam_back_recv)

        own_slots = slot_in.at[pl.ds(2 * SOURCES + 2 * seam_pair, 2)]

        def spread(k):
            to = lat_of(lax.rem(place + 1 + k, PLACES), half)
            send(seam_result, own_slots, seam_out_send, seam_out_recv.at[seam_pair], lon, to).start()

        each(PLACES - 1, spread)
        slot_in[2 * SOURCES + 2 * seam_pair] = seam_result[0]
        slot_in[2 * SOURCES + 2 * seam_pair + 1] = seam_result[1]
        homeward[2 * PLACES] = seam_result[seam_side]

    def go_home(s):
        own = jnp.logical_and(is_worker, work_source == s)

        @pl.when(own)
        def _():
            take(returned.at[s, 0], back_recv.at[s])

        @pl.when(jnp.logical_not(own))
        def _():
            take(returned.at[s], back_recv.at[s])

        stays = jnp.logical_and(is_source, source == s)

        @pl.when(stays)
        def _():
            homeward[2 * place] = returned[s, 0]
            homeward[2 * place + 1] = returned[s, 1]

        @pl.when(jnp.logical_not(stays))
        def _():
            send(
                returned.at[s],
                homeward.at[pl.ds(2 * place, 2)],
                home_send,
                home_recv,
                lon,
                lat_of(source_place(s, half), half),
            ).start()

        slot_in[half * SOURCES + s] = returned[s, half]

    each(SOURCES, go_home)
    take(slot_in.at[pl.ds(0, SOURCES)], cross_recv)
    for pair in range(2):

        @pl.when(jnp.logical_not(jnp.logical_and(at_seam, seam_pair == pair)))
        def _(pair=pair):
            take(seam_slots[pair], seam_out_recv.at[pair])

    for slot in range(SLOTS):
        slots_out[slot] = slot_in[plan[56 + slot, 0]][:, :COLS]

    @pl.when(is_source)
    def _():
        take(homeward.at[pl.ds(0, 2 * PLACES - 2)], home_recv)
        for j in range(ROWS):
            lat_row = lat * ROWS + j
            polar = jnp.logical_or(lat_row < NH, lat_row >= NLAT - NH)
            filtered = homeward[plan[32 + j, 0]][:, :COLS]
            next_out[:, j, :] = jnp.where(polar, tracer[:, j, :] + filtered, next_out[:, j, :])

    @pl.when(hands_north)
    def _():
        sent(far_in, far_send)

    @pl.when(hands_south)
    def _():
        sent(far_in.at[0], far_send)

    @pl.when(any_north)
    def _():
        sent(south_edge, edge_send.at[0])

    @pl.when(any_south)
    def _():
        sent(north_edge, edge_send.at[1])

    @pl.when(jnp.logical_not(all_polar))
    def _():
        sent(lon_edge, edge_send.at[2])
        sent(lon_edge, edge_send.at[3])

    @pl.when(low_seam)
    def _():
        sent(south_edge, seam_send.at[0])

    @pl.when(high_seam)
    def _():
        sent(north_edge, seam_send.at[0])

    @pl.when(at_seam)
    def _():
        sent(homeward.at[pl.ds(0, 2 * PLACES - 2)], seam_out_send)

        @pl.when(jnp.logical_not(seam_worker))
        def _():
            sent(seam_own.at[lon], seam_send.at[1])

        @pl.when(seam_worker)
        def _():
            sent(smoothed, seam_back_send.at[0])
            sent(smoothed.at[pl.ds(0, N_LON - 1)], seam_back_send.at[1])

    @pl.when(is_source)
    def _():
        sent(outbound.at[pl.ds(0, 2 * PLACES - 2)], out_send)
        sent(homeward.at[pl.ds(0, 2 * SOURCES - 2)], home_send)

    @pl.when(jnp.logical_not(is_source))
    def _():
        sent(homeward.at[pl.ds(0, 2 * SOURCES)], home_send)

    @pl.when(is_worker)
    def _():
        sent(smoothed.at[pl.ds(0, 2 * SOURCES - 1)], gather_send)
        sent(smoothed.at[pl.ds(0, N_LON - 1)], back_send)

    @pl.when(jnp.logical_not(is_worker))
    def _():
        sent(smoothed.at[pl.ds(0, 2 * SOURCES)], gather_send)

    @pl.when(across)
    def _():
        sent(smoothed, cross_send)


def shards(tracer, zonal_wind, meridional_wind, polar_target, cutoff_wave):
    tables = [jnp.asarray(table) for table in filter_tables()]
    factors = jnp.asarray(row_factors())
    f32, bf16 = jnp.float32, jnp.bfloat16
    block = (LEV, ROWS, COLS)
    anywhere, in_vmem = pl.BlockSpec(memory_space=pltpu.HBM), pl.BlockSpec(memory_space=pltpu.VMEM)
    dma = pltpu.SemaphoreType.DMA
    square, wide = (LEV * N_LON, LEV * N_LON), (LANES, 2 * LANES)
    message = (LEV, LANES)
    in_hbm = [
        pltpu.with_memory_space_constraint(a, pltpu.HBM)
        for a in (
            polar_target.reshape(2, NPOLAR // 2),
            cutoff_wave.reshape(2, NPOLAR // 2),
            jnp.asarray(polar_row_table()),
            tracer,
            zonal_wind,
            meridional_wind,
            factors,
            *tables,
        )
    ]
    return pl.pallas_call(
        substep_kernel,
        out_shape=(
            jax.ShapeDtypeStruct(block, f32),
            jax.ShapeDtypeStruct((SLOTS, LEV, COLS), f32),
        ),
        in_specs=[anywhere] * 11,
        out_specs=(in_vmem, in_vmem),
        scratch_shapes=[
            pltpu.VMEM((2, NPOLAR // 2), jnp.int32),
            pltpu.VMEM((2, NPOLAR // 2), jnp.int32),
            pltpu.VMEM((8, NPOLAR), jnp.int32),
            pltpu.VMEM((ENTRIES, 128), jnp.int32),
            pltpu.SMEM((ENTRIES, 128), jnp.int32),
            pltpu.VMEM(block, f32),
            pltpu.VMEM(block, f32),
            pltpu.VMEM(block, f32),
            pltpu.VMEM((3, ROWS, 128), f32),
            pltpu.VMEM(square, f32),
            pltpu.VMEM(square, f32),
            pltpu.VMEM(wide, f32),
            pltpu.VMEM(square, bf16),
            pltpu.VMEM(square, bf16),
            pltpu.VMEM(square, bf16),
            pltpu.VMEM(square, bf16),
            pltpu.VMEM(wide, bf16),
            pltpu.VMEM(wide, bf16),
            pltpu.VMEM((2, N_LON, LANES), f32),
            pltpu.VMEM(message, f32),
            pltpu.VMEM(message, f32),
            pltpu.VMEM(message, f32),
            pltpu.VMEM((2, *message), f32),
            pltpu.VMEM(message, f32),
            pltpu.VMEM((2, *message), f32),
            pltpu.VMEM(message, f32),
            pltpu.VMEM((FLAT, LANES), f32),
            pltpu.VMEM((ROWS, *message), f32),
            pltpu.VMEM((2 * PLACES, *message), f32),
            pltpu.VMEM((SOURCES, 2, *message), f32),
            pltpu.VMEM((N_LON, *message), f32),
            pltpu.VMEM((N_LON, *message), f32),
            pltpu.VMEM((SOURCES, 2, *message), f32),
            pltpu.VMEM((2 * SOURCES + 4, *message), f32),
            pltpu.VMEM((2 * PLACES + 1, *message), f32),
            pltpu.VMEM((N_LON, 2, *message), f32),
            pltpu.VMEM((N_LON, 2, *message), f32),
            pltpu.VMEM((2, *message), f32),
            pltpu.VMEM((2, *message), f32),
            dma((12,)),
            dma((4,)),
            dma((4,)),
            dma,
            dma((SOURCES,)),
            dma,
            dma,
            dma,
            dma((SOURCES,)),
            dma,
            dma,
            dma,
            dma,
            dma((2,)),
            dma((2,)),
            dma((2,)),
            dma,
            dma,
            dma((2,)),
            pltpu.SemaphoreType.REGULAR((2,)),
            pltpu.SemaphoreType.REGULAR,
            pltpu.SemaphoreType.REGULAR,
            pltpu.SemaphoreType.REGULAR,
            dma,
            dma,
        ],
        compiler_params=pltpu.CompilerParams(
            collective_id=0, has_side_effects=True, vmem_limit_bytes=32 * 2**20
        ),
        name="substep",
    )(*in_hbm)


def solution(mesh):
    placed = (P(None, "lat", "lon"), P(None, "lat", "lon"), P(None, "lat", "lon"), P(), P())
    return jax.shard_map(
        shards,
        mesh=mesh,
        in_specs=placed,
        out_specs=(P(None, "lat", "lon"), P("lat", None, "lon")),
        check_vma=False,
    )
```

```python
import math

import jax
import jax.numpy as jnp
import numpy as np
from jax import lax
from jax.experimental import pallas as pl
from jax.experimental.pallas import tpu as pltpu
from jax.sharding import PartitionSpec as P

courant_number = 0.4
LEV, NLAT, NLON = 8, 768, 7200
NH, NPOLAR, SLOTS = 128, 256, 8
N_LAT, N_LON = 32, 32
ROWS, COLS, LANES = NLAT // N_LAT, NLON // N_LON, 256
FLAT = LEV * ROWS
SOURCES, PLACES = 6, 16
SEAM_LOW = (3, 27)
SEAM_LON = 15
SEAM_LINES = (3, 4, 27, 28)
RELAYS = (10, 7, 24, 21)
ENTRIES = 72
NEAR = 4
MESH = pl.DeviceIdType.MESH


def half_of(lat):
    return lax.rem(lax.div(lat, 4), 2)


def place_of(lat):
    return lax.div(lat, 8) * 4 + lax.rem(lat, 4)


def lat_of(place, half):
    return lax.div(place, 4) * 8 + half * 4 + lax.rem(place, 4)


def source_place(source, half):
    return jnp.where(source < 4 - 2 * half, source, source + 10)


def worker_lon(worker):
    return 2 * worker + jnp.where(worker < SOURCES, 2, 4)


def worker_at(lon):
    chip = lax.div(lon, 2)
    worker = jnp.where(chip < SEAM_LON // 2, chip - 1, chip - 2)
    found = jnp.logical_and(worker >= 0, worker < 2 * SOURCES)
    found = jnp.logical_and(found, chip != SEAM_LON // 2)
    return worker, jnp.logical_and(found, lax.rem(lon, 2) == 0)


def alternate(lon, k):
    step = lax.div(k + 1, 2)
    return lax.rem(lon + N_LON + jnp.where(lax.rem(k, 2) == 1, step, -step), N_LON)


def filter_tables():
    angle = np.arange(N_LON)[:, None] * np.arange(N_LON)[None, :] % N_LON * (2 * np.pi / N_LON)
    across = np.zeros((2, LEV // 2, N_LON, N_LON, LEV))
    for pair in range(LEV // 2):
        across[0, pair, :, :, 2 * pair] = np.cos(angle)
        across[0, pair, :, :, 2 * pair + 1] = np.sin(angle)
        across[1, pair, :, :, 2 * pair] = -np.sin(angle)
        across[1, pair, :, :, 2 * pair + 1] = np.cos(angle)
    across = across.reshape(LEV * N_LON, LEV * N_LON)
    middle = np.arange(N_LON)[:, None] * np.arange(COLS)[None, :] * (2 * np.pi / NLON)
    twiddle = np.zeros((2, N_LON, LANES), np.float32)
    twiddle[0, :, :COLS] = np.cos(middle)
    twiddle[1, :, :COLS] = np.sin(middle)
    inner = np.arange(COLS)[:, None] * np.arange(COLS)[None, :] % COLS * (2 * np.pi / COLS)
    within = np.zeros((LANES, 2 * LANES))
    within[:COLS, :COLS] = np.cos(inner)
    within[:COLS, LANES : LANES + COLS] = np.sin(inner)
    return [a.astype(np.float32) for a in (across, across.T, within, twiddle)]


def row_factors():
    row = np.arange(NLAT, dtype=np.float32)
    step = np.float32(math.pi / NLAT)
    face = np.sin(((row + np.float32(1.0)) * step).astype(np.float64)).astype(np.float32)
    face[-1] = 0.0
    centre = np.sin(((row + np.float32(0.5)) * step).astype(np.float64)).astype(np.float32)
    below = np.concatenate([np.zeros(1, np.float32), face[:-1]])
    table = np.stack([face, below, centre]).reshape(3, N_LAT, ROWS).transpose(1, 0, 2)
    return np.ascontiguousarray(np.broadcast_to(table[..., None], (N_LAT, 3, ROWS, 128)))


def polar_row_table():
    index = np.arange(NPOLAR)
    glob = np.where(index < NH, index, index + NLAT - NPOLAR)
    home, own_row = glob // ROWS, glob % ROWS
    home_half, home_place = (home // 4) % 2, home // 8 * 4 + home % 4
    home_source = home_half * SOURCES + np.where(
        home_place < 4 - 2 * home_half, home_place, home_place - 10
    )
    seam = np.zeros(NPOLAR, np.int32)
    for pair, low in enumerate(SEAM_LOW):
        for side in range(2):
            row = (home == low + side) & (own_row == (0 if side else ROWS - 1))
            home_source = np.where(row, 2 * SOURCES + 2 * pair + side, home_source)
            seam[row] = 1
    return np.stack([home, own_row, home_source, seam] * 2).astype(np.int32)


def routing_plan(target, cutoff, rows, lon, lat):
    half, place = half_of(lat), place_of(lat)
    home, own_row, home_source, seam = (rows[i : i + 1] for i in range(4))
    target = jnp.concatenate([target[0:1], target[1:2]], axis=1)
    cutoff = jnp.concatenate([cutoff[0:1], cutoff[1:2]], axis=1)
    target_lat = target >> 3
    target_code = ((target_lat >> 3) * 4 + (target_lat & 3)) * 2 + ((target_lat >> 2) & 1)
    worker, is_worker = worker_at(lon)
    worker_home = jnp.where(is_worker, lat_of(source_place(lax.div(worker, 2), half), half), lat)
    worker_target = jnp.where(is_worker, place * 2 + lax.rem(worker, 2), -1)
    entry = lax.broadcasted_iota(jnp.int32, (ENTRIES, NPOLAR), 0)
    none = jnp.zeros((ENTRIES, NPOLAR), jnp.int32)
    row_target = jnp.where(seam == 1, 2 * PLACES, target_code)
    filtered_code = jnp.where(is_worker, target_code, jnp.where(seam == 1, -1, 0))
    mine = home == lat
    filtered_here = jnp.where((home == worker_home) & (filtered_code == worker_target), cutoff, 0)
    leaving = jnp.where(mine & (target_code == entry), own_row, none)
    landing = jnp.where(mine & (own_row == entry - 32), row_target, none)
    slot = jnp.where(target == lat * SLOTS + entry - 56, home_source, none)
    value = jnp.where(entry < 32, leaving, jnp.where(entry < 56, landing, slot))
    value = jnp.where(entry < 64, value, jnp.where(entry == 64, filtered_here, none))
    return jnp.sum(value, axis=1, keepdims=True)


def is_any(value, choices):
    found = value == choices[0]
    for choice in choices[1:]:
        found = jnp.logical_or(found, value == choice)
    return found


def chosen(value, choices, results):
    found = results[-1]
    for choice, result in zip(choices[:-1], results[:-1]):
        found = jnp.where(value == choice, result, found)
    return found


def split_value(value):
    high = value.astype(jnp.bfloat16)
    low = (value - high.astype(jnp.float32)).astype(jnp.bfloat16)
    return high, low


def mxu(left_side, right_side):
    return jnp.dot(left_side, right_side, preferred_element_type=jnp.float32)


def dot_left(table_high, table_low, value):
    high, low = split_value(value)
    return mxu(table_high, high) + (mxu(table_high, low) + mxu(table_low, high))


def dot_right(value, table_high, table_low):
    high, low = split_value(value)
    return mxu(high, table_high) + (mxu(low, table_high) + mxu(high, table_low))


def band_filter(values, cut, tables):
    fwd_high, fwd_low, inv_high, inv_low, in_high, in_low, cos_mid, sin_mid = tables
    part = N_LON * LEV // 2
    spread = dot_left(fwd_high, fwd_low, values)
    real, imag = spread[:part], spread[part:]
    turned = jnp.concatenate(
        [real * cos_mid + imag * sin_mid, imag * cos_mid - real * sin_mid], axis=0
    )
    parts = dot_right(turned, in_high, in_low)
    real = parts[:part, :LANES] + parts[part:, LANES:]
    imag = parts[part:, :LANES] - parts[:part, LANES:]
    shape = (N_LON, LANES)
    wave = lax.broadcasted_iota(jnp.int32, shape, 0) + N_LON * lax.broadcasted_iota(
        jnp.int32, shape, 1
    )
    scale = jnp.where(jnp.minimum(wave, NLON - wave) <= cut, 1.0 / NLON, 0.0)
    scale = jnp.concatenate([scale] * (LEV // 2), axis=0)
    parts = dot_right(jnp.concatenate([real * scale, imag * scale], axis=0), in_high, in_low)
    real = parts[:part, :LANES] - parts[part:, LANES:]
    imag = parts[part:, :LANES] + parts[:part, LANES:]
    turned = jnp.concatenate(
        [real * cos_mid - imag * sin_mid, imag * cos_mid + real * sin_mid], axis=0
    )
    return dot_left(inv_high, inv_low, turned)


def with_edge_terms(values):
    low, high = values[:, :128], values[:, 128:]
    lane = lax.broadcasted_iota(jnp.int32, low.shape, 1)
    last = COLS - 1 - 128
    count = values.shape[0]
    next_first = pltpu.roll(pltpu.roll(high, 1, 1), count - LEV, 0)
    product = high * next_first
    flux = pltpu.roll(pltpu.roll(high, 127, 1) + product, 128 - (last + 2), 1)
    low = jnp.where(lane == 0, low + pltpu.roll(flux, LEV, 0), low)
    high = jnp.where(lane == last, high - pltpu.roll(product, 126, 1), high)
    return jnp.concatenate([low, jnp.where(lane <= last, high, 0.0)], axis=1)


def each(count, step):
    lax.fori_loop(0, count, lambda k, carry: (step(k), carry)[1], 0)


def widened(block):
    pad = jnp.zeros((LEV, ROWS, LANES - COLS), jnp.float32)
    return jnp.concatenate([block, pad], axis=2).reshape(FLAT, LANES)


def spread_rows(edge):
    return jnp.broadcast_to(edge[:, None, :], (LEV, ROWS, LANES)).reshape(FLAT, LANES)


def substep_kernel(
    target_hbm,
    cutoff_hbm,
    polar_hbm,
    tracer_hbm,
    zonal_hbm,
    merid_hbm,
    factor_hbm,
    forward_hbm,
    inverse_hbm,
    within_hbm,
    tw_hbm,
    next_out,
    slots_out,
    target,
    cutoff,
    polar_rows,
    plan_made,
    plan,
    tracer,
    zonal,
    merid,
    factor,
    forward,
    inverse,
    within,
    fh,
    fl,
    ih,
    il,
    wh,
    wl,
    tw,
    lon_edge,
    east_in,
    west_in,
    south_edge,
    north_edge,
    south_in,
    north_in,
    increment,
    by_row,
    outbound,
    column,
    gathered,
    smoothed,
    returned,
    slot_in,
    homeward,
    seam_own,
    seam_other,
    seam_result,
    far_in,
    load_sem,
    edge_send,
    edge_recv,
    out_send,
    out_recv,
    gather_send,
    gather_recv,
    back_send,
    back_recv,
    cross_send,
    cross_recv,
    home_send,
    home_recv,
    seam_send,
    seam_recv,
    seam_back_send,
    seam_back_recv,
    seam_out_send,
    seam_out_recv,
    line_sem,
    bridge_sem,
    both_sem,
    seam_ready,
    far_send,
    far_recv,
):
    lon, lat = lax.axis_index("lon"), lax.axis_index("lat")
    half, place = half_of(lat), place_of(lat)
    first_places = 4 - 2 * half
    is_source = jnp.logical_or(place < first_places, place >= first_places + 10)
    source = jnp.where(place < first_places, place, place - 10)
    worker, is_worker = worker_at(lon)
    work_source, work_half = lax.div(worker, 2), lax.rem(worker, 2)
    across = jnp.logical_and(is_worker, work_half != half)
    east, west = lax.rem(lon + 1, N_LON), lax.rem(lon + N_LON - 1, N_LON)
    low_seam = is_any(lat, SEAM_LOW)
    high_seam = is_any(lat, [low + 1 for low in SEAM_LOW])
    at_seam = jnp.logical_or(low_seam, high_seam)
    seam_side = jnp.where(high_seam, 1, 0)
    other_lat = jnp.where(high_seam, lat - 1, lat + 1)
    seam_worker = jnp.logical_and(at_seam, lon == SEAM_LON)
    has_north, has_south = lax.rem(lat, 4) != 3, lax.rem(lat, 4) != 0
    far_north = jnp.logical_not(jnp.logical_or(has_north, jnp.logical_or(low_seam, lat == N_LAT - 1)))
    far_south = jnp.logical_not(jnp.logical_or(has_south, jnp.logical_or(high_seam, lat == 0)))
    any_north, any_south = jnp.logical_or(has_north, far_north), jnp.logical_or(has_south, far_south)
    is_relay = is_any(lat, RELAYS)
    served = chosen(lat, RELAYS, SEAM_LINES)
    far_relay = chosen(other_lat, SEAM_LINES, RELAYS)
    z = lax.div(lon, 2)
    opposite = lat_of(place, 1 - half)
    hands_north = jnp.logical_and(
        lax.rem(lat, 4) == 3, jnp.logical_not(is_any(opposite, (*SEAM_LOW, N_LAT - 1)))
    )
    hands_south = jnp.logical_and(
        lax.rem(lat, 4) == 0, jnp.logical_not(is_any(opposite, (0, *[low + 1 for low in SEAM_LOW])))
    )
    z_below, z_above = lax.max(z - NEAR, 0), lax.min(z + NEAR, N_LON // 2 - 1)
    bridge = lon == jnp.where(half == 0, N_LON - 2, 0)
    bridge_to = jnp.where(half == 0, 0, N_LON - 2)
    all_polar = jnp.logical_or(lat * ROWS + ROWS <= NH, lat * ROWS >= NLAT - NH)

    loads = [
        pltpu.make_async_copy(a, b, load_sem.at[i])
        for i, (a, b) in enumerate(
            [
                (tracer_hbm, tracer),
                (zonal_hbm, zonal),
                (merid_hbm, merid),
                (factor_hbm.at[lat], factor),
                (forward_hbm, forward),
                (inverse_hbm, inverse),
                (within_hbm, within),
                (tw_hbm, tw),
                (target_hbm, target),
                (cutoff_hbm, cutoff),
                (polar_hbm, polar_rows),
            ]
        )
    ]
    for load in loads:
        load.start()

    barrier = pltpu.get_barrier_semaphore()

    def greet(to_lon, to_lat):
        pl.semaphore_signal(
            barrier, inc=1, device_id={"lon": to_lon, "lat": to_lat}, device_id_type=MESH
        )

    each(PLACES - 1, lambda k: greet(lon, lat_of(lax.rem(place + 1 + k, PLACES), half)))

    @pl.when(is_relay)
    def _():
        each(N_LON - 1, lambda k: greet(lax.rem(lon + 1 + k, N_LON), lat))

    @pl.when(jnp.logical_not(is_relay))
    def _():
        def greet_near(k):
            @pl.when(z_below * 2 + k != lon)
            def _():
                greet(z_below * 2 + k, lat)

        each(2 * (z_above - z_below + 1), greet_near)

    @pl.when(bridge)
    def _():
        greet(bridge_to, lat_of(place, 1 - half))

    @pl.when(at_seam)
    def _():
        greet(SEAM_LON, far_relay)

        @pl.when(seam_worker)
        def _():
            each(N_LON, lambda k: greet(lax.rem(lon + k, N_LON), far_relay))

    def send(what, where, send_sem, recv_sem, to_lon, to_lat):
        return pltpu.make_async_remote_copy(
            src_ref=what,
            dst_ref=where,
            send_sem=send_sem,
            recv_sem=recv_sem,
            device_id={"lon": to_lon, "lat": to_lat},
            device_id_type=MESH,
        )

    def take(where, recv_sem):
        send(where, where, recv_sem, recv_sem, lon, lat).wait_recv()

    def sent(what, send_sem):
        send(what, what, send_sem, send_sem, lon, lat).wait_send()

    for load in loads[:4]:
        load.wait()
    t = widened(tracer[...])
    u = widened(zonal[...])
    v = widened(merid[...])
    lane = lax.broadcasted_iota(jnp.int32, (FLAT, LANES), 1)
    narrow = lane[:, :128]
    last = COLS - 1 - 128
    edge = jnp.where(
        narrow == 0,
        t[:, :128],
        jnp.where(
            narrow == 1,
            pltpu.roll(t[:, 128:], 128 + 1 - last, 1),
            pltpu.roll(u[:, 128:], 128 + 2 - last, 1),
        ),
    )
    edge = jnp.concatenate([edge, jnp.zeros((LANES - FLAT, 128), jnp.float32)], axis=0)
    lon_edge[...] = edge.T[:8]
    for level in range(LEV):
        top, bottom = level * ROWS + ROWS - 1, level * ROWS
        south_edge[0, level : level + 1, :] = t[top : top + 1]
        south_edge[1, level : level + 1, :] = v[top : top + 1]
        north_edge[level : level + 1, :] = t[bottom : bottom + 1]

    for load in loads[4:]:
        load.wait()
    lookup = routing_plan(target[...], cutoff[...], polar_rows[...], lon, lat)
    plan_made[...] = jnp.broadcast_to(lookup, plan_made.shape)
    plan_load = pltpu.make_async_copy(plan_made, plan, load_sem.at[11])
    plan_load.start()
    plan_load.wait()

    @pl.when(jnp.logical_or(is_worker, seam_worker))
    def _():
        fh[...], fl[...] = split_value(forward[...])
        ih[...], il[...] = split_value(inverse[...])
        wh[...], wl[...] = split_value(within[...])

    pl.semaphore_wait(
        barrier,
        PLACES
        - 1
        + jnp.where(is_relay, N_LON - 1, 2 * (z_above - z_below) + 1)

        + jnp.where(bridge, 1, 0)
        + jnp.where(is_relay, 1, 0)
        + jnp.where(jnp.logical_and(is_relay, lon == SEAM_LON), N_LON, 0),
    )

    @pl.when(has_north)
    def _():
        send(south_edge, south_in, edge_send.at[0], edge_recv.at[0], lon, lat + 1).start()

    @pl.when(has_south)
    def _():
        send(north_edge, north_in, edge_send.at[1], edge_recv.at[1], lon, lat - 1).start()

    def tell(to_lon, to_lat, sem):
        pl.semaphore_signal(
            sem, inc=1, device_id={"lon": to_lon, "lat": to_lat}, device_id_type=MESH
        )

    def tell_along(distance, sem):
        @pl.when(z >= distance)
        def _():
            tell(lon - 2 * distance, lat, sem)

        @pl.when(z + distance < N_LON // 2)
        def _():
            tell(lon + 2 * distance, lat, sem)

    def heard_along(distance, sem):
        pl.semaphore_wait(
            sem,
            jnp.where(z >= distance, 1, 0) + jnp.where(z + distance < N_LON // 2, 1, 0),
        )

    @pl.when(is_relay)
    def _():
        tell(lon, served, seam_ready)

    @pl.when(jnp.logical_not(is_relay))
    def _():
        tell_along(NEAR, line_sem.at[0])

    @pl.when(jnp.logical_not(any_south))
    def _():
        south_in[...] = jnp.zeros(south_in.shape, jnp.float32)

    @pl.when(jnp.logical_not(any_north))
    def _():
        north_in[...] = jnp.zeros(north_in.shape, jnp.float32)

    def by_lane(i):
        rows = jnp.concatenate([factor[i], factor[i]], axis=1)
        return jnp.broadcast_to(rows[None], (LEV, ROWS, LANES)).reshape(FLAT, LANES)

    def change_within():
        @pl.when(any_south)
        def _():
            take(south_in, edge_recv.at[0])

        @pl.when(any_north)
        def _():
            take(north_in, edge_recv.at[1])

        t, u, v = widened(tracer[...]), widened(zonal[...]), widened(merid[...])
        row = lax.rem(lax.broadcasted_iota(jnp.int32, (FLAT, LANES), 0), ROWS)
        lane = lax.broadcasted_iota(jnp.int32, (FLAT, LANES), 1)
        east_flux = u * (t + pltpu.roll(t, LANES - 1, 1)) * 0.5
        zonal_div = east_flux - pltpu.roll(east_flux, 1, 1)
        above = jnp.where(row == ROWS - 1, spread_rows(north_in[...]), pltpu.roll(t, FLAT - 1, 0))
        north_flux = v * by_lane(0) * (t + above) * 0.5
        below_flux = spread_rows(south_in[1]) * by_lane(1) * (spread_rows(south_in[0]) + t) * 0.5
        south_flux = jnp.where(row == 0, below_flux, pltpu.roll(north_flux, 1, 0))
        change = -courant_number * (zonal_div + (north_flux - south_flux) / by_lane(2))
        return t, u, jnp.where(lane < COLS, change, 0.0), lane

    def plain_rows():
        take(west_in, edge_recv.at[2])
        take(east_in, edge_recv.at[3])
        columns = jnp.concatenate(
            [east_in[...], west_in[...], jnp.zeros((112, LANES), jnp.float32)], axis=0
        ).T[:FLAT]
        tracer_east, tracer_west, wind_west = columns[:, 0:1], columns[:, 9:10], columns[:, 10:11]
        t, u = widened(tracer[...]), widened(zonal[...])
        lane = lax.broadcasted_iota(jnp.int32, (FLAT, LANES), 1)
        half_courant = 0.5 * courant_number
        change = increment[...]
        change = jnp.where(lane == COLS - 1, change - half_courant * (u * tracer_east), change)
        change = jnp.where(lane == 0, change + half_courant * (wind_west * (tracer_west + t)), change)
        next_out[...] = (t + change).reshape(LEV, ROWS, LANES)[:, :, :COLS]

    @pl.when(is_source)
    def _():
        t, u, change, lane = change_within()
        increment[...] = change
        last_wind = 0.5 * courant_number * u[:, COLS - 1 : COLS]
        marked = jnp.where(lane == COLS, t[:, 0:1], change)
        marked = jnp.where(lane == COLS + 1, last_wind, marked)
        marked = jnp.where(lane == COLS + 2, last_wind * t[:, COLS - 1 : COLS], marked)
        for level in range(LEV):
            by_row[:, level, :] = marked[level * ROWS : (level + 1) * ROWS, :]

        @pl.when(low_seam)
        def _():
            seam_own[lon, 0] = by_row[ROWS - 1]
            seam_own[lon, 1] = south_edge[1]

        @pl.when(high_seam)
        def _():
            seam_own[lon, 0] = by_row[0]
            seam_own[lon, 1] = north_edge[...]

        def leave(k):
            to = lax.rem(place + 1 + k, PLACES)
            outbound[2 * to] = by_row[plan[2 * to, 0]]
            outbound[2 * to + 1] = by_row[plan[2 * to + 1, 0]]
            send(
                outbound.at[pl.ds(2 * to, 2)],
                column.at[source],
                out_send,
                out_recv.at[source],
                lon,
                lat_of(to, half),
            ).start()

        each(PLACES - 1, leave)
        column[source, 0] = by_row[plan[2 * place, 0]]
        column[source, 1] = by_row[plan[2 * place + 1, 0]]

    @pl.when(jnp.logical_not(is_relay))
    def _():
        heard_along(NEAR, line_sem.at[0])
        tell_along(2 * NEAR, line_sem.at[1])

    @pl.when(at_seam)
    def _():
        pl.semaphore_wait(seam_ready, 1)

    @pl.when(low_seam)
    def _():
        send(
            south_edge, seam_other.at[lon], seam_send.at[0], seam_recv.at[0], SEAM_LON, other_lat
        ).start()

    @pl.when(high_seam)
    def _():
        send(
            north_edge, seam_other.at[lon, 0], seam_send.at[0], seam_recv.at[0], SEAM_LON, other_lat
        ).start()

    @pl.when(jnp.logical_not(is_relay))
    def _():
        heard_along(2 * NEAR, line_sem.at[1])

    @pl.when(jnp.logical_and(at_seam, lon != SEAM_LON))
    def _():
        send(
            seam_own.at[lon],
            seam_own.at[lon],
            seam_send.at[1],
            seam_recv.at[1],
            SEAM_LON,
            lat,
        ).start()

    @pl.when(bridge)
    def _():
        tell(bridge_to, lat_of(place, 1 - half), bridge_sem)
        pl.semaphore_wait(bridge_sem, 1)
        each(N_LON - 1, lambda k: tell(lax.rem(lon + 1 + k, N_LON), lat, both_sem))

    @pl.when(jnp.logical_not(all_polar))
    def _():
        send(lon_edge, west_in, edge_send.at[2], edge_recv.at[2], east, lat).start()
        send(lon_edge, east_in, edge_send.at[3], edge_recv.at[3], west, lat).start()

    def to_worker(s, t_half):
        to = worker_lon(2 * s + t_half)

        @pl.when(to != lon)
        def _():
            send(
                column.at[s, t_half], gathered.at[lon], gather_send, gather_recv, to, lat
            ).start()

        @pl.when(to == lon)
        def _():
            gathered[lon] = column[s, t_half]

    def pass_on(s):
        @pl.when(jnp.logical_not(jnp.logical_and(is_source, source == s)))
        def _():
            take(column.at[s], out_recv.at[s])

        to_worker(s, 0)

        @pl.when(half == 0)
        def _():
            to_worker(s, 1)

    each(SOURCES, pass_on)

    @pl.when(half == 1)
    def _():
        each(SOURCES, lambda s: to_worker(s, 1))

    @pl.when(jnp.logical_not(bridge))
    def _():
        pl.semaphore_wait(both_sem, 1)

    @pl.when(far_north)
    def _():
        send(south_edge, far_in, edge_send.at[0], far_recv, lon, opposite).start()

    @pl.when(far_south)
    def _():
        send(north_edge, far_in.at[0], edge_send.at[1], far_recv, lon, opposite).start()

    @pl.when(seam_worker)
    def _():
        take(seam_own.at[pl.ds(0, N_LON - 1)], seam_recv.at[1])

        @pl.when(low_seam)
        def _():
            take(seam_other.at[pl.ds(0, N_LON // 2)], seam_recv.at[0])
            scale = -0.5 * courant_number * factor[0, ROWS - 1 :, :] / factor[2, ROWS - 1 :, :]
            scale = jnp.concatenate([scale, scale], axis=1)[None]
            gathered[...] = seam_own[:, 0] + scale * seam_own[:, 1] * seam_other[:, 0]

        @pl.when(high_seam)
        def _():
            take(seam_other, seam_recv.at[0])
            scale = 0.5 * courant_number * factor[1, :1, :] / factor[2, :1, :]
            scale = jnp.concatenate([scale, scale], axis=1)[None]
            gathered[...] = seam_own[:, 0] + scale * seam_other[:, 1] * (
                seam_other[:, 0] + seam_own[:, 1]
            )

    @pl.when(is_worker)
    def _():
        take(gathered.at[pl.ds(0, N_LON - 1)], gather_recv)

    @pl.when(jnp.logical_or(is_worker, seam_worker))
    def _():
        cos_mid = jnp.concatenate([tw[0]] * (LEV // 2), axis=0)
        sin_mid = jnp.concatenate([tw[1]] * (LEV // 2), axis=0)
        tables = (fh[...], fl[...], ih[...], il[...], wh[...], wl[...], cos_mid, sin_mid)
        values = with_edge_terms(gathered[...].reshape(N_LON * LEV, LANES))
        smoothed[...] = band_filter(values, plan[64, 0], tables).reshape(N_LON, LEV, LANES)

    @pl.when(is_worker)
    def _():
        def to_slot(to):
            send(
                smoothed.at[to],
                slot_in.at[half * SOURCES + work_source],
                cross_send,
                cross_recv,
                to,
                opposite,
            ).start()

        def to_line(to):
            @pl.when(to != lon)
            def _():
                send(
                    smoothed.at[to],
                    returned.at[work_source, work_half],
                    back_send,
                    back_recv.at[work_source],
                    to,
                    lat,
                ).start()

        @pl.when(jnp.logical_and(across, half == 1))
        def _():
            each(N_LON, to_slot)

        each(N_LON, to_line)

        @pl.when(jnp.logical_and(across, half == 0))
        def _():
            each(N_LON, lambda k: to_slot(alternate(lon, k)))

        returned[work_source, work_half] = smoothed[lon]

    @pl.when(seam_worker)
    def _():
        def to_seam(to, to_lat, sem):
            send(
                smoothed.at[to], seam_result.at[seam_side], sem, seam_back_recv, to, to_lat
            ).start()

        def to_own_line(to):
            @pl.when(to != lon)
            def _():
                to_seam(to, lat, seam_back_send.at[1])

        @pl.when(half == 0)
        def _():
            each(N_LON, to_own_line)

        each(N_LON, lambda to: to_seam(to, other_lat, seam_back_send.at[0]))

        @pl.when(half == 1)
        def _():
            each(N_LON, to_own_line)

        seam_result[seam_side] = smoothed[lon]

    @pl.when(hands_north)
    def _():
        take(far_in, far_recv)
        send(far_in, south_in, far_send, edge_recv.at[0], lon, opposite + 1).start()

    @pl.when(hands_south)
    def _():
        take(far_in.at[0], far_recv)
        send(far_in.at[0], north_in, far_send, edge_recv.at[1], lon, opposite - 1).start()

    @pl.when(jnp.logical_and(is_source, jnp.logical_not(all_polar)))
    def _():
        plain_rows()

    seam_pair = jnp.where(lat < NLAT // ROWS // 2, 0, 1)
    seam_slots = [slot_in.at[pl.ds(2 * SOURCES + 2 * pair, 2)] for pair in range(2)]

    @pl.when(at_seam)
    def _():
        @pl.when(seam_worker)
        def _():
            take(seam_result.at[0], seam_back_recv)

        @pl.when(jnp.logical_not(seam_worker))
        def _():
            take(seam_result, seam_back_recv)

        own_slots = slot_in.at[pl.ds(2 * SOURCES + 2 * seam_pair, 2)]

        def spread(k):
            to = lat_of(lax.rem(place + 1 + k, PLACES), half)
            send(seam_result, own_slots, seam_out_send, seam_out_recv.at[seam_pair], lon, to).start()

        each(PLACES - 1, spread)
        slot_in[2 * SOURCES + 2 * seam_pair] = seam_result[0]
        slot_in[2 * SOURCES + 2 * seam_pair + 1] = seam_result[1]
        homeward[2 * PLACES] = seam_result[seam_side]

    def go_home(s):
        own = jnp.logical_and(is_worker, work_source == s)

        @pl.when(own)
        def _():
            take(returned.at[s, 0], back_recv.at[s])

        @pl.when(jnp.logical_not(own))
        def _():
            take(returned.at[s], back_recv.at[s])

        stays = jnp.logical_and(is_source, source == s)

        @pl.when(stays)
        def _():
            homeward[2 * place] = returned[s, 0]
            homeward[2 * place + 1] = returned[s, 1]

        @pl.when(jnp.logical_not(stays))
        def _():
            send(
                returned.at[s],
                homeward.at[pl.ds(2 * place, 2)],
                home_send,
                home_recv,
                lon,
                lat_of(source_place(s, half), half),
            ).start()

        slot_in[half * SOURCES + s] = returned[s, half]

    each(SOURCES, go_home)
    take(slot_in.at[pl.ds(0, SOURCES)], cross_recv)
    for pair in range(2):

        @pl.when(jnp.logical_not(jnp.logical_and(at_seam, seam_pair == pair)))
        def _(pair=pair):
            take(seam_slots[pair], seam_out_recv.at[pair])

    for slot in range(SLOTS):
        slots_out[slot] = slot_in[plan[56 + slot, 0]][:, :COLS]

    @pl.when(jnp.logical_not(is_source))
    def _():
        increment[...] = change_within()[2]
        plain_rows()

    @pl.when(is_source)
    def _():
        take(homeward.at[pl.ds(0, 2 * PLACES - 2)], home_recv)
        for j in range(ROWS):
            lat_row = lat * ROWS + j
            polar = jnp.logical_or(lat_row < NH, lat_row >= NLAT - NH)
            filtered = homeward[plan[32 + j, 0]][:, :COLS]
            next_out[:, j, :] = jnp.where(polar, tracer[:, j, :] + filtered, next_out[:, j, :])

    @pl.when(hands_north)
    def _():
        sent(far_in, far_send)

    @pl.when(hands_south)
    def _():
        sent(far_in.at[0], far_send)

    @pl.when(any_north)
    def _():
        sent(south_edge, edge_send.at[0])

    @pl.when(any_south)
    def _():
        sent(north_edge, edge_send.at[1])

    @pl.when(jnp.logical_not(all_polar))
    def _():
        sent(lon_edge, edge_send.at[2])
        sent(lon_edge, edge_send.at[3])

    @pl.when(low_seam)
    def _():
        sent(south_edge, seam_send.at[0])

    @pl.when(high_seam)
    def _():
        sent(north_edge, seam_send.at[0])

    @pl.when(at_seam)
    def _():
        sent(homeward.at[pl.ds(0, 2 * PLACES - 2)], seam_out_send)

        @pl.when(jnp.logical_not(seam_worker))
        def _():
            sent(seam_own.at[lon], seam_send.at[1])

        @pl.when(seam_worker)
        def _():
            sent(smoothed, seam_back_send.at[0])
            sent(smoothed.at[pl.ds(0, N_LON - 1)], seam_back_send.at[1])

    @pl.when(is_source)
    def _():
        sent(outbound.at[pl.ds(0, 2 * PLACES - 2)], out_send)
        sent(homeward.at[pl.ds(0, 2 * SOURCES - 2)], home_send)

    @pl.when(jnp.logical_not(is_source))
    def _():
        sent(homeward.at[pl.ds(0, 2 * SOURCES)], home_send)

    @pl.when(is_worker)
    def _():
        sent(smoothed.at[pl.ds(0, 2 * SOURCES - 1)], gather_send)
        sent(smoothed.at[pl.ds(0, N_LON - 1)], back_send)

    @pl.when(jnp.logical_not(is_worker))
    def _():
        sent(smoothed.at[pl.ds(0, 2 * SOURCES)], gather_send)

    @pl.when(across)
    def _():
        sent(smoothed, cross_send)


def shards(tracer, zonal_wind, meridional_wind, polar_target, cutoff_wave):
    tables = [jnp.asarray(table) for table in filter_tables()]
    factors = jnp.asarray(row_factors())
    f32, bf16 = jnp.float32, jnp.bfloat16
    block = (LEV, ROWS, COLS)
    anywhere, in_vmem = pl.BlockSpec(memory_space=pltpu.HBM), pl.BlockSpec(memory_space=pltpu.VMEM)
    dma = pltpu.SemaphoreType.DMA
    square, wide = (LEV * N_LON, LEV * N_LON), (LANES, 2 * LANES)
    message = (LEV, LANES)
    in_hbm = [
        pltpu.with_memory_space_constraint(a, pltpu.HBM)
        for a in (
            polar_target.reshape(2, NPOLAR // 2),
            cutoff_wave.reshape(2, NPOLAR // 2),
            jnp.asarray(polar_row_table()),
            tracer,
            zonal_wind,
            meridional_wind,
            factors,
            *tables,
        )
    ]
    return pl.pallas_call(
        substep_kernel,
        out_shape=(
            jax.ShapeDtypeStruct(block, f32),
            jax.ShapeDtypeStruct((SLOTS, LEV, COLS), f32),
        ),
        in_specs=[anywhere] * 11,
        out_specs=(in_vmem, in_vmem),
        scratch_shapes=[
            pltpu.VMEM((2, NPOLAR // 2), jnp.int32),
            pltpu.VMEM((2, NPOLAR // 2), jnp.int32),
            pltpu.VMEM((8, NPOLAR), jnp.int32),
            pltpu.VMEM((ENTRIES, 128), jnp.int32),
            pltpu.SMEM((ENTRIES, 128), jnp.int32),
            pltpu.VMEM(block, f32),
            pltpu.VMEM(block, f32),
            pltpu.VMEM(block, f32),
            pltpu.VMEM((3, ROWS, 128), f32),
            pltpu.VMEM(square, f32),
            pltpu.VMEM(square, f32),
            pltpu.VMEM(wide, f32),
            pltpu.VMEM(square, bf16),
            pltpu.VMEM(square, bf16),
            pltpu.VMEM(square, bf16),
            pltpu.VMEM(square, bf16),
            pltpu.VMEM(wide, bf16),
            pltpu.VMEM(wide, bf16),
            pltpu.VMEM((2, N_LON, LANES), f32),
            pltpu.VMEM(message, f32),
            pltpu.VMEM(message, f32),
            pltpu.VMEM(message, f32),
            pltpu.VMEM((2, *message), f32),
            pltpu.VMEM(message, f32),
            pltpu.VMEM((2, *message), f32),
            pltpu.VMEM(message, f32),
            pltpu.VMEM((FLAT, LANES), f32),
            pltpu.VMEM((ROWS, *message), f32),
            pltpu.VMEM((2 * PLACES, *message), f32),
            pltpu.VMEM((SOURCES, 2, *message), f32),
            pltpu.VMEM((N_LON, *message), f32),
            pltpu.VMEM((N_LON, *message), f32),
            pltpu.VMEM((SOURCES, 2, *message), f32),
            pltpu.VMEM((2 * SOURCES + 4, *message), f32),
            pltpu.VMEM((2 * PLACES + 1, *message), f32),
            pltpu.VMEM((N_LON, 2, *message), f32),
            pltpu.VMEM((N_LON, 2, *message), f32),
            pltpu.VMEM((2, *message), f32),
            pltpu.VMEM((2, *message), f32),
            dma((12,)),
            dma((4,)),
            dma((4,)),
            dma,
            dma((SOURCES,)),
            dma,
            dma,
            dma,
            dma((SOURCES,)),
            dma,
            dma,
            dma,
            dma,
            dma((2,)),
            dma((2,)),
            dma((2,)),
            dma,
            dma,
            dma((2,)),
            pltpu.SemaphoreType.REGULAR((2,)),
            pltpu.SemaphoreType.REGULAR,
            pltpu.SemaphoreType.REGULAR,
            pltpu.SemaphoreType.REGULAR,
            dma,
            dma,
        ],
        compiler_params=pltpu.CompilerParams(
            collective_id=0, has_side_effects=True, vmem_limit_bytes=32 * 2**20
        ),
        name="substep",
    )(*in_hbm)


def solution(mesh):
    placed = (P(None, "lat", "lon"), P(None, "lat", "lon"), P(None, "lat", "lon"), P(), P())
    return jax.shard_map(
        shards,
        mesh=mesh,
        in_specs=placed,
        out_specs=(P(None, "lat", "lon"), P("lat", None, "lon")),
        check_vma=False,
    )
```

```python
import math

import jax
import jax.numpy as jnp
import numpy as np
from jax import lax
from jax.experimental import pallas as pl
from jax.experimental.pallas import tpu as pltpu
from jax.sharding import PartitionSpec as P

courant_number = 0.4
LEV, NLAT, NLON = 8, 768, 7200
NH, NPOLAR, SLOTS = 128, 256, 8
N_LAT, N_LON = 32, 32
ROWS, COLS, LANES = NLAT // N_LAT, NLON // N_LON, 256
FLAT = LEV * ROWS
SOURCES, PLACES = 6, 16
SEAM_LOW = (3, 27)
SEAM_LON = 15
LATE_SEAM_LON = 21
SEAM_LINES = (3, 4, 27, 28)
RELAYS = (10, 7, 24, 21)
ENTRIES = 72
NEAR = 4
MESH = pl.DeviceIdType.MESH


def half_of(lat):
    return lax.rem(lax.div(lat, 4), 2)


def place_of(lat):
    return lax.div(lat, 8) * 4 + lax.rem(lat, 4)


def lat_of(place, half):
    return lax.div(place, 4) * 8 + half * 4 + lax.rem(place, 4)


def source_place(source, half):
    return jnp.where(source < 4 - 2 * half, source, source + 10)


def worker_lon(worker):
    return 2 * worker + jnp.where(worker < SOURCES, 2, 4)


def worker_at(lon):
    chip = lax.div(lon, 2)
    worker = jnp.where(chip < SEAM_LON // 2, chip - 1, chip - 2)
    found = jnp.logical_and(worker >= 0, worker < 2 * SOURCES)
    found = jnp.logical_and(found, chip != SEAM_LON // 2)
    return worker, jnp.logical_and(found, lax.rem(lon, 2) == 0)


def alternate(lon, k):
    step = lax.div(k + 1, 2)
    return lax.rem(lon + N_LON + jnp.where(lax.rem(k, 2) == 1, step, -step), N_LON)


def filter_tables():
    angle = np.arange(N_LON)[:, None] * np.arange(N_LON)[None, :] % N_LON * (2 * np.pi / N_LON)
    across = np.zeros((2, LEV // 2, N_LON, N_LON, LEV))
    for pair in range(LEV // 2):
        across[0, pair, :, :, 2 * pair] = np.cos(angle)
        across[0, pair, :, :, 2 * pair + 1] = np.sin(angle)
        across[1, pair, :, :, 2 * pair] = -np.sin(angle)
        across[1, pair, :, :, 2 * pair + 1] = np.cos(angle)
    across = across.reshape(LEV * N_LON, LEV * N_LON)
    middle = np.arange(N_LON)[:, None] * np.arange(COLS)[None, :] * (2 * np.pi / NLON)
    twiddle = np.zeros((2, N_LON, LANES), np.float32)
    twiddle[0, :, :COLS] = np.cos(middle)
    twiddle[1, :, :COLS] = np.sin(middle)
    inner = np.arange(COLS)[:, None] * np.arange(COLS)[None, :] % COLS * (2 * np.pi / COLS)
    within = np.zeros((LANES, 2 * LANES))
    within[:COLS, :COLS] = np.cos(inner)
    within[:COLS, LANES : LANES + COLS] = np.sin(inner)
    return [a.astype(np.float32) for a in (across, across.T, within, twiddle)]


def row_factors():
    row = np.arange(NLAT, dtype=np.float32)
    step = np.float32(math.pi / NLAT)
    face = np.sin(((row + np.float32(1.0)) * step).astype(np.float64)).astype(np.float32)
    face[-1] = 0.0
    centre = np.sin(((row + np.float32(0.5)) * step).astype(np.float64)).astype(np.float32)
    below = np.concatenate([np.zeros(1, np.float32), face[:-1]])
    table = np.stack([face, below, centre]).reshape(3, N_LAT, ROWS).transpose(1, 0, 2)
    return np.ascontiguousarray(np.broadcast_to(table[..., None], (N_LAT, 3, ROWS, 128)))


def polar_row_table():
    index = np.arange(NPOLAR)
    glob = np.where(index < NH, index, index + NLAT - NPOLAR)
    home, own_row = glob // ROWS, glob % ROWS
    home_half, home_place = (home // 4) % 2, home // 8 * 4 + home % 4
    home_source = home_half * SOURCES + np.where(
        home_place < 4 - 2 * home_half, home_place, home_place - 10
    )
    seam = np.zeros(NPOLAR, np.int32)
    for pair, low in enumerate(SEAM_LOW):
        for side in range(2):
            row = (home == low + side) & (own_row == (0 if side else ROWS - 1))
            home_source = np.where(row, 2 * SOURCES + 2 * pair + side, home_source)
            seam[row] = 1
    return np.stack([home, own_row, home_source, seam] * 2).astype(np.int32)


def routing_plan(target, cutoff, rows, lon, lat):
    half, place = half_of(lat), place_of(lat)
    home, own_row, home_source, seam = (rows[i : i + 1] for i in range(4))
    target = jnp.concatenate([target[0:1], target[1:2]], axis=1)
    cutoff = jnp.concatenate([cutoff[0:1], cutoff[1:2]], axis=1)
    target_lat = target >> 3
    target_code = ((target_lat >> 3) * 4 + (target_lat & 3)) * 2 + ((target_lat >> 2) & 1)
    worker, is_worker = worker_at(lon)
    worker_home = jnp.where(is_worker, lat_of(source_place(lax.div(worker, 2), half), half), lat)
    worker_target = jnp.where(is_worker, place * 2 + lax.rem(worker, 2), -1)
    entry = lax.broadcasted_iota(jnp.int32, (ENTRIES, NPOLAR), 0)
    none = jnp.zeros((ENTRIES, NPOLAR), jnp.int32)
    row_target = jnp.where(seam == 1, 2 * PLACES, target_code)
    filtered_code = jnp.where(is_worker, target_code, jnp.where(seam == 1, -1, 0))
    mine = home == lat
    filtered_here = jnp.where((home == worker_home) & (filtered_code == worker_target), cutoff, 0)
    leaving = jnp.where(mine & (target_code == entry), own_row, none)
    landing = jnp.where(mine & (own_row == entry - 32), row_target, none)
    slot = jnp.where(target == lat * SLOTS + entry - 56, home_source, none)
    value = jnp.where(entry < 32, leaving, jnp.where(entry < 56, landing, slot))
    value = jnp.where(entry < 64, value, jnp.where(entry == 64, filtered_here, none))
    return jnp.sum(value, axis=1, keepdims=True)


def is_any(value, choices):
    found = value == choices[0]
    for choice in choices[1:]:
        found = jnp.logical_or(found, value == choice)
    return found


def chosen(value, choices, results):
    found = results[-1]
    for choice, result in zip(choices[:-1], results[:-1]):
        found = jnp.where(value == choice, result, found)
    return found


def split_value(value):
    high = value.astype(jnp.bfloat16)
    low = (value - high.astype(jnp.float32)).astype(jnp.bfloat16)
    return high, low


def mxu(left_side, right_side):
    return jnp.dot(left_side, right_side, preferred_element_type=jnp.float32)


def dot_left(table_high, table_low, value):
    high, low = split_value(value)
    return mxu(table_high, high) + (mxu(table_high, low) + mxu(table_low, high))


def dot_right(value, table_high, table_low):
    high, low = split_value(value)
    return mxu(high, table_high) + (mxu(low, table_high) + mxu(high, table_low))


def band_filter(values, cut, tables):
    fwd_high, fwd_low, inv_high, inv_low, in_high, in_low, cos_mid, sin_mid = tables
    part = N_LON * LEV // 2
    spread = dot_left(fwd_high, fwd_low, values)
    real, imag = spread[:part], spread[part:]
    turned = jnp.concatenate(
        [real * cos_mid + imag * sin_mid, imag * cos_mid - real * sin_mid], axis=0
    )
    parts = dot_right(turned, in_high, in_low)
    real = parts[:part, :LANES] + parts[part:, LANES:]
    imag = parts[part:, :LANES] - parts[:part, LANES:]
    shape = (N_LON, LANES)
    wave = lax.broadcasted_iota(jnp.int32, shape, 0) + N_LON * lax.broadcasted_iota(
        jnp.int32, shape, 1
    )
    scale = jnp.where(jnp.minimum(wave, NLON - wave) <= cut, 1.0 / NLON, 0.0)
    scale = jnp.concatenate([scale] * (LEV // 2), axis=0)
    parts = dot_right(jnp.concatenate([real * scale, imag * scale], axis=0), in_high, in_low)
    real = parts[:part, :LANES] - parts[part:, LANES:]
    imag = parts[part:, :LANES] + parts[:part, LANES:]
    turned = jnp.concatenate(
        [real * cos_mid - imag * sin_mid, imag * cos_mid + real * sin_mid], axis=0
    )
    return dot_left(inv_high, inv_low, turned)


def with_edge_terms(values):
    low, high = values[:, :128], values[:, 128:]
    lane = lax.broadcasted_iota(jnp.int32, low.shape, 1)
    last = COLS - 1 - 128
    count = values.shape[0]
    next_first = pltpu.roll(pltpu.roll(high, 1, 1), count - LEV, 0)
    product = high * next_first
    flux = pltpu.roll(pltpu.roll(high, 127, 1) + product, 128 - (last + 2), 1)
    low = jnp.where(lane == 0, low + pltpu.roll(flux, LEV, 0), low)
    high = jnp.where(lane == last, high - pltpu.roll(product, 126, 1), high)
    return jnp.concatenate([low, jnp.where(lane <= last, high, 0.0)], axis=1)


def each(count, step):
    lax.fori_loop(0, count, lambda k, carry: (step(k), carry)[1], 0)


def widened(block):
    pad = jnp.zeros((LEV, ROWS, LANES - COLS), jnp.float32)
    return jnp.concatenate([block, pad], axis=2).reshape(FLAT, LANES)


def substep_kernel(
    target_hbm,
    cutoff_hbm,
    polar_hbm,
    tracer_hbm,
    zonal_hbm,
    merid_hbm,
    factor_hbm,
    forward_hbm,
    inverse_hbm,
    within_hbm,
    tw_hbm,
    next_out,
    slots_out,
    target,
    cutoff,
    polar_rows,
    plan_made,
    plan,
    tracer,
    zonal,
    merid,
    factor,
    forward,
    inverse,
    within,
    fh,
    fl,
    ih,
    il,
    wh,
    wl,
    tw,
    lon_edge,
    east_in,
    west_in,
    south_edge,
    north_edge,
    south_in,
    north_in,
    increment,
    by_row,
    outbound,
    column,
    gathered,
    smoothed,
    returned,
    slot_in,
    homeward,
    seam_own,
    seam_other,
    seam_result,
    far_in,
    load_sem,
    edge_send,
    edge_recv,
    out_send,
    out_recv,
    gather_send,
    gather_recv,
    back_send,
    back_recv,
    cross_send,
    cross_recv,
    home_send,
    home_recv,
    seam_send,
    seam_recv,
    seam_back_send,
    seam_back_recv,
    seam_out_send,
    seam_out_recv,
    line_sem,
    bridge_sem,
    both_sem,
    seam_ready,
    far_send,
    far_recv,
):
    lon, lat = lax.axis_index("lon"), lax.axis_index("lat")
    half, place = half_of(lat), place_of(lat)
    first_places = 4 - 2 * half
    is_source = jnp.logical_or(place < first_places, place >= first_places + 10)
    source = jnp.where(place < first_places, place, place - 10)
    worker, is_worker = worker_at(lon)
    work_source, work_half = lax.div(worker, 2), lax.rem(worker, 2)
    across = jnp.logical_and(is_worker, work_half != half)
    east, west = lax.rem(lon + 1, N_LON), lax.rem(lon + N_LON - 1, N_LON)
    own_seam_lon = jnp.where(half == 0, SEAM_LON, LATE_SEAM_LON)
    other_seam_lon = jnp.where(half == 0, LATE_SEAM_LON, SEAM_LON)
    low_seam = is_any(lat, SEAM_LOW)
    high_seam = is_any(lat, [low + 1 for low in SEAM_LOW])
    at_seam = jnp.logical_or(low_seam, high_seam)
    seam_side = jnp.where(high_seam, 1, 0)
    other_lat = jnp.where(high_seam, lat - 1, lat + 1)
    seam_worker = jnp.logical_and(at_seam, lon == own_seam_lon)
    has_north, has_south = lax.rem(lat, 4) != 3, lax.rem(lat, 4) != 0
    far_north = jnp.logical_not(jnp.logical_or(has_north, jnp.logical_or(low_seam, lat == N_LAT - 1)))
    far_south = jnp.logical_not(jnp.logical_or(has_south, jnp.logical_or(high_seam, lat == 0)))
    any_north, any_south = jnp.logical_or(has_north, far_north), jnp.logical_or(has_south, far_south)
    is_relay = is_any(lat, RELAYS)
    served = chosen(lat, RELAYS, SEAM_LINES)
    far_relay = chosen(other_lat, SEAM_LINES, RELAYS)
    z = lax.div(lon, 2)
    opposite = lat_of(place, 1 - half)
    hands_north = jnp.logical_and(
        lax.rem(lat, 4) == 3, jnp.logical_not(is_any(opposite, (*SEAM_LOW, N_LAT - 1)))
    )
    hands_south = jnp.logical_and(
        lax.rem(lat, 4) == 0, jnp.logical_not(is_any(opposite, (0, *[low + 1 for low in SEAM_LOW])))
    )
    z_below, z_above = lax.max(z - NEAR, 0), lax.min(z + NEAR, N_LON // 2 - 1)
    bridge = lon == jnp.where(half == 0, N_LON - 2, 0)
    bridge_to = jnp.where(half == 0, 0, N_LON - 2)
    all_polar = jnp.logical_or(lat * ROWS + ROWS <= NH, lat * ROWS >= NLAT - NH)

    loads = [
        pltpu.make_async_copy(a, b, load_sem.at[i])
        for i, (a, b) in enumerate(
            [
                (tracer_hbm, tracer),
                (zonal_hbm, zonal),
                (merid_hbm, merid),
                (factor_hbm.at[lat], factor),
                (forward_hbm, forward),
                (inverse_hbm, inverse),
                (within_hbm, within),
                (tw_hbm, tw),
                (target_hbm, target),
                (cutoff_hbm, cutoff),
                (polar_hbm, polar_rows),
            ]
        )
    ]
    for load in loads:
        load.start()

    barrier = pltpu.get_barrier_semaphore()

    def greet(to_lon, to_lat):
        pl.semaphore_signal(
            barrier, inc=1, device_id={"lon": to_lon, "lat": to_lat}, device_id_type=MESH
        )

    each(PLACES - 1, lambda k: greet(lon, lat_of(lax.rem(place + 1 + k, PLACES), half)))

    @pl.when(is_relay)
    def _():
        each(N_LON - 1, lambda k: greet(lax.rem(lon + 1 + k, N_LON), lat))

    @pl.when(jnp.logical_not(is_relay))
    def _():
        def greet_near(k):
            @pl.when(z_below * 2 + k != lon)
            def _():
                greet(z_below * 2 + k, lat)

        each(2 * (z_above - z_below + 1), greet_near)

    @pl.when(bridge)
    def _():
        greet(bridge_to, lat_of(place, 1 - half))

    @pl.when(at_seam)
    def _():
        greet(other_seam_lon, far_relay)

        @pl.when(seam_worker)
        def _():
            each(N_LON, lambda k: greet(lax.rem(lon + k, N_LON), far_relay))

    def send(what, where, send_sem, recv_sem, to_lon, to_lat):
        return pltpu.make_async_remote_copy(
            src_ref=what,
            dst_ref=where,
            send_sem=send_sem,
            recv_sem=recv_sem,
            device_id={"lon": to_lon, "lat": to_lat},
            device_id_type=MESH,
        )

    def take(where, recv_sem):
        send(where, where, recv_sem, recv_sem, lon, lat).wait_recv()

    def sent(what, send_sem):
        send(what, what, send_sem, send_sem, lon, lat).wait_send()

    for load in loads[:4]:
        load.wait()
    t = widened(tracer[...])
    u = widened(zonal[...])
    v = widened(merid[...])
    lane = lax.broadcasted_iota(jnp.int32, (FLAT, LANES), 1)
    narrow = lane[:, :128]
    last = COLS - 1 - 128
    edge = jnp.where(
        narrow == 0,
        t[:, :128],
        jnp.where(
            narrow == 1,
            pltpu.roll(t[:, 128:], 128 + 1 - last, 1),
            pltpu.roll(u[:, 128:], 128 + 2 - last, 1),
        ),
    )
    edge = jnp.concatenate([edge, jnp.zeros((LANES - FLAT, 128), jnp.float32)], axis=0)
    lon_edge[...] = edge.T[:8]
    for level in range(LEV):
        top, bottom = level * ROWS + ROWS - 1, level * ROWS
        south_edge[0, level : level + 1, :] = t[top : top + 1]
        south_edge[1, level : level + 1, :] = v[top : top + 1]
        north_edge[level : level + 1, :] = t[bottom : bottom + 1]

    def by_lane(i):
        rows = jnp.concatenate([factor[i], factor[i]], axis=1)
        return jnp.broadcast_to(rows[None], (LEV, ROWS, LANES)).reshape(FLAT, LANES)

    row = lax.rem(lax.broadcasted_iota(jnp.int32, (FLAT, LANES), 0), ROWS)
    east_flux = u * (t + pltpu.roll(t, LANES - 1, 1)) * 0.5
    zonal_div = east_flux - pltpu.roll(east_flux, 1, 1)
    above = jnp.where(row == ROWS - 1, 0.0, pltpu.roll(t, FLAT - 1, 0))
    north_flux = v * by_lane(0) * (t + above) * 0.5
    south_flux = jnp.where(row == 0, 0.0, pltpu.roll(north_flux, 1, 0))
    change = -courant_number * (zonal_div + (north_flux - south_flux) / by_lane(2))
    change = jnp.where(lane < COLS, change, 0.0)
    increment[...] = change

    @pl.when(is_source)
    def _():
        last_wind = 0.5 * courant_number * u[:, COLS - 1 : COLS]
        marked = jnp.where(lane == COLS, t[:, 0:1], change)
        marked = jnp.where(lane == COLS + 1, last_wind, marked)
        marked = jnp.where(lane == COLS + 2, last_wind * t[:, COLS - 1 : COLS], marked)
        for level in range(LEV):
            by_row[:, level, :] = marked[level * ROWS : (level + 1) * ROWS, :]

    for load in loads[4:]:
        load.wait()
    lookup = routing_plan(target[...], cutoff[...], polar_rows[...], lon, lat)
    plan_made[...] = jnp.broadcast_to(lookup, plan_made.shape)
    plan_load = pltpu.make_async_copy(plan_made, plan, load_sem.at[11])
    plan_load.start()
    plan_load.wait()

    pl.semaphore_wait(
        barrier,
        PLACES
        - 1
        + jnp.where(is_relay, N_LON - 1, 2 * (z_above - z_below) + 1)

        + jnp.where(bridge, 1, 0)
        + jnp.where(is_relay, 1, 0)
        + jnp.where(jnp.logical_and(is_relay, lon == own_seam_lon), N_LON, 0),
    )

    @pl.when(has_north)
    def _():
        send(south_edge, south_in, edge_send.at[0], edge_recv.at[0], lon, lat + 1).start()

    @pl.when(has_south)
    def _():
        send(north_edge, north_in, edge_send.at[1], edge_recv.at[1], lon, lat - 1).start()

    def tell(to_lon, to_lat, sem):
        pl.semaphore_signal(
            sem, inc=1, device_id={"lon": to_lon, "lat": to_lat}, device_id_type=MESH
        )

    def tell_along(distance, sem):
        @pl.when(z >= distance)
        def _():
            tell(lon - 2 * distance, lat, sem)

        @pl.when(z + distance < N_LON // 2)
        def _():
            tell(lon + 2 * distance, lat, sem)

    def heard_along(distance, sem):
        pl.semaphore_wait(
            sem,
            jnp.where(z >= distance, 1, 0) + jnp.where(z + distance < N_LON // 2, 1, 0),
        )

    @pl.when(is_relay)
    def _():
        tell(lon, served, seam_ready)

    @pl.when(jnp.logical_not(is_relay))
    def _():
        tell_along(NEAR, line_sem.at[0])

    def edge_scale(face, row):
        scale = 0.5 * courant_number * factor[face, row : row + 1, :] / factor[2, row : row + 1, :]
        return jnp.concatenate([scale, scale], axis=1)

    def from_north():
        return -edge_scale(0, ROWS - 1) * south_edge[1] * north_in[...]

    def from_south():
        return edge_scale(1, 0) * south_in[1] * (south_in[0] + north_edge[...])

    def plain_rows():
        @pl.when(jnp.logical_and(any_south, jnp.logical_not(is_source)))
        def _():
            take(south_in, edge_recv.at[0])

        @pl.when(jnp.logical_and(any_north, jnp.logical_not(is_source)))
        def _():
            take(north_in, edge_recv.at[1])

        take(west_in, edge_recv.at[2])
        take(east_in, edge_recv.at[3])
        columns = jnp.concatenate(
            [east_in[...], west_in[...], jnp.zeros((112, LANES), jnp.float32)], axis=0
        ).T[:FLAT]
        tracer_east, tracer_west, wind_west = columns[:, 0:1], columns[:, 9:10], columns[:, 10:11]
        t, u = widened(tracer[...]), widened(zonal[...])
        lane = lax.broadcasted_iota(jnp.int32, (FLAT, LANES), 1)
        half_courant = 0.5 * courant_number
        change = increment[...]
        change = jnp.where(lane == COLS - 1, change - half_courant * (u * tracer_east), change)
        change = jnp.where(lane == 0, change + half_courant * (wind_west * (tracer_west + t)), change)
        next_out[...] = (t + change).reshape(LEV, ROWS, LANES)[:, :, :COLS]

        @pl.when(any_south)
        def _():
            next_out[:, 0, :] = next_out[:, 0, :] + from_south()[:, :COLS]

        @pl.when(any_north)
        def _():
            next_out[:, ROWS - 1, :] = next_out[:, ROWS - 1, :] + from_north()[:, :COLS]

    @pl.when(is_source)
    def _():
        @pl.when(has_south)
        def _():
            take(south_in, edge_recv.at[0])
            by_row[0] = by_row[0] + from_south()

        @pl.when(has_north)
        def _():
            take(north_in, edge_recv.at[1])
            by_row[ROWS - 1] = by_row[ROWS - 1] + from_north()

        @pl.when(low_seam)
        def _():
            seam_own[lon, 0] = by_row[ROWS - 1]
            seam_own[lon, 1] = south_edge[1]

        @pl.when(high_seam)
        def _():
            seam_own[lon, 0] = by_row[0]
            seam_own[lon, 1] = north_edge[...]

        def leave(k):
            to = lax.rem(place + 1 + k, PLACES)
            outbound[2 * to] = by_row[plan[2 * to, 0]]
            outbound[2 * to + 1] = by_row[plan[2 * to + 1, 0]]
            send(
                outbound.at[pl.ds(2 * to, 2)],
                column.at[source],
                out_send,
                out_recv.at[source],
                lon,
                lat_of(to, half),
            ).start()

        each(PLACES - 1, leave)
        column[source, 0] = by_row[plan[2 * place, 0]]
        column[source, 1] = by_row[plan[2 * place + 1, 0]]

    @pl.when(jnp.logical_not(is_relay))
    def _():
        heard_along(NEAR, line_sem.at[0])
        tell_along(2 * NEAR, line_sem.at[1])

    @pl.when(at_seam)
    def _():
        pl.semaphore_wait(seam_ready, 1)

    @pl.when(low_seam)
    def _():
        send(
            south_edge, seam_other.at[lon], seam_send.at[0], seam_recv.at[0], other_seam_lon, other_lat
        ).start()

    @pl.when(high_seam)
    def _():
        send(
            north_edge, seam_other.at[lon, 0], seam_send.at[0], seam_recv.at[0], other_seam_lon, other_lat
        ).start()

    @pl.when(jnp.logical_not(is_relay))
    def _():
        heard_along(2 * NEAR, line_sem.at[1])

    @pl.when(jnp.logical_and(at_seam, lon != own_seam_lon))
    def _():
        send(
            seam_own.at[lon],
            seam_own.at[lon],
            seam_send.at[1],
            seam_recv.at[1],
            own_seam_lon,
            lat,
        ).start()

    @pl.when(bridge)
    def _():
        tell(bridge_to, lat_of(place, 1 - half), bridge_sem)
        pl.semaphore_wait(bridge_sem, 1)
        each(N_LON - 1, lambda k: tell(lax.rem(lon + 1 + k, N_LON), lat, both_sem))

    @pl.when(jnp.logical_not(all_polar))
    def _():
        send(lon_edge, west_in, edge_send.at[2], edge_recv.at[2], east, lat).start()
        send(lon_edge, east_in, edge_send.at[3], edge_recv.at[3], west, lat).start()

    def to_worker(s, t_half):
        to = worker_lon(2 * s + t_half)

        @pl.when(to != lon)
        def _():
            send(
                column.at[s, t_half], gathered.at[lon], gather_send, gather_recv, to, lat
            ).start()

        @pl.when(to == lon)
        def _():
            gathered[lon] = column[s, t_half]

    def pass_on(s):
        @pl.when(jnp.logical_not(jnp.logical_and(is_source, source == s)))
        def _():
            take(column.at[s], out_recv.at[s])

        to_worker(s, 0)

        @pl.when(half == 0)
        def _():
            to_worker(s, 1)

    each(SOURCES, pass_on)

    @pl.when(half == 1)
    def _():
        each(SOURCES, lambda s: to_worker(s, 1))

    @pl.when(jnp.logical_or(is_worker, seam_worker))
    def _():
        fh[...], fl[...] = split_value(forward[...])
        ih[...], il[...] = split_value(inverse[...])
        wh[...], wl[...] = split_value(within[...])

    @pl.when(jnp.logical_not(bridge))
    def _():
        pl.semaphore_wait(both_sem, 1)

    @pl.when(far_north)
    def _():
        send(south_edge, far_in, edge_send.at[0], far_recv, lon, opposite).start()

    @pl.when(far_south)
    def _():
        send(north_edge, far_in.at[0], edge_send.at[1], far_recv, lon, opposite).start()

    @pl.when(seam_worker)
    def _():
        take(seam_own.at[pl.ds(0, N_LON - 1)], seam_recv.at[1])

        @pl.when(low_seam)
        def _():
            take(seam_other.at[pl.ds(0, N_LON // 2)], seam_recv.at[0])
            scale = -0.5 * courant_number * factor[0, ROWS - 1 :, :] / factor[2, ROWS - 1 :, :]
            scale = jnp.concatenate([scale, scale], axis=1)[None]
            gathered[...] = seam_own[:, 0] + scale * seam_own[:, 1] * seam_other[:, 0]

        @pl.when(high_seam)
        def _():
            take(seam_other, seam_recv.at[0])
            scale = 0.5 * courant_number * factor[1, :1, :] / factor[2, :1, :]
            scale = jnp.concatenate([scale, scale], axis=1)[None]
            gathered[...] = seam_own[:, 0] + scale * seam_other[:, 1] * (
                seam_other[:, 0] + seam_own[:, 1]
            )

    @pl.when(is_worker)
    def _():
        take(gathered.at[pl.ds(0, N_LON - 1)], gather_recv)

    @pl.when(jnp.logical_or(is_worker, seam_worker))
    def _():
        cos_mid = jnp.concatenate([tw[0]] * (LEV // 2), axis=0)
        sin_mid = jnp.concatenate([tw[1]] * (LEV // 2), axis=0)
        tables = (fh[...], fl[...], ih[...], il[...], wh[...], wl[...], cos_mid, sin_mid)
        values = with_edge_terms(gathered[...].reshape(N_LON * LEV, LANES))
        smoothed[...] = band_filter(values, plan[64, 0], tables).reshape(N_LON, LEV, LANES)

    @pl.when(is_worker)
    def _():
        def to_slot(to):
            send(
                smoothed.at[to],
                slot_in.at[half * SOURCES + work_source],
                cross_send,
                cross_recv,
                to,
                opposite,
            ).start()

        def to_line(to):
            @pl.when(to != lon)
            def _():
                send(
                    smoothed.at[to],
                    returned.at[work_source, work_half],
                    back_send,
                    back_recv.at[work_source],
                    to,
                    lat,
                ).start()

        @pl.when(jnp.logical_and(across, half == 1))
        def _():
            each(N_LON, to_slot)

        each(N_LON, to_line)

        @pl.when(jnp.logical_and(across, half == 0))
        def _():
            each(N_LON, lambda k: to_slot(alternate(lon, k)))

        returned[work_source, work_half] = smoothed[lon]

    @pl.when(seam_worker)
    def _():
        def to_seam(to, to_lat, sem):
            send(
                smoothed.at[to], seam_result.at[seam_side], sem, seam_back_recv, to, to_lat
            ).start()

        def to_own_line(to):
            @pl.when(to != lon)
            def _():
                to_seam(to, lat, seam_back_send.at[1])

        @pl.when(half == 0)
        def _():
            each(N_LON, to_own_line)

        def from_ends(k):
            step = lax.div(k, 2)
            return jnp.where(lax.rem(k, 2) == 0, step, N_LON - 1 - step)

        each(N_LON, lambda k: to_seam(from_ends(k), other_lat, seam_back_send.at[0]))

        @pl.when(half == 1)
        def _():
            each(N_LON, to_own_line)

        seam_result[seam_side] = smoothed[lon]

    @pl.when(hands_north)
    def _():
        take(far_in, far_recv)
        send(far_in, south_in, far_send, edge_recv.at[0], lon, opposite + 1).start()

    @pl.when(hands_south)
    def _():
        take(far_in.at[0], far_recv)
        send(far_in.at[0], north_in, far_send, edge_recv.at[1], lon, opposite - 1).start()

    @pl.when(jnp.logical_and(is_source, jnp.logical_not(all_polar)))
    def _():
        plain_rows()

    from_far = jnp.logical_or(far_north, far_south)

    @pl.when(jnp.logical_not(jnp.logical_or(is_source, from_far)))
    def _():
        plain_rows()

    seam_pair = jnp.where(lat < NLAT // ROWS // 2, 0, 1)
    seam_slots = [slot_in.at[pl.ds(2 * SOURCES + 2 * pair, 2)] for pair in range(2)]

    @pl.when(at_seam)
    def _():
        @pl.when(seam_worker)
        def _():
            take(seam_result.at[0], seam_back_recv)

        @pl.when(jnp.logical_not(seam_worker))
        def _():
            take(seam_result, seam_back_recv)

        own_slots = slot_in.at[pl.ds(2 * SOURCES + 2 * seam_pair, 2)]

        def spread(k):
            to = lat_of(lax.rem(place + 1 + k, PLACES), half)
            send(seam_result, own_slots, seam_out_send, seam_out_recv.at[seam_pair], lon, to).start()

        each(PLACES - 1, spread)
        slot_in[2 * SOURCES + 2 * seam_pair] = seam_result[0]
        slot_in[2 * SOURCES + 2 * seam_pair + 1] = seam_result[1]
        homeward[2 * PLACES] = seam_result[seam_side]

    def go_home(s):
        own = jnp.logical_and(is_worker, work_source == s)

        @pl.when(own)
        def _():
            take(returned.at[s, 0], back_recv.at[s])

        @pl.when(jnp.logical_not(own))
        def _():
            take(returned.at[s], back_recv.at[s])

        stays = jnp.logical_and(is_source, source == s)

        @pl.when(stays)
        def _():
            homeward[2 * place] = returned[s, 0]
            homeward[2 * place + 1] = returned[s, 1]

        @pl.when(jnp.logical_not(stays))
        def _():
            send(
                returned.at[s],
                homeward.at[pl.ds(2 * place, 2)],
                home_send,
                home_recv,
                lon,
                lat_of(source_place(s, half), half),
            ).start()

        slot_in[half * SOURCES + s] = returned[s, half]

    each(SOURCES, go_home)

    @pl.when(from_far)
    def _():
        plain_rows()

    take(slot_in.at[pl.ds(0, SOURCES)], cross_recv)
    for pair in range(2):

        @pl.when(jnp.logical_not(jnp.logical_and(at_seam, seam_pair == pair)))
        def _(pair=pair):
            take(seam_slots[pair], seam_out_recv.at[pair])

    for slot in range(SLOTS):
        slots_out[slot] = slot_in[plan[56 + slot, 0]][:, :COLS]

    @pl.when(is_source)
    def _():
        take(homeward.at[pl.ds(0, 2 * PLACES - 2)], home_recv)
        for j in range(ROWS):
            lat_row = lat * ROWS + j
            polar = jnp.logical_or(lat_row < NH, lat_row >= NLAT - NH)
            filtered = homeward[plan[32 + j, 0]][:, :COLS]
            next_out[:, j, :] = jnp.where(polar, tracer[:, j, :] + filtered, next_out[:, j, :])

    @pl.when(hands_north)
    def _():
        sent(far_in, far_send)

    @pl.when(hands_south)
    def _():
        sent(far_in.at[0], far_send)

    @pl.when(any_north)
    def _():
        sent(south_edge, edge_send.at[0])

    @pl.when(any_south)
    def _():
        sent(north_edge, edge_send.at[1])

    @pl.when(jnp.logical_not(all_polar))
    def _():
        sent(lon_edge, edge_send.at[2])
        sent(lon_edge, edge_send.at[3])

    @pl.when(low_seam)
    def _():
        sent(south_edge, seam_send.at[0])

    @pl.when(high_seam)
    def _():
        sent(north_edge, seam_send.at[0])

    @pl.when(at_seam)
    def _():
        sent(homeward.at[pl.ds(0, 2 * PLACES - 2)], seam_out_send)

        @pl.when(jnp.logical_not(seam_worker))
        def _():
            sent(seam_own.at[lon], seam_send.at[1])

        @pl.when(seam_worker)
        def _():
            sent(smoothed, seam_back_send.at[0])
            sent(smoothed.at[pl.ds(0, N_LON - 1)], seam_back_send.at[1])

    @pl.when(is_source)
    def _():
        sent(outbound.at[pl.ds(0, 2 * PLACES - 2)], out_send)
        sent(homeward.at[pl.ds(0, 2 * SOURCES - 2)], home_send)

    @pl.when(jnp.logical_not(is_source))
    def _():
        sent(homeward.at[pl.ds(0, 2 * SOURCES)], home_send)

    @pl.when(is_worker)
    def _():
        sent(smoothed.at[pl.ds(0, 2 * SOURCES - 1)], gather_send)
        sent(smoothed.at[pl.ds(0, N_LON - 1)], back_send)

    @pl.when(jnp.logical_not(is_worker))
    def _():
        sent(smoothed.at[pl.ds(0, 2 * SOURCES)], gather_send)

    @pl.when(across)
    def _():
        sent(smoothed, cross_send)


def shards(tracer, zonal_wind, meridional_wind, polar_target, cutoff_wave):
    tables = [jnp.asarray(table) for table in filter_tables()]
    factors = jnp.asarray(row_factors())
    f32, bf16 = jnp.float32, jnp.bfloat16
    block = (LEV, ROWS, COLS)
    anywhere, in_vmem = pl.BlockSpec(memory_space=pltpu.HBM), pl.BlockSpec(memory_space=pltpu.VMEM)
    dma = pltpu.SemaphoreType.DMA
    square, wide = (LEV * N_LON, LEV * N_LON), (LANES, 2 * LANES)
    message = (LEV, LANES)
    in_hbm = [
        pltpu.with_memory_space_constraint(a, pltpu.HBM)
        for a in (
            polar_target.reshape(2, NPOLAR // 2),
            cutoff_wave.reshape(2, NPOLAR // 2),
            jnp.asarray(polar_row_table()),
            tracer,
            zonal_wind,
            meridional_wind,
            factors,
            *tables,
        )
    ]
    return pl.pallas_call(
        substep_kernel,
        out_shape=(
            jax.ShapeDtypeStruct(block, f32),
            jax.ShapeDtypeStruct((SLOTS, LEV, COLS), f32),
        ),
        in_specs=[anywhere] * 11,
        out_specs=(in_vmem, in_vmem),
        scratch_shapes=[
            pltpu.VMEM((2, NPOLAR // 2), jnp.int32),
            pltpu.VMEM((2, NPOLAR // 2), jnp.int32),
            pltpu.VMEM((8, NPOLAR), jnp.int32),
            pltpu.VMEM((ENTRIES, 128), jnp.int32),
            pltpu.SMEM((ENTRIES, 128), jnp.int32),
            pltpu.VMEM(block, f32),
            pltpu.VMEM(block, f32),
            pltpu.VMEM(block, f32),
            pltpu.VMEM((3, ROWS, 128), f32),
            pltpu.VMEM(square, f32),
            pltpu.VMEM(square, f32),
            pltpu.VMEM(wide, f32),
            pltpu.VMEM(square, bf16),
            pltpu.VMEM(square, bf16),
            pltpu.VMEM(square, bf16),
            pltpu.VMEM(square, bf16),
            pltpu.VMEM(wide, bf16),
            pltpu.VMEM(wide, bf16),
            pltpu.VMEM((2, N_LON, LANES), f32),
            pltpu.VMEM(message, f32),
            pltpu.VMEM(message, f32),
            pltpu.VMEM(message, f32),
            pltpu.VMEM((2, *message), f32),
            pltpu.VMEM(message, f32),
            pltpu.VMEM((2, *message), f32),
            pltpu.VMEM(message, f32),
            pltpu.VMEM((FLAT, LANES), f32),
            pltpu.VMEM((ROWS, *message), f32),
            pltpu.VMEM((2 * PLACES, *message), f32),
            pltpu.VMEM((SOURCES, 2, *message), f32),
            pltpu.VMEM((N_LON, *message), f32),
            pltpu.VMEM((N_LON, *message), f32),
            pltpu.VMEM((SOURCES, 2, *message), f32),
            pltpu.VMEM((2 * SOURCES + 4, *message), f32),
            pltpu.VMEM((2 * PLACES + 1, *message), f32),
            pltpu.VMEM((N_LON, 2, *message), f32),
            pltpu.VMEM((N_LON, 2, *message), f32),
            pltpu.VMEM((2, *message), f32),
            pltpu.VMEM((2, *message), f32),
            dma((12,)),
            dma((4,)),
            dma((4,)),
            dma,
            dma((SOURCES,)),
            dma,
            dma,
            dma,
            dma((SOURCES,)),
            dma,
            dma,
            dma,
            dma,
            dma((2,)),
            dma((2,)),
            dma((2,)),
            dma,
            dma,
            dma((2,)),
            pltpu.SemaphoreType.REGULAR((2,)),
            pltpu.SemaphoreType.REGULAR,
            pltpu.SemaphoreType.REGULAR,
            pltpu.SemaphoreType.REGULAR,
            dma,
            dma,
        ],
        compiler_params=pltpu.CompilerParams(
            collective_id=0, has_side_effects=True, vmem_limit_bytes=32 * 2**20
        ),
        name="substep",
    )(*in_hbm)


def solution(mesh):
    placed = (P(None, "lat", "lon"), P(None, "lat", "lon"), P(None, "lat", "lon"), P(), P())
    return jax.shard_map(
        shards,
        mesh=mesh,
        in_specs=placed,
        out_specs=(P(None, "lat", "lon"), P("lat", None, "lon")),
        check_vma=False,
    )
```

```python
import math

import jax
import jax.numpy as jnp
import numpy as np
from jax import lax
from jax.experimental import pallas as pl
from jax.experimental.pallas import tpu as pltpu
from jax.sharding import PartitionSpec as P

courant_number = 0.4
LEV, NLAT, NLON = 8, 768, 7200
NH, NPOLAR, SLOTS = 128, 256, 8
N_LAT, N_LON = 32, 32
ROWS, COLS, LANES = NLAT // N_LAT, NLON // N_LON, 256
FLAT = LEV * ROWS
SOURCES, PLACES = 6, 16
SEAM_LOW = (3, 27)
SEAM_LON = 15
SEAM_LINES = (3, 4, 27, 28)
RELAYS = (10, 7, 24, 21)
ENTRIES = 72
NEAR = 4
MESH = pl.DeviceIdType.MESH


def half_of(lat):
    return lax.rem(lax.div(lat, 4), 2)


def place_of(lat):
    return lax.div(lat, 8) * 4 + lax.rem(lat, 4)


def lat_of(place, half):
    return lax.div(place, 4) * 8 + half * 4 + lax.rem(place, 4)


def source_place(source, half):
    return jnp.where(source < 4 - 2 * half, source, source + 10)


def worker_lon(worker):
    return 2 * worker + jnp.where(worker < SOURCES, 2, 4)


def worker_at(lon):
    chip = lax.div(lon, 2)
    worker = jnp.where(chip < SEAM_LON // 2, chip - 1, chip - 2)
    found = jnp.logical_and(worker >= 0, worker < 2 * SOURCES)
    found = jnp.logical_and(found, chip != SEAM_LON // 2)
    return worker, jnp.logical_and(found, lax.rem(lon, 2) == 0)


def alternate(lon, k):
    step = lax.div(k + 1, 2)
    return lax.rem(lon + N_LON + jnp.where(lax.rem(k, 2) == 1, step, -step), N_LON)


def filter_tables():
    angle = np.arange(N_LON)[:, None] * np.arange(N_LON)[None, :] % N_LON * (2 * np.pi / N_LON)
    across = np.zeros((2, LEV // 2, N_LON, N_LON, LEV))
    for pair in range(LEV // 2):
        across[0, pair, :, :, 2 * pair] = np.cos(angle)
        across[0, pair, :, :, 2 * pair + 1] = np.sin(angle)
        across[1, pair, :, :, 2 * pair] = -np.sin(angle)
        across[1, pair, :, :, 2 * pair + 1] = np.cos(angle)
    across = across.reshape(LEV * N_LON, LEV * N_LON)
    middle = np.arange(N_LON)[:, None] * np.arange(COLS)[None, :] * (2 * np.pi / NLON)
    twiddle = np.zeros((2, N_LON, LANES), np.float32)
    twiddle[0, :, :COLS] = np.cos(middle)
    twiddle[1, :, :COLS] = np.sin(middle)
    inner = np.arange(COLS)[:, None] * np.arange(COLS)[None, :] % COLS * (2 * np.pi / COLS)
    within = np.zeros((LANES, 2 * LANES))
    within[:COLS, :COLS] = np.cos(inner)
    within[:COLS, LANES : LANES + COLS] = np.sin(inner)
    return [a.astype(np.float32) for a in (across, across.T, within, twiddle)]


def row_factors():
    row = np.arange(NLAT, dtype=np.float32)
    step = np.float32(math.pi / NLAT)
    face = np.sin(((row + np.float32(1.0)) * step).astype(np.float64)).astype(np.float32)
    face[-1] = 0.0
    centre = np.sin(((row + np.float32(0.5)) * step).astype(np.float64)).astype(np.float32)
    below = np.concatenate([np.zeros(1, np.float32), face[:-1]])
    table = np.stack([face, below, centre]).reshape(3, N_LAT, ROWS).transpose(1, 0, 2)
    return np.ascontiguousarray(np.broadcast_to(table[..., None], (N_LAT, 3, ROWS, 128)))


def polar_row_table():
    index = np.arange(NPOLAR)
    glob = np.where(index < NH, index, index + NLAT - NPOLAR)
    home, own_row = glob // ROWS, glob % ROWS
    home_half, home_place = (home // 4) % 2, home // 8 * 4 + home % 4
    home_source = home_half * SOURCES + np.where(
        home_place < 4 - 2 * home_half, home_place, home_place - 10
    )
    seam = np.zeros(NPOLAR, np.int32)
    for pair, low in enumerate(SEAM_LOW):
        for side in range(2):
            row = (home == low + side) & (own_row == (0 if side else ROWS - 1))
            home_source = np.where(row, 2 * SOURCES + 2 * pair + side, home_source)
            seam[row] = 1
    return np.stack([home, own_row, home_source, seam] * 2).astype(np.int32)


def routing_plan(target, cutoff, rows, lon, lat):
    half, place = half_of(lat), place_of(lat)
    home, own_row, home_source, seam = (rows[i : i + 1] for i in range(4))
    target = jnp.concatenate([target[0:1], target[1:2]], axis=1)
    cutoff = jnp.concatenate([cutoff[0:1], cutoff[1:2]], axis=1)
    target_lat = target >> 3
    target_code = ((target_lat >> 3) * 4 + (target_lat & 3)) * 2 + ((target_lat >> 2) & 1)
    worker, is_worker = worker_at(lon)
    worker_home = jnp.where(is_worker, lat_of(source_place(lax.div(worker, 2), half), half), lat)
    worker_target = jnp.where(is_worker, place * 2 + lax.rem(worker, 2), -1)
    entry = lax.broadcasted_iota(jnp.int32, (ENTRIES, NPOLAR), 0)
    none = jnp.zeros((ENTRIES, NPOLAR), jnp.int32)
    row_target = jnp.where(seam == 1, 2 * PLACES, target_code)
    filtered_code = jnp.where(is_worker, target_code, jnp.where(seam == 1, -1, 0))
    mine = home == lat
    filtered_here = jnp.where((home == worker_home) & (filtered_code == worker_target), cutoff, 0)
    leaving = jnp.where(mine & (target_code == entry), own_row, none)
    landing = jnp.where(mine & (own_row == entry - 32), row_target, none)
    slot = jnp.where(target == lat * SLOTS + entry - 56, home_source, none)
    value = jnp.where(entry < 32, leaving, jnp.where(entry < 56, landing, slot))
    value = jnp.where(entry < 64, value, jnp.where(entry == 64, filtered_here, none))
    return jnp.sum(value, axis=1, keepdims=True)


def is_any(value, choices):
    found = value == choices[0]
    for choice in choices[1:]:
        found = jnp.logical_or(found, value == choice)
    return found


def chosen(value, choices, results):
    found = results[-1]
    for choice, result in zip(choices[:-1], results[:-1]):
        found = jnp.where(value == choice, result, found)
    return found


def split_value(value):
    high = value.astype(jnp.bfloat16)
    low = (value - high.astype(jnp.float32)).astype(jnp.bfloat16)
    return high, low


def mxu(left_side, right_side):
    return jnp.dot(left_side, right_side, preferred_element_type=jnp.float32)


def dot_left(table_high, table_low, value):
    high, low = split_value(value)
    return mxu(table_high, high) + (mxu(table_high, low) + mxu(table_low, high))


def dot_right(value, table_high, table_low):
    high, low = split_value(value)
    return mxu(high, table_high) + (mxu(low, table_high) + mxu(high, table_low))


def band_filter(values, cut, tables):
    fwd_high, fwd_low, inv_high, inv_low, in_high, in_low, cos_mid, sin_mid = tables
    part = N_LON * LEV // 2
    spread = dot_left(fwd_high, fwd_low, values)
    real, imag = spread[:part], spread[part:]
    turned = jnp.concatenate(
        [real * cos_mid + imag * sin_mid, imag * cos_mid - real * sin_mid], axis=0
    )
    parts = dot_right(turned, in_high, in_low)
    real = parts[:part, :LANES] + parts[part:, LANES:]
    imag = parts[part:, :LANES] - parts[:part, LANES:]
    shape = (N_LON, LANES)
    wave = lax.broadcasted_iota(jnp.int32, shape, 0) + N_LON * lax.broadcasted_iota(
        jnp.int32, shape, 1
    )
    scale = jnp.where(jnp.minimum(wave, NLON - wave) <= cut, 1.0 / NLON, 0.0)
    scale = jnp.concatenate([scale] * (LEV // 2), axis=0)
    parts = dot_right(jnp.concatenate([real * scale, imag * scale], axis=0), in_high, in_low)
    real = parts[:part, :LANES] - parts[part:, LANES:]
    imag = parts[part:, :LANES] + parts[:part, LANES:]
    turned = jnp.concatenate(
        [real * cos_mid - imag * sin_mid, imag * cos_mid + real * sin_mid], axis=0
    )
    return dot_left(inv_high, inv_low, turned)


def with_edge_terms(values):
    low, high = values[:, :128], values[:, 128:]
    lane = lax.broadcasted_iota(jnp.int32, low.shape, 1)
    last = COLS - 1 - 128
    count = values.shape[0]
    next_first = pltpu.roll(pltpu.roll(high, 1, 1), count - LEV, 0)
    product = high * next_first
    flux = pltpu.roll(pltpu.roll(high, 127, 1) + product, 128 - (last + 2), 1)
    low = jnp.where(lane == 0, low + pltpu.roll(flux, LEV, 0), low)
    high = jnp.where(lane == last, high - pltpu.roll(product, 126, 1), high)
    return jnp.concatenate([low, jnp.where(lane <= last, high, 0.0)], axis=1)


def each(count, step):
    lax.fori_loop(0, count, lambda k, carry: (step(k), carry)[1], 0)


def widened(block):
    pad = jnp.zeros((LEV, ROWS, LANES - COLS), jnp.float32)
    return jnp.concatenate([block, pad], axis=2).reshape(FLAT, LANES)


def substep_kernel(
    target_hbm,
    cutoff_hbm,
    polar_hbm,
    tracer_hbm,
    zonal_hbm,
    merid_hbm,
    factor_hbm,
    forward_hbm,
    inverse_hbm,
    within_hbm,
    tw_hbm,
    next_out,
    slots_out,
    target,
    cutoff,
    polar_rows,
    plan_made,
    plan,
    tracer,
    zonal,
    merid,
    factor,
    forward,
    inverse,
    within,
    fh,
    fl,
    ih,
    il,
    wh,
    wl,
    tw,
    lon_edge,
    east_in,
    west_in,
    south_edge,
    north_edge,
    south_in,
    north_in,
    increment,
    by_row,
    outbound,
    column,
    gathered,
    smoothed,
    returned,
    slot_in,
    homeward,
    seam_own,
    seam_other,
    seam_result,
    far_in,
    load_sem,
    edge_send,
    edge_recv,
    out_send,
    out_recv,
    gather_send,
    gather_recv,
    back_send,
    back_recv,
    cross_send,
    cross_recv,
    home_send,
    home_recv,
    seam_send,
    seam_recv,
    seam_back_send,
    seam_back_recv,
    seam_out_send,
    seam_out_recv,
    line_sem,
    bridge_sem,
    both_sem,
    seam_ready,
    far_send,
    far_recv,
):
    lon, lat = lax.axis_index("lon"), lax.axis_index("lat")
    half, place = half_of(lat), place_of(lat)
    first_places = 4 - 2 * half
    is_source = jnp.logical_or(place < first_places, place >= first_places + 10)
    source = jnp.where(place < first_places, place, place - 10)
    worker, is_worker = worker_at(lon)
    work_source, work_half = lax.div(worker, 2), lax.rem(worker, 2)
    across = jnp.logical_and(is_worker, work_half != half)
    east, west = lax.rem(lon + 1, N_LON), lax.rem(lon + N_LON - 1, N_LON)
    low_seam = is_any(lat, SEAM_LOW)
    high_seam = is_any(lat, [low + 1 for low in SEAM_LOW])
    at_seam = jnp.logical_or(low_seam, high_seam)
    seam_side = jnp.where(high_seam, 1, 0)
    other_lat = jnp.where(high_seam, lat - 1, lat + 1)
    seam_worker = jnp.logical_and(at_seam, lon == SEAM_LON)
    has_north, has_south = lax.rem(lat, 4) != 3, lax.rem(lat, 4) != 0
    far_north = jnp.logical_not(jnp.logical_or(has_north, jnp.logical_or(low_seam, lat == N_LAT - 1)))
    far_south = jnp.logical_not(jnp.logical_or(has_south, jnp.logical_or(high_seam, lat == 0)))
    any_north, any_south = jnp.logical_or(has_north, far_north), jnp.logical_or(has_south, far_south)
    is_relay = is_any(lat, RELAYS)
    served = chosen(lat, RELAYS, SEAM_LINES)
    far_relay = chosen(other_lat, SEAM_LINES, RELAYS)
    z = lax.div(lon, 2)
    opposite = lat_of(place, 1 - half)
    hands_north = jnp.logical_and(
        lax.rem(lat, 4) == 3, jnp.logical_not(is_any(opposite, (*SEAM_LOW, N_LAT - 1)))
    )
    hands_south = jnp.logical_and(
        lax.rem(lat, 4) == 0, jnp.logical_not(is_any(opposite, (0, *[low + 1 for low in SEAM_LOW])))
    )
    z_below, z_above = lax.max(z - NEAR, 0), lax.min(z + NEAR, N_LON // 2 - 1)
    bridge = lon == jnp.where(half == 0, N_LON - 2, 0)
    bridge_to = jnp.where(half == 0, 0, N_LON - 2)
    all_polar = jnp.logical_or(lat * ROWS + ROWS <= NH, lat * ROWS >= NLAT - NH)

    loads = [
        pltpu.make_async_copy(a, b, load_sem.at[i])
        for i, (a, b) in enumerate(
            [
                (tracer_hbm, tracer),
                (zonal_hbm, zonal),
                (merid_hbm, merid),
                (factor_hbm.at[lat], factor),
                (forward_hbm, forward),
                (inverse_hbm, inverse),
                (within_hbm, within),
                (tw_hbm, tw),
                (target_hbm, target),
                (cutoff_hbm, cutoff),
                (polar_hbm, polar_rows),
            ]
        )
    ]
    for load in loads:
        load.start()

    barrier = pltpu.get_barrier_semaphore()

    def greet(to_lon, to_lat):
        pl.semaphore_signal(
            barrier, inc=1, device_id={"lon": to_lon, "lat": to_lat}, device_id_type=MESH
        )

    each(PLACES - 1, lambda k: greet(lon, lat_of(lax.rem(place + 1 + k, PLACES), half)))

    @pl.when(is_relay)
    def _():
        each(N_LON - 1, lambda k: greet(lax.rem(lon + 1 + k, N_LON), lat))

    @pl.when(jnp.logical_not(is_relay))
    def _():
        def greet_near(k):
            @pl.when(z_below * 2 + k != lon)
            def _():
                greet(z_below * 2 + k, lat)

        each(2 * (z_above - z_below + 1), greet_near)

    @pl.when(bridge)
    def _():
        greet(bridge_to, lat_of(place, 1 - half))

    @pl.when(at_seam)
    def _():
        greet(SEAM_LON, far_relay)

        @pl.when(seam_worker)
        def _():
            each(N_LON, lambda k: greet(lax.rem(lon + k, N_LON), far_relay))

    def send(what, where, send_sem, recv_sem, to_lon, to_lat):
        return pltpu.make_async_remote_copy(
            src_ref=what,
            dst_ref=where,
            send_sem=send_sem,
            recv_sem=recv_sem,
            device_id={"lon": to_lon, "lat": to_lat},
            device_id_type=MESH,
        )

    def take(where, recv_sem):
        send(where, where, recv_sem, recv_sem, lon, lat).wait_recv()

    def sent(what, send_sem):
        send(what, what, send_sem, send_sem, lon, lat).wait_send()

    for load in loads[:4]:
        load.wait()
    t = widened(tracer[...])
    u = widened(zonal[...])
    v = widened(merid[...])
    lane = lax.broadcasted_iota(jnp.int32, (FLAT, LANES), 1)
    narrow = lane[:, :128]
    last = COLS - 1 - 128
    edge = jnp.where(
        narrow == 0,
        t[:, :128],
        jnp.where(
            narrow == 1,
            pltpu.roll(t[:, 128:], 128 + 1 - last, 1),
            pltpu.roll(u[:, 128:], 128 + 2 - last, 1),
        ),
    )
    edge = jnp.concatenate([edge, jnp.zeros((LANES - FLAT, 128), jnp.float32)], axis=0)
    lon_edge[...] = edge.T[:8]
    for level in range(LEV):
        top, bottom = level * ROWS + ROWS - 1, level * ROWS
        south_edge[0, level : level + 1, :] = t[top : top + 1]
        south_edge[1, level : level + 1, :] = v[top : top + 1]
        north_edge[level : level + 1, :] = t[bottom : bottom + 1]

    def by_lane(i):
        rows = jnp.concatenate([factor[i], factor[i]], axis=1)
        return jnp.broadcast_to(rows[None], (LEV, ROWS, LANES)).reshape(FLAT, LANES)

    row = lax.rem(lax.broadcasted_iota(jnp.int32, (FLAT, LANES), 0), ROWS)
    east_flux = u * (t + pltpu.roll(t, LANES - 1, 1)) * 0.5
    zonal_div = east_flux - pltpu.roll(east_flux, 1, 1)
    above = jnp.where(row == ROWS - 1, 0.0, pltpu.roll(t, FLAT - 1, 0))
    north_flux = v * by_lane(0) * (t + above) * 0.5
    south_flux = jnp.where(row == 0, 0.0, pltpu.roll(north_flux, 1, 0))
    change = -courant_number * (zonal_div + (north_flux - south_flux) / by_lane(2))
    change = jnp.where(lane < COLS, change, 0.0)
    increment[...] = change

    @pl.when(is_source)
    def _():
        last_wind = 0.5 * courant_number * u[:, COLS - 1 : COLS]
        marked = jnp.where(lane == COLS, t[:, 0:1], change)
        marked = jnp.where(lane == COLS + 1, last_wind, marked)
        marked = jnp.where(lane == COLS + 2, last_wind * t[:, COLS - 1 : COLS], marked)
        for level in range(LEV):
            by_row[:, level, :] = marked[level * ROWS : (level + 1) * ROWS, :]

    for load in loads[4:]:
        load.wait()
    lookup = routing_plan(target[...], cutoff[...], polar_rows[...], lon, lat)
    plan_made[...] = jnp.broadcast_to(lookup, plan_made.shape)
    plan_load = pltpu.make_async_copy(plan_made, plan, load_sem.at[11])
    plan_load.start()
    plan_load.wait()

    pl.semaphore_wait(
        barrier,
        PLACES
        - 1
        + jnp.where(is_relay, N_LON - 1, 2 * (z_above - z_below) + 1)

        + jnp.where(bridge, 1, 0)
        + jnp.where(is_relay, 1, 0)
        + jnp.where(jnp.logical_and(is_relay, lon == SEAM_LON), N_LON, 0),
    )

    @pl.when(has_north)
    def _():
        send(south_edge, south_in, edge_send.at[0], edge_recv.at[0], lon, lat + 1).start()

    @pl.when(has_south)
    def _():
        send(north_edge, north_in, edge_send.at[1], edge_recv.at[1], lon, lat - 1).start()

    def tell(to_lon, to_lat, sem):
        pl.semaphore_signal(
            sem, inc=1, device_id={"lon": to_lon, "lat": to_lat}, device_id_type=MESH
        )

    def tell_along(distance, sem):
        @pl.when(z >= distance)
        def _():
            tell(lon - 2 * distance, lat, sem)

        @pl.when(z + distance < N_LON // 2)
        def _():
            tell(lon + 2 * distance, lat, sem)

    def heard_along(distance, sem):
        pl.semaphore_wait(
            sem,
            jnp.where(z >= distance, 1, 0) + jnp.where(z + distance < N_LON // 2, 1, 0),
        )

    @pl.when(is_relay)
    def _():
        tell(lon, served, seam_ready)

    @pl.when(jnp.logical_not(is_relay))
    def _():
        tell_along(NEAR, line_sem.at[0])

    def edge_scale(face, row):
        scale = 0.5 * courant_number * factor[face, row : row + 1, :] / factor[2, row : row + 1, :]
        return jnp.concatenate([scale, scale], axis=1)

    def from_north():
        return -edge_scale(0, ROWS - 1) * south_edge[1] * north_in[...]

    def from_south():
        return edge_scale(1, 0) * south_in[1] * (south_in[0] + north_edge[...])

    def plain_rows():
        @pl.when(jnp.logical_and(any_south, jnp.logical_not(is_source)))
        def _():
            take(south_in, edge_recv.at[0])

        @pl.when(jnp.logical_and(any_north, jnp.logical_not(is_source)))
        def _():
            take(north_in, edge_recv.at[1])

        take(west_in, edge_recv.at[2])
        take(east_in, edge_recv.at[3])
        columns = jnp.concatenate(
            [east_in[...], west_in[...], jnp.zeros((112, LANES), jnp.float32)], axis=0
        ).T[:FLAT]
        tracer_east, tracer_west, wind_west = columns[:, 0:1], columns[:, 9:10], columns[:, 10:11]
        t, u = widened(tracer[...]), widened(zonal[...])
        lane = lax.broadcasted_iota(jnp.int32, (FLAT, LANES), 1)
        half_courant = 0.5 * courant_number
        change = increment[...]
        change = jnp.where(lane == COLS - 1, change - half_courant * (u * tracer_east), change)
        change = jnp.where(lane == 0, change + half_courant * (wind_west * (tracer_west + t)), change)
        next_out[...] = (t + change).reshape(LEV, ROWS, LANES)[:, :, :COLS]

        @pl.when(any_south)
        def _():
            next_out[:, 0, :] = next_out[:, 0, :] + from_south()[:, :COLS]

        @pl.when(any_north)
        def _():
            next_out[:, ROWS - 1, :] = next_out[:, ROWS - 1, :] + from_north()[:, :COLS]

    @pl.when(is_source)
    def _():
        @pl.when(has_south)
        def _():
            take(south_in, edge_recv.at[0])
            by_row[0] = by_row[0] + from_south()

        @pl.when(has_north)
        def _():
            take(north_in, edge_recv.at[1])
            by_row[ROWS - 1] = by_row[ROWS - 1] + from_north()

        @pl.when(low_seam)
        def _():
            seam_own[lon, 0] = by_row[ROWS - 1]
            seam_own[lon, 1] = south_edge[1]

        @pl.when(high_seam)
        def _():
            seam_own[lon, 0] = by_row[0]
            seam_own[lon, 1] = north_edge[...]

        def leave(k):
            to = lax.rem(place + 1 + k, PLACES)
            outbound[2 * to] = by_row[plan[2 * to, 0]]
            outbound[2 * to + 1] = by_row[plan[2 * to + 1, 0]]
            send(
                outbound.at[pl.ds(2 * to, 2)],
                column.at[source],
                out_send,
                out_recv.at[source],
                lon,
                lat_of(to, half),
            ).start()

        each(PLACES - 1, leave)
        column[source, 0] = by_row[plan[2 * place, 0]]
        column[source, 1] = by_row[plan[2 * place + 1, 0]]

    @pl.when(jnp.logical_not(is_relay))
    def _():
        heard_along(NEAR, line_sem.at[0])
        tell_along(2 * NEAR, line_sem.at[1])

    @pl.when(at_seam)
    def _():
        pl.semaphore_wait(seam_ready, 1)

    @pl.when(low_seam)
    def _():
        send(
            south_edge, seam_other.at[lon], seam_send.at[0], seam_recv.at[0], SEAM_LON, other_lat
        ).start()

    @pl.when(high_seam)
    def _():
        send(
            north_edge, seam_other.at[lon, 0], seam_send.at[0], seam_recv.at[0], SEAM_LON, other_lat
        ).start()

    @pl.when(jnp.logical_not(is_relay))
    def _():
        heard_along(2 * NEAR, line_sem.at[1])

    @pl.when(jnp.logical_and(at_seam, lon != SEAM_LON))
    def _():
        send(
            seam_own.at[lon],
            seam_own.at[lon],
            seam_send.at[1],
            seam_recv.at[1],
            SEAM_LON,
            lat,
        ).start()

    @pl.when(bridge)
    def _():
        tell(bridge_to, lat_of(place, 1 - half), bridge_sem)
        pl.semaphore_wait(bridge_sem, 1)
        each(N_LON - 1, lambda k: tell(lax.rem(lon + 1 + k, N_LON), lat, both_sem))

    @pl.when(jnp.logical_not(all_polar))
    def _():
        send(lon_edge, west_in, edge_send.at[2], edge_recv.at[2], east, lat).start()
        send(lon_edge, east_in, edge_send.at[3], edge_recv.at[3], west, lat).start()

    def to_worker(s, t_half):
        to = worker_lon(2 * s + t_half)

        @pl.when(to != lon)
        def _():
            send(
                column.at[s, t_half], gathered.at[lon], gather_send, gather_recv, to, lat
            ).start()

        @pl.when(to == lon)
        def _():
            gathered[lon] = column[s, t_half]

    def pass_on(s):
        @pl.when(jnp.logical_not(jnp.logical_and(is_source, source == s)))
        def _():
            take(column.at[s], out_recv.at[s])

        to_worker(s, 0)

        @pl.when(half == 0)
        def _():
            to_worker(s, 1)

    each(SOURCES, pass_on)

    @pl.when(half == 1)
    def _():
        each(SOURCES, lambda s: to_worker(s, 1))

    @pl.when(jnp.logical_or(is_worker, seam_worker))
    def _():
        fh[...], fl[...] = split_value(forward[...])
        ih[...], il[...] = split_value(inverse[...])
        wh[...], wl[...] = split_value(within[...])

    @pl.when(jnp.logical_not(bridge))
    def _():
        pl.semaphore_wait(both_sem, 1)

    @pl.when(far_north)
    def _():
        send(south_edge, far_in, edge_send.at[0], far_recv, lon, opposite).start()

    @pl.when(far_south)
    def _():
        send(north_edge, far_in.at[0], edge_send.at[1], far_recv, lon, opposite).start()

    @pl.when(seam_worker)
    def _():
        take(seam_own.at[pl.ds(0, N_LON - 1)], seam_recv.at[1])

        @pl.when(low_seam)
        def _():
            take(seam_other.at[pl.ds(0, N_LON // 2)], seam_recv.at[0])
            scale = -0.5 * courant_number * factor[0, ROWS - 1 :, :] / factor[2, ROWS - 1 :, :]
            scale = jnp.concatenate([scale, scale], axis=1)[None]
            gathered[...] = seam_own[:, 0] + scale * seam_own[:, 1] * seam_other[:, 0]

        @pl.when(high_seam)
        def _():
            take(seam_other, seam_recv.at[0])
            scale = 0.5 * courant_number * factor[1, :1, :] / factor[2, :1, :]
            scale = jnp.concatenate([scale, scale], axis=1)[None]
            gathered[...] = seam_own[:, 0] + scale * seam_other[:, 1] * (
                seam_other[:, 0] + seam_own[:, 1]
            )

    @pl.when(is_worker)
    def _():
        take(gathered.at[pl.ds(0, N_LON - 1)], gather_recv)

    @pl.when(jnp.logical_or(is_worker, seam_worker))
    def _():
        cos_mid = jnp.concatenate([tw[0]] * (LEV // 2), axis=0)
        sin_mid = jnp.concatenate([tw[1]] * (LEV // 2), axis=0)
        tables = (fh[...], fl[...], ih[...], il[...], wh[...], wl[...], cos_mid, sin_mid)
        values = with_edge_terms(gathered[...].reshape(N_LON * LEV, LANES))
        smoothed[...] = band_filter(values, plan[64, 0], tables).reshape(N_LON, LEV, LANES)

    @pl.when(is_worker)
    def _():
        def to_slot(to):
            send(
                smoothed.at[to],
                slot_in.at[half * SOURCES + work_source],
                cross_send,
                cross_recv,
                to,
                opposite,
            ).start()

        def to_line(to):
            @pl.when(to != lon)
            def _():
                send(
                    smoothed.at[to],
                    returned.at[work_source, work_half],
                    back_send,
                    back_recv.at[work_source],
                    to,
                    lat,
                ).start()

        @pl.when(jnp.logical_and(across, half == 1))
        def _():
            each(N_LON, to_slot)

        each(N_LON, to_line)

        @pl.when(jnp.logical_and(across, half == 0))
        def _():
            each(N_LON, lambda k: to_slot(alternate(lon, k)))

        returned[work_source, work_half] = smoothed[lon]

    @pl.when(seam_worker)
    def _():
        def to_seam(to, to_lat, sem):
            send(
                smoothed.at[to], seam_result.at[seam_side], sem, seam_back_recv, to, to_lat
            ).start()

        def to_own_line(to):
            @pl.when(to != lon)
            def _():
                to_seam(to, lat, seam_back_send.at[1])

        @pl.when(half == 0)
        def _():
            each(N_LON, to_own_line)

        each(N_LON, lambda to: to_seam(to, other_lat, seam_back_send.at[0]))

        @pl.when(half == 1)
        def _():
            each(N_LON, to_own_line)

        seam_result[seam_side] = smoothed[lon]

    @pl.when(hands_north)
    def _():
        take(far_in, far_recv)
        send(far_in, south_in, far_send, edge_recv.at[0], lon, opposite + 1).start()

    @pl.when(hands_south)
    def _():
        take(far_in.at[0], far_recv)
        send(far_in.at[0], north_in, far_send, edge_recv.at[1], lon, opposite - 1).start()

    @pl.when(jnp.logical_and(is_source, jnp.logical_not(all_polar)))
    def _():
        plain_rows()

    from_far = jnp.logical_or(far_north, far_south)

    @pl.when(jnp.logical_not(jnp.logical_or(is_source, from_far)))
    def _():
        plain_rows()

    seam_pair = jnp.where(lat < NLAT // ROWS // 2, 0, 1)
    seam_slots = [slot_in.at[pl.ds(2 * SOURCES + 2 * pair, 2)] for pair in range(2)]

    @pl.when(at_seam)
    def _():
        @pl.when(seam_worker)
        def _():
            take(seam_result.at[0], seam_back_recv)

        @pl.when(jnp.logical_not(seam_worker))
        def _():
            take(seam_result, seam_back_recv)

        own_slots = slot_in.at[pl.ds(2 * SOURCES + 2 * seam_pair, 2)]

        def spread(k):
            to = lat_of(lax.rem(place + 1 + k, PLACES), half)
            send(seam_result, own_slots, seam_out_send, seam_out_recv.at[seam_pair], lon, to).start()

        each(PLACES - 1, spread)
        slot_in[2 * SOURCES + 2 * seam_pair] = seam_result[0]
        slot_in[2 * SOURCES + 2 * seam_pair + 1] = seam_result[1]
        homeward[2 * PLACES] = seam_result[seam_side]

    def go_home(s):
        own = jnp.logical_and(is_worker, work_source == s)

        @pl.when(own)
        def _():
            take(returned.at[s, 0], back_recv.at[s])

        @pl.when(jnp.logical_not(own))
        def _():
            take(returned.at[s], back_recv.at[s])

        stays = jnp.logical_and(is_source, source == s)

        @pl.when(stays)
        def _():
            homeward[2 * place] = returned[s, 0]
            homeward[2 * place + 1] = returned[s, 1]

        @pl.when(jnp.logical_not(stays))
        def _():
            send(
                returned.at[s],
                homeward.at[pl.ds(2 * place, 2)],
                home_send,
                home_recv,
                lon,
                lat_of(source_place(s, half), half),
            ).start()

        slot_in[half * SOURCES + s] = returned[s, half]

    each(SOURCES, go_home)

    @pl.when(from_far)
    def _():
        plain_rows()

    take(slot_in.at[pl.ds(0, SOURCES)], cross_recv)
    for pair in range(2):

        @pl.when(jnp.logical_not(jnp.logical_and(at_seam, seam_pair == pair)))
        def _(pair=pair):
            take(seam_slots[pair], seam_out_recv.at[pair])

    for slot in range(SLOTS):
        slots_out[slot] = slot_in[plan[56 + slot, 0]][:, :COLS]

    @pl.when(is_source)
    def _():
        take(homeward.at[pl.ds(0, 2 * PLACES - 2)], home_recv)
        for j in range(ROWS):
            lat_row = lat * ROWS + j
            polar = jnp.logical_or(lat_row < NH, lat_row >= NLAT - NH)
            filtered = homeward[plan[32 + j, 0]][:, :COLS]
            next_out[:, j, :] = jnp.where(polar, tracer[:, j, :] + filtered, next_out[:, j, :])

    @pl.when(hands_north)
    def _():
        sent(far_in, far_send)

    @pl.when(hands_south)
    def _():
        sent(far_in.at[0], far_send)

    @pl.when(any_north)
    def _():
        sent(south_edge, edge_send.at[0])

    @pl.when(any_south)
    def _():
        sent(north_edge, edge_send.at[1])

    @pl.when(jnp.logical_not(all_polar))
    def _():
        sent(lon_edge, edge_send.at[2])
        sent(lon_edge, edge_send.at[3])

    @pl.when(low_seam)
    def _():
        sent(south_edge, seam_send.at[0])

    @pl.when(high_seam)
    def _():
        sent(north_edge, seam_send.at[0])

    @pl.when(at_seam)
    def _():
        sent(homeward.at[pl.ds(0, 2 * PLACES - 2)], seam_out_send)

        @pl.when(jnp.logical_not(seam_worker))
        def _():
            sent(seam_own.at[lon], seam_send.at[1])

        @pl.when(seam_worker)
        def _():
            sent(smoothed, seam_back_send.at[0])
            sent(smoothed.at[pl.ds(0, N_LON - 1)], seam_back_send.at[1])

    @pl.when(is_source)
    def _():
        sent(outbound.at[pl.ds(0, 2 * PLACES - 2)], out_send)
        sent(homeward.at[pl.ds(0, 2 * SOURCES - 2)], home_send)

    @pl.when(jnp.logical_not(is_source))
    def _():
        sent(homeward.at[pl.ds(0, 2 * SOURCES)], home_send)

    @pl.when(is_worker)
    def _():
        sent(smoothed.at[pl.ds(0, 2 * SOURCES - 1)], gather_send)
        sent(smoothed.at[pl.ds(0, N_LON - 1)], back_send)

    @pl.when(jnp.logical_not(is_worker))
    def _():
        sent(smoothed.at[pl.ds(0, 2 * SOURCES)], gather_send)

    @pl.when(across)
    def _():
        sent(smoothed, cross_send)


def shards(tracer, zonal_wind, meridional_wind, polar_target, cutoff_wave):
    tables = [jnp.asarray(table) for table in filter_tables()]
    factors = jnp.asarray(row_factors())
    f32, bf16 = jnp.float32, jnp.bfloat16
    block = (LEV, ROWS, COLS)
    anywhere, in_vmem = pl.BlockSpec(memory_space=pltpu.HBM), pl.BlockSpec(memory_space=pltpu.VMEM)
    dma = pltpu.SemaphoreType.DMA
    square, wide = (LEV * N_LON, LEV * N_LON), (LANES, 2 * LANES)
    message = (LEV, LANES)
    in_hbm = [
        pltpu.with_memory_space_constraint(a, pltpu.HBM)
        for a in (
            polar_target.reshape(2, NPOLAR // 2),
            cutoff_wave.reshape(2, NPOLAR // 2),
            jnp.asarray(polar_row_table()),
            tracer,
            zonal_wind,
            meridional_wind,
            factors,
            *tables,
        )
    ]
    return pl.pallas_call(
        substep_kernel,
        out_shape=(
            jax.ShapeDtypeStruct(block, f32),
            jax.ShapeDtypeStruct((SLOTS, LEV, COLS), f32),
        ),
        in_specs=[anywhere] * 11,
        out_specs=(in_vmem, in_vmem),
        scratch_shapes=[
            pltpu.VMEM((2, NPOLAR // 2), jnp.int32),
            pltpu.VMEM((2, NPOLAR // 2), jnp.int32),
            pltpu.VMEM((8, NPOLAR), jnp.int32),
            pltpu.VMEM((ENTRIES, 128), jnp.int32),
            pltpu.SMEM((ENTRIES, 128), jnp.int32),
            pltpu.VMEM(block, f32),
            pltpu.VMEM(block, f32),
            pltpu.VMEM(block, f32),
            pltpu.VMEM((3, ROWS, 128), f32),
            pltpu.VMEM(square, f32),
            pltpu.VMEM(square, f32),
            pltpu.VMEM(wide, f32),
            pltpu.VMEM(square, bf16),
            pltpu.VMEM(square, bf16),
            pltpu.VMEM(square, bf16),
            pltpu.VMEM(square, bf16),
            pltpu.VMEM(wide, bf16),
            pltpu.VMEM(wide, bf16),
            pltpu.VMEM((2, N_LON, LANES), f32),
            pltpu.VMEM(message, f32),
            pltpu.VMEM(message, f32),
            pltpu.VMEM(message, f32),
            pltpu.VMEM((2, *message), f32),
            pltpu.VMEM(message, f32),
            pltpu.VMEM((2, *message), f32),
            pltpu.VMEM(message, f32),
            pltpu.VMEM((FLAT, LANES), f32),
            pltpu.VMEM((ROWS, *message), f32),
            pltpu.VMEM((2 * PLACES, *message), f32),
            pltpu.VMEM((SOURCES, 2, *message), f32),
            pltpu.VMEM((N_LON, *message), f32),
            pltpu.VMEM((N_LON, *message), f32),
            pltpu.VMEM((SOURCES, 2, *message), f32),
            pltpu.VMEM((2 * SOURCES + 4, *message), f32),
            pltpu.VMEM((2 * PLACES + 1, *message), f32),
            pltpu.VMEM((N_LON, 2, *message), f32),
            pltpu.VMEM((N_LON, 2, *message), f32),
            pltpu.VMEM((2, *message), f32),
            pltpu.VMEM((2, *message), f32),
            dma((12,)),
            dma((4,)),
            dma((4,)),
            dma,
            dma((SOURCES,)),
            dma,
            dma,
            dma,
            dma((SOURCES,)),
            dma,
            dma,
            dma,
            dma,
            dma((2,)),
            dma((2,)),
            dma((2,)),
            dma,
            dma,
            dma((2,)),
            pltpu.SemaphoreType.REGULAR((2,)),
            pltpu.SemaphoreType.REGULAR,
            pltpu.SemaphoreType.REGULAR,
            pltpu.SemaphoreType.REGULAR,
            dma,
            dma,
        ],
        compiler_params=pltpu.CompilerParams(
            collective_id=0, has_side_effects=True, vmem_limit_bytes=32 * 2**20
        ),
        name="substep",
    )(*in_hbm)


def solution(mesh):
    placed = (P(None, "lat", "lon"), P(None, "lat", "lon"), P(None, "lat", "lon"), P(), P())
    return jax.shard_map(
        shards,
        mesh=mesh,
        in_specs=placed,
        out_specs=(P(None, "lat", "lon"), P("lat", None, "lon")),
        check_vma=False,
    )
```
